32 devices in a mesh: dp: 4 (over y, x), fsdp: 8 (over z, core).
Axes of the slice: x: 2, y: 2, z: 4, core: 2. Of those that a mesh axis runs over, the one named last changes fastest.
Arguments:
- tokens: bfloat16 [4, 2048, 1536], P('dp', 'fsdp'), may hold values from -6 to 6
- segment_ids: int32 [4, 2048], P('dp', 'fsdp'), may hold values from 0 to 1, as said below
- routes: int32 [4, 2048, 2], P('dp', 'fsdp'), may hold values from 0 to 7, as said below
- query_weight: bfloat16 [1536, 1536], P(('dp', 'fsdp')), may hold values from -0.15625 to 0.15625
- key_value_weight: bfloat16 [1536, 1024], P(('dp', 'fsdp')), may hold values from -0.15625 to 0.15625
- output_weight: bfloat16 [1536, 1536], P(None, ('dp', 'fsdp')), may hold values from -0.625 to 0.625
- router_weight: bfloat16 [1536, 8], P(('dp', 'fsdp')), may hold values from -0.109375 to 0.109375
- gain_before: bfloat16 [1536], P(('dp', 'fsdp')), may hold values from 0.099609375 to 1.8984375
- gain_middle: bfloat16 [1536], P(('dp', 'fsdp')), may hold values from 0.099609375 to 1.8984375
- inner_weight: bfloat16 [1536, 2, 8192], P('dp', None, 'fsdp'), may hold values from -0.15625 to 0.15625
- outer_weight: bfloat16 [8192, 1536], P('fsdp', 'dp'), may hold values from -0.1875 to 0.1875
- cotangent: bfloat16 [4, 2048, 1536], P('dp', 'fsdp'), may hold values from -6 to 6
Outputs:
- block_out: bfloat16 [4, 2048, 1536], P('dp', 'fsdp')
- tokens_grad: float32 [4, 2048, 1536], P('dp', 'fsdp')
- query_grad: float32 [1536, 1536], P(('dp', 'fsdp'))
- keyval_grad: float32 [1536, 1024], P(('dp', 'fsdp'))
- output_grad: float32 [1536, 1536], P(None, ('dp', 'fsdp'))
- router_grad: float32 [1536, 8], P(('dp', 'fsdp'))
- before_grad: float32 [1536], P(('dp', 'fsdp'))
- middle_grad: float32 [1536], P(('dp', 'fsdp'))
- inner_grad: float32 [1536, 2, 8192], P('dp', None, 'fsdp')
- outer_grad: float32 [8192, 1536], P('fsdp', 'dp')
The draws below stay inside these ranges and needn't reach their ends.
Inputs may be any that keep to these rules, and one draw needn't show every extreme that they name: `segment_ids`: ids never fall along a sequence and are 0 at its start. Among the 1 sequence of each dp index, one holds a short document within its first 256 positions and then one document to its end. Where 1 is 2 or more, another one is cut into 7 documents. `routes`: each token names two different experts. Among the tokens of one device (one index of dp and of fsdp) no expert is named more than 96 times, and for each dp index some expert is named exactly 96 times by every device.
All inputs are finite; a program needn't handle non-finite values.
Results may differ from the reference program's by a relative error of at most 0.015.
Values may be sent and summed in bfloat16 or wider, within the bound.
No kernel may reach another device: no remote copies, remote signals or barrier semaphores. Data moves between devices by JAX's collectives and lax.ppermute only.
A program may use at most 320 MiB of HBM per device.

```python
import jax
import jax.numpy as jnp
from jax import lax

MODEL_WIDTH = 1536
QUERY_HEADS = 24
KEY_VALUE_HEADS = 8
HEAD_SIZE = 64
FF = 1024
EXPERTS = 8
TOP = 2
SEQ_LEN = 2048
TOK_DEV = 256
SEQS_G = 1
SEQS = 4
LOC = 256
CAP = 96
REPL = 1
SLAB = 1024
N_DP = 4
N_FSDP = 8


def draw_segment_ids(key, part):
    key = jax.random.fold_in(key, 11)
    key_cut, key_use, key_single, key_first, key_force = jax.random.split(key, 5)
    cut_draws = jax.random.randint(key_cut, (SEQS, 6, 3), 0, SEQ_LEN)
    cut_spots = cut_draws[:, :, 0] * cut_draws[:, :, 1] // SEQ_LEN * cut_draws[:, :, 2] // SEQ_LEN + 1
    cut_used = jax.random.randint(key_use, (SEQS, 6), 0, 2)
    single_doc = jax.random.randint(key_single, (N_DP, 1), 0, SEQS_G)
    keep_cuts = (jnp.arange(SEQS_G)[None, :] != single_doc).reshape(SEQS).astype(jnp.int32)
    many_seqs = 1 if SEQS_G > 1 else 0
    forced_row = (jnp.arange(SEQS_G)[None, :] == (single_doc + 1) % SEQS_G).reshape(SEQS).astype(jnp.int32) * many_seqs
    spacing = max(SEQ_LEN // 8, 1)
    forced_off = jax.random.randint(key_force, (SEQS, 6), 0, spacing)
    forced_spots = (jnp.arange(6, dtype=jnp.int32)[None, :] + 1) * spacing + forced_off
    cut_spots = jnp.where(forced_row[:, None] == 1, forced_spots, cut_spots)
    cut_used = jnp.maximum(cut_used, forced_row[:, None])
    first_len = jax.random.randint(key_first, (SEQS, 1), 1, max(LOC, 2))
    active = cut_used * keep_cuts[:, None]
    positions = jnp.arange(SEQ_LEN, dtype=jnp.int32)
    boundary = jnp.sum((cut_spots[:, :, None] == positions[None, None, :]).astype(jnp.int32) * active[:, :, None], 1)
    boundary = jnp.minimum(boundary, 1)
    spanning = (positions[None, :] == first_len).astype(jnp.int32) * (1 - keep_cuts)[:, None]
    boundary = boundary + spanning
    return jnp.cumsum(boundary, 1).astype(jnp.int32)


def draw_routes(key, part):
    key = jax.random.fold_in(key, 23)
    key_busy, key_rank, key_other, key_offset, key_swap = jax.random.split(key, 5)
    devices = N_DP * N_FSDP
    busiest = jnp.repeat(jax.random.randint(key_busy, (N_DP,), 0, EXPERTS), N_FSDP)[:, None]
    rank_of = jax.vmap(lambda subkey: jax.random.permutation(subkey, TOK_DEV))(jax.random.split(key_rank, devices)).astype(jnp.int32)
    other_list = jax.vmap(lambda subkey: jax.random.permutation(subkey, EXPERTS - 1))(jax.random.split(key_other, devices)).astype(jnp.int32)
    offset = jax.random.randint(key_offset, (devices, 1), 0, EXPERTS - 1)
    is_busy = rank_of < CAP
    later_spot = CAP + 2 * (rank_of - CAP)

    def other_at(spot):
        index_of = (offset + spot) % (EXPERTS - 1)
        return (busiest + 1 + jnp.take_along_axis(other_list, index_of, 1)) % EXPERTS
    first = jnp.where(is_busy, busiest, other_at(jnp.where(is_busy, 0, later_spot)))
    second = jnp.where(is_busy, other_at(rank_of), other_at(later_spot + 1))
    swapped = jax.random.randint(key_swap, (devices, TOK_DEV), 0, 2) == 1
    routed = jnp.stack([jnp.where(swapped, second, first), jnp.where(swapped, first, second)], -1)
    routed = routed.reshape(N_DP, N_FSDP, SEQS_G, LOC, 2).transpose(0, 2, 1, 3, 4)
    return routed.reshape(SEQS, SEQ_LEN, 2).astype(jnp.int32)


def shard_levels(key, dims, shards, smallest, top_value):
    factor_of, own = 1.0, jax.random.fold_in(key, 6)
    for axis_at, parts in shards:
        draws = jnp.exp(jax.random.uniform(jax.random.fold_in(own, axis_at), (parts,), jnp.float32, smallest / len(shards), top_value / len(shards)))
        factor_of = factor_of * jnp.repeat(draws, dims[axis_at] // parts).reshape([-1 if axis == axis_at else 1 for axis in range(len(dims))])
    return factor_of


def centred(key, shape, scale, limit, cuts=(), kind=jnp.bfloat16):
    loudness = shard_levels(key, shape, cuts, -0.22, 0.18) if cuts else 1.0
    drawn = jax.random.normal(key, shape, jnp.float32) * scale * loudness
    return jnp.minimum(jnp.maximum(drawn, -limit), limit).astype(kind)


def setup_inputs(seed: int = 0) -> dict:
    splits = jax.random.split(jax.random.key(seed), 13)
    tokens = centred(splits[0], (SEQS, SEQ_LEN, MODEL_WIDTH), 1.0, 6.0, ((0, 4), (1, 8)))
    segment_ids = draw_segment_ids(jax.random.fold_in(splits[12], 71), 0)
    routes = draw_routes(jax.random.fold_in(splits[12], 71), 0)
    query_weight = centred(splits[3], (MODEL_WIDTH, QUERY_HEADS * HEAD_SIZE), MODEL_WIDTH ** -0.5, 0.15625, ((0, 32),))
    key_value_weight = centred(splits[4], (MODEL_WIDTH, 2 * KEY_VALUE_HEADS * HEAD_SIZE), MODEL_WIDTH ** -0.5, 0.15625, ((0, 32),))
    output_weight = centred(splits[5], (QUERY_HEADS * HEAD_SIZE, MODEL_WIDTH), (QUERY_HEADS * HEAD_SIZE // 16) ** -0.5, 0.625, ((1, 32),))
    router_weight = centred(splits[6], (MODEL_WIDTH, EXPERTS), (2 * MODEL_WIDTH) ** -0.5, 0.109375, ((0, 32),))
    gain_before = jnp.clip(1.0 + 0.18 * jax.random.normal(splits[7], (MODEL_WIDTH,), jnp.float32), 0.099609375, 1.8984375).astype(jnp.bfloat16)
    gain_middle = jnp.clip(1.0 + 0.18 * jax.random.normal(splits[8], (MODEL_WIDTH,), jnp.float32), 0.099609375, 1.8984375).astype(jnp.bfloat16)
    inner_weight = centred(splits[9], (MODEL_WIDTH, 2, EXPERTS * FF), MODEL_WIDTH ** -0.5, 0.15625, ((0, 4), (2, 8)))
    outer_weight = centred(splits[10], (EXPERTS * FF, MODEL_WIDTH), FF ** -0.5, 0.1875, ((0, 8), (1, 4)))
    cotangent = centred(splits[11], (SEQS, SEQ_LEN, MODEL_WIDTH), 1.0, 6.0, ((0, 4), (1, 8)))
    return dict(tokens=tokens, segment_ids=segment_ids, routes=routes, query_weight=query_weight, key_value_weight=key_value_weight, output_weight=output_weight, router_weight=router_weight, gain_before=gain_before, gain_middle=gain_middle, inner_weight=inner_weight, outer_weight=outer_weight, cotangent=cotangent)


HIGHEST_PRECISION = lax.Precision.HIGHEST
EPSILON = 1e-05
NEGATIVE_LARGE = -1e+30

@jax.custom_vjp
def low(v):
    return lax.optimization_barrier(v.astype(jnp.bfloat16)).astype(jnp.float32)

@jax.custom_vjp
def low_back(v):
    return v

def low_keep(v):
    return (low(v), None)

def low_pass(kept, grad):
    return (grad,)

def back_keep(v):
    return (v, None)

def back_low(kept, grad):
    return (low(grad),)
low.defvjp(low_keep, low_pass)
low_back.defvjp(back_keep, back_low)

def normalize(hidden, gain_vec):
    return hidden * lax.rsqrt(lax.optimization_barrier(jnp.mean(hidden * hidden, -1, keepdims=True)) + EPSILON) * gain_vec

def attend_sequence(inputs):
    query_matrix, every_key, every_value, segments = inputs
    span_length = query_matrix.shape[0]
    row_block = min(512, span_length)
    key_spots = jnp.arange(span_length, dtype=jnp.int32)

    def one_block(start):
        query_rows = lax.dynamic_slice_in_dim(query_matrix, start, row_block, 0)
        query_seg = lax.dynamic_slice_in_dim(segments, start, row_block, 0)
        query_spots = start + jnp.arange(row_block, dtype=jnp.int32)
        scores = low_back(jnp.einsum('ikgd,jkd->kgij', query_rows, every_key, precision=HIGHEST_PRECISION) * HEAD_SIZE ** (-0.5))
        allowed = (query_seg[:, None] == segments[None, :]) & (key_spots[None, :] <= query_spots[:, None])
        scores = jnp.where(allowed[None, None], scores, NEGATIVE_LARGE)
        running_totals = jax.nn.logsumexp(scores, -1, keepdims=True)
        weights = low(jnp.exp(scores - running_totals))
        return jnp.einsum('kgij,jkd->ikgd', weights, every_value, precision=HIGHEST_PRECISION)
    starts = (jnp.arange(span_length // row_block, dtype=jnp.int32) * row_block).astype(jnp.int32)
    blocks = lax.map(jax.checkpoint(one_block), starts)
    return blocks.reshape(query_matrix.shape)

def expert_block(inputs):
    rows_in, inner_part, outer_part = inputs
    summed = jnp.zeros((rows_in.shape[0], outer_part.shape[-1]), jnp.float32)
    for slab_index in range(REPL):
        copied = low_back(rows_in)
        gate_pre = low_back(jnp.dot(copied, inner_part[slab_index, :, 0], precision=HIGHEST_PRECISION))
        up_pre = low_back(jnp.dot(copied, inner_part[slab_index, :, 1], precision=HIGHEST_PRECISION))
        hidden = low(jax.nn.silu(gate_pre) * up_pre)
        summed = summed + low(jnp.dot(hidden, outer_part[slab_index], precision=HIGHEST_PRECISION))
    return low_back(summed)

def group_forward(params, group):
    tokens, segments, routes = group
    query_weight, key_value_weight, output_weight, router_weight, gain_before, gain_middle, inner_weight, outer_weight = params
    sequence_count, span_length, model_width = tokens.shape
    flat = tokens.reshape(sequence_count * span_length, model_width)
    normed = low(normalize(flat, gain_before))
    query_matrix = low_back(low(jnp.dot(normed, query_weight, precision=HIGHEST_PRECISION)))
    key_value_rows = low_back(low(jnp.dot(normed, key_value_weight, precision=HIGHEST_PRECISION)))
    half_columns = KEY_VALUE_HEADS * HEAD_SIZE
    query_matrix = query_matrix.reshape(sequence_count, span_length, KEY_VALUE_HEADS, QUERY_HEADS // KEY_VALUE_HEADS, HEAD_SIZE)
    every_key = key_value_rows[:, :half_columns].reshape(sequence_count, span_length, KEY_VALUE_HEADS, HEAD_SIZE)
    every_value = key_value_rows[:, half_columns:].reshape(sequence_count, span_length, KEY_VALUE_HEADS, HEAD_SIZE)
    mixed = lax.map(attend_sequence, (query_matrix, every_key, every_value, segments))
    mixed = low_back(low(mixed.reshape(sequence_count * span_length, QUERY_HEADS * HEAD_SIZE)))
    middle = flat + low_back(jnp.dot(mixed, output_weight, precision=HIGHEST_PRECISION))
    expert_in = low(normalize(middle, gain_middle))
    logits = jnp.dot(expert_in, router_weight, precision=HIGHEST_PRECISION)
    device_rows = expert_in.reshape(sequence_count, N_FSDP, LOC, model_width).transpose(1, 0, 2, 3).reshape(N_FSDP, TOK_DEV, model_width)
    device_logits = logits.reshape(sequence_count, N_FSDP, LOC, EXPERTS).transpose(1, 0, 2, 3).reshape(N_FSDP, TOK_DEV, EXPERTS)
    device_routes = routes.reshape(sequence_count, N_FSDP, LOC, TOP).transpose(1, 0, 2, 3).reshape(N_FSDP, TOK_DEV * TOP).astype(jnp.int32)
    chosen = device_routes[..., None] == jnp.arange(EXPERTS, dtype=jnp.int32)
    chosen_logits = lax.optimization_barrier(jnp.sum(jnp.where(chosen.reshape(N_FSDP, TOK_DEV, TOP, EXPERTS), device_logits[:, :, None, :], 0.0), -1))
    gates = jax.nn.softmax(chosen_logits, -1)
    marks = chosen.astype(jnp.int32)
    earlier = (jnp.cumsum(marks, 1) - marks).astype(jnp.int32)
    slot_index = (device_routes * CAP + lax.optimization_barrier(jnp.sum(earlier * marks, -1))).astype(jnp.int32)
    pair_rows = jnp.repeat(device_rows, TOP, axis=1)
    buffers = jax.vmap(lambda index_row, value_rows: jnp.zeros((EXPERTS * CAP, model_width), value_rows.dtype).at[index_row].set(value_rows))(slot_index, pair_rows)
    by_expert = buffers.reshape(N_FSDP, EXPERTS, CAP, model_width).transpose(1, 0, 2, 3).reshape(EXPERTS, N_FSDP * CAP, model_width)
    inner_split = inner_weight.reshape(model_width, 2, EXPERTS, REPL, SLAB).transpose(2, 3, 0, 1, 4)
    outer_split = outer_weight.reshape(EXPERTS, REPL, SLAB, model_width)
    expert_out = lax.map(jax.checkpoint(expert_block), (by_expert, inner_split, outer_split))
    returned = expert_out.reshape(EXPERTS, N_FSDP, CAP, model_width).transpose(1, 0, 2, 3).reshape(N_FSDP, EXPERTS * CAP, model_width)
    picked = jax.vmap(lambda rows_all, index_row: rows_all[index_row])(returned, slot_index).reshape(N_FSDP, TOK_DEV, TOP, model_width)
    combined = lax.optimization_barrier(jnp.sum(gates[..., None] * picked, 2))
    combined = combined.reshape(N_FSDP, sequence_count, LOC, model_width).transpose(1, 0, 2, 3).reshape(sequence_count * span_length, model_width)
    return (middle + combined).reshape(sequence_count, span_length, model_width)

def reference(tokens, segment_ids, routes, query_weight, key_value_weight, output_weight, router_weight, gain_before, gain_middle, inner_weight, outer_weight, cotangent):
    params = tuple((source.astype(jnp.float32) for source in (query_weight, key_value_weight, output_weight, router_weight, gain_before, gain_middle, inner_weight, outer_weight)))
    inputs = tokens.astype(jnp.float32)
    seg_groups = segment_ids.reshape(N_DP, SEQS_G, SEQ_LEN)
    route_groups = routes.reshape(N_DP, SEQS_G, SEQ_LEN, TOP)

    def forward(token_rows, weights):
        grouped = (token_rows.reshape(N_DP, SEQS_G, SEQ_LEN, MODEL_WIDTH), seg_groups, route_groups)
        outputs = lax.map(lambda group: group_forward(weights, group), grouped)
        return outputs.reshape(SEQS, SEQ_LEN, MODEL_WIDTH)
    block_out, pullback = jax.vjp(forward, inputs, params)
    tokens_grad, weight_grads = pullback(cotangent.astype(jnp.float32))
    return (block_out.astype(jnp.bfloat16), tokens_grad, weight_grads[0], weight_grads[1], weight_grads[2], weight_grads[3], weight_grads[4], weight_grads[5], weight_grads[6], weight_grads[7])
```

```python
import jax
import jax.numpy as jnp
from jax import lax
from jax.experimental import pallas as pl
from jax.experimental.pallas import tpu as pltpu
from jax.sharding import PartitionSpec as P

QUERY_HEADS = 24
KEY_VALUE_HEADS = 8
HEAD_SIZE = 64


HIGHEST_PRECISION = lax.Precision.HIGHEST
EPSILON = 1e-05
NEGATIVE_LARGE = -1e30


def normalize(hidden, gain_vec):
    factor = lax.rsqrt(jnp.mean(hidden * hidden, -1, keepdims=True) + EPSILON)
    unit_rows = hidden * factor
    return (unit_rows * gain_vec.astype(jnp.float32), unit_rows, factor)


def normalize_back(grad_rows, unit_rows, factor, gain_vec):
    scaled = grad_rows * gain_vec.astype(jnp.float32)
    inner_part = factor * (scaled - unit_rows * jnp.mean(scaled * unit_rows, -1, keepdims=True))
    return (inner_part, jnp.sum(grad_rows * unit_rows, 0))


def split_block(gathered, offset, key_tile_block):
    sequence_count = gathered.shape[0]
    portion_rows = lax.slice_in_dim(gathered, offset, offset + key_tile_block, axis=1)
    half_columns = KEY_VALUE_HEADS * HEAD_SIZE
    key_portion = portion_rows[..., :half_columns].reshape(
        sequence_count, key_tile_block, KEY_VALUE_HEADS, HEAD_SIZE
    )
    value_portion = portion_rows[..., half_columns:].reshape(
        sequence_count, key_tile_block, KEY_VALUE_HEADS, HEAD_SIZE
    )
    return (key_portion, value_portion)


def block_scores(query_matrix, key_portion, allowed):
    raw_scores = jnp.einsum(
        "sikgd,sjkd->skgij", query_matrix, key_portion, preferred_element_type=jnp.float32
    ) * HEAD_SIZE ** (-0.5)
    return jnp.where(allowed[:, None, None], raw_scores, NEGATIVE_LARGE)


def mask_for(seg_all, seg_mine, positions, offset, key_tile_block):
    key_seg = lax.slice_in_dim(seg_all, offset, offset + key_tile_block, axis=1)
    key_spots = offset + jnp.arange(key_tile_block, dtype=jnp.int32)
    same_doc = seg_mine[:, :, None] == key_seg[:, None, :]
    causal = key_spots[None, None, :] <= positions[None, :, None]
    return same_doc & causal


def log_totals(query_matrix, gathered, block_masks, key_tile_block):
    sequence_count, resident_rows = (query_matrix.shape[0], query_matrix.shape[1])
    running_totals = jnp.full(
        (sequence_count, KEY_VALUE_HEADS, QUERY_HEADS // KEY_VALUE_HEADS, resident_rows),
        NEGATIVE_LARGE,
        jnp.float32,
    )
    for block_index, allowed in enumerate(block_masks):
        key_portion, value_portion = split_block(
            gathered, block_index * key_tile_block, key_tile_block
        )

        def log_live(present_value, key_portion=key_portion, allowed=allowed):
            scores = block_scores(query_matrix, key_portion, allowed)
            return jnp.logaddexp(present_value, jax.nn.logsumexp(scores, -1))

        running_totals = lax.cond(
            jnp.any(allowed), log_live, lambda present_value: present_value, running_totals
        )
    return running_totals


def attend_values(query_matrix, gathered, block_masks, key_tile_block, running_totals):
    result = jnp.zeros(query_matrix.shape, jnp.float32)
    for block_index, allowed in enumerate(block_masks):
        key_portion, value_portion = split_block(
            gathered, block_index * key_tile_block, key_tile_block
        )

        def attend_live(
            present_value, key_portion=key_portion, value_portion=value_portion, allowed=allowed
        ):
            probs = jnp.exp(
                block_scores(query_matrix, key_portion, allowed) - running_totals[..., None]
            ).astype(jnp.bfloat16)
            return present_value + jnp.einsum(
                "skgij,sjkd->sikgd", probs, value_portion, preferred_element_type=jnp.float32
            )

        result = lax.cond(
            jnp.any(allowed), attend_live, lambda present_value: present_value, result
        )
    token_count = query_matrix.shape[0] * query_matrix.shape[1]
    return result.reshape(token_count, -1).astype(jnp.bfloat16)


def attend_back(
    query_matrix, mixed_gradient, gathered, block_masks, key_tile_block, running_totals
):
    sequence_count = query_matrix.shape[0]
    delta = jnp.zeros(running_totals.shape, jnp.float32)
    for block_index, allowed in enumerate(block_masks):
        key_portion, value_portion = split_block(
            gathered, block_index * key_tile_block, key_tile_block
        )

        def live_delta(
            present_value, key_portion=key_portion, value_portion=value_portion, allowed=allowed
        ):
            probs = jnp.exp(
                block_scores(query_matrix, key_portion, allowed) - running_totals[..., None]
            )
            grad_probs = jnp.einsum(
                "sikgd,sjkd->skgij",
                mixed_gradient,
                value_portion,
                preferred_element_type=jnp.float32,
            )
            return present_value + jnp.sum(probs * grad_probs, -1)

        delta = lax.cond(jnp.any(allowed), live_delta, lambda present_value: present_value, delta)
    grad_queries = jnp.zeros(query_matrix.shape, jnp.float32)
    key_terms = []
    for block_index, allowed in enumerate(block_masks):
        key_portion, value_portion = split_block(
            gathered, block_index * key_tile_block, key_tile_block
        )

        def live_grad(
            present_value, key_portion=key_portion, value_portion=value_portion, allowed=allowed
        ):
            probs = jnp.exp(
                block_scores(query_matrix, key_portion, allowed) - running_totals[..., None]
            )
            grad_probs = jnp.einsum(
                "sikgd,sjkd->skgij",
                mixed_gradient,
                value_portion,
                preferred_element_type=jnp.float32,
            )
            grad_scores = (probs * (grad_probs - delta[..., None])).astype(jnp.bfloat16)
            updated = present_value + jnp.einsum(
                "skgij,sjkd->sikgd", grad_scores, key_portion, preferred_element_type=jnp.float32
            ) * HEAD_SIZE ** (-0.5)
            grad_keys = jnp.einsum(
                "skgij,sikgd->sjkd", grad_scores, query_matrix, preferred_element_type=jnp.float32
            ) * HEAD_SIZE ** (-0.5)
            grad_values = jnp.einsum(
                "skgij,sikgd->sjkd",
                probs.astype(jnp.bfloat16),
                mixed_gradient,
                preferred_element_type=jnp.float32,
            )
            both_parts = jnp.concatenate(
                [
                    grad_keys.reshape(sequence_count, key_tile_block, -1),
                    grad_values.reshape(sequence_count, key_tile_block, -1),
                ],
                -1,
            )
            return (updated, both_parts)

        def dead_grad(present_value):
            return (
                present_value,
                jnp.zeros(
                    (sequence_count, key_tile_block, 2 * KEY_VALUE_HEADS * HEAD_SIZE), jnp.float32
                ),
            )

        grad_queries, block_term = lax.cond(jnp.any(allowed), live_grad, dead_grad, grad_queries)
        key_terms.append(block_term)
    return (grad_queries, jnp.concatenate(key_terms, 1), delta)


def expert_forward(inner_use, outer_use, received):
    model_width = received.shape[-1]
    rows_in = received.reshape(-1, model_width)
    pre_rows = jnp.dot(rows_in, inner_use, preferred_element_type=jnp.float32)
    slab_width = outer_use.shape[0]
    hidden_rows = (jax.nn.silu(pre_rows[:, :slab_width]) * pre_rows[:, slab_width:]).astype(
        jnp.bfloat16
    )
    part_rows = jnp.dot(hidden_rows, outer_use, preferred_element_type=jnp.float32).astype(
        jnp.bfloat16
    )
    return part_rows.reshape(received.shape)


def expert_back(inner_use, outer_use, rows_flat, grad_flat):
    pre_rows = jnp.dot(rows_flat, inner_use, preferred_element_type=jnp.float32)
    slab_width = outer_use.shape[0]
    gate_pre = pre_rows[:, :slab_width]
    up_pre = pre_rows[:, slab_width:]
    sigma = jax.nn.sigmoid(gate_pre)
    swish = gate_pre * sigma
    hidden_rows = (swish * up_pre).astype(jnp.bfloat16)
    grad_hidden = jnp.dot(grad_flat, outer_use.T, preferred_element_type=jnp.float32)
    grad_gate = grad_hidden * up_pre * sigma * (1.0 + gate_pre * (1.0 - sigma))
    grad_up = grad_hidden * swish
    grad_pre = jnp.concatenate([grad_gate, grad_up], 1).astype(jnp.bfloat16)
    grad_in = jnp.dot(grad_pre, inner_use.T, preferred_element_type=jnp.float32).astype(
        jnp.bfloat16
    )
    return (hidden_rows, grad_pre, grad_in)


def per_device(
    tokens,
    segment_ids,
    routes,
    query_weight,
    key_value_weight,
    output_weight,
    router_weight,
    gain_before,
    gain_middle,
    inner_weight,
    outer_weight,
    cotangent,
):
    sequence_count, resident_rows, model_width = tokens.shape
    token_count = sequence_count * resident_rows
    experts = router_weight.shape[1]
    copies = lax.axis_size("fsdp") // experts
    capacity = 3 * token_count // 8
    seg_all = lax.all_gather(segment_ids, "fsdp", axis=1, tiled=True)
    seq_length = seg_all.shape[1]
    key_tile_block = min(256, seq_length)
    positions = lax.axis_index("fsdp") * resident_rows + jnp.arange(resident_rows, dtype=jnp.int32)
    block_masks = [
        mask_for(seg_all, segment_ids, positions, offset, key_tile_block)
        for offset in range(0, seq_length, key_tile_block)
    ]
    start_rows = tokens.reshape(token_count, model_width).astype(jnp.float32)
    route_flat = routes.reshape(token_count * 2)
    picks = route_flat[:, None] == jnp.arange(experts, dtype=jnp.int32)[None, :]
    marks = picks.astype(jnp.int32)
    slot_index = route_flat * capacity + jnp.sum((jnp.cumsum(marks, 0) - marks) * marks, 1)
    chosen_mask = picks.reshape(token_count, 2, experts)

    def layer_weights():
        return (
            lax.all_gather(query_weight, ("dp", "fsdp"), axis=0, tiled=True),
            lax.all_gather(key_value_weight, ("dp", "fsdp"), axis=0, tiled=True),
            lax.all_gather(output_weight, ("dp", "fsdp"), axis=1, tiled=True),
            lax.all_gather(router_weight, ("dp", "fsdp"), axis=0, tiled=True),
            lax.all_gather(gain_before, ("dp", "fsdp"), axis=0, tiled=True),
            lax.all_gather(gain_middle, ("dp", "fsdp"), axis=0, tiled=True),
        )

    def expert_weights():
        inner_full, outer_full = (
            lax.all_gather(inner_weight, "dp", axis=0, tiled=True),
            lax.all_gather(outer_weight, "dp", axis=1, tiled=True),
        )
        return (inner_full.reshape(model_width, -1), outer_full)

    def attention_front(weights):
        normed, unit_rows, factor = normalize(start_rows, weights[4])
        normed_low = normed.astype(jnp.bfloat16)
        query_matrix = jnp.dot(normed_low, weights[0], preferred_element_type=jnp.float32).astype(
            jnp.bfloat16
        )
        query_matrix = query_matrix.reshape(
            sequence_count,
            resident_rows,
            KEY_VALUE_HEADS,
            QUERY_HEADS // KEY_VALUE_HEADS,
            HEAD_SIZE,
        )
        key_value_rows = jnp.dot(normed_low, weights[1], preferred_element_type=jnp.float32).astype(
            jnp.bfloat16
        )
        gathered = lax.all_gather(
            key_value_rows.reshape(sequence_count, resident_rows, -1), "fsdp", axis=1, tiled=True
        )
        return (normed_low, unit_rows, factor, query_matrix, gathered)

    def middle_part(weights, mixed_low):
        middle = start_rows + jnp.dot(mixed_low, weights[2], preferred_element_type=jnp.float32)
        expert_in, unit_rows, factor = normalize(middle, weights[5])
        expert_low = expert_in.astype(jnp.bfloat16)
        logits = jnp.dot(
            expert_low.astype(jnp.float32),
            weights[3].astype(jnp.float32),
            precision=HIGHEST_PRECISION,
        )
        return (middle, unit_rows, factor, expert_low, logits)

    def gates_for(logits):
        chosen_logits = jnp.sum(jnp.where(chosen_mask, logits[:, None, :], 0.0), -1)
        return jax.nn.softmax(chosen_logits, -1)

    def to_slots(pair_rows):
        packed = (
            jnp.zeros((experts * capacity, model_width), pair_rows.dtype)
            .at[slot_index]
            .set(pair_rows)
        )
        return jnp.repeat(packed.reshape(experts, capacity, model_width), copies, axis=0)

    def from_slots(returned_rows):
        summed = jnp.sum(
            returned_rows.reshape(experts, copies, capacity, model_width).astype(jnp.float32), 1
        )
        return summed.reshape(experts * capacity, model_width)[slot_index]

    weights = layer_weights()
    inner_all, outer_all = expert_weights()
    normed_low, unit_first, factor_first, query_matrix, gathered = attention_front(weights)
    running_totals = log_totals(query_matrix, gathered, block_masks, key_tile_block)
    mixed_low = attend_values(query_matrix, gathered, block_masks, key_tile_block, running_totals)
    middle, unit_second, factor_second, expert_low, logits = middle_part(weights, mixed_low)
    gates = gates_for(logits)
    sent = to_slots(jnp.repeat(expert_low, 2, axis=0))
    part_rows = expert_forward(
        inner_all, outer_all, lax.all_to_all(sent, "fsdp", split_axis=0, concat_axis=0, tiled=True)
    )
    returned_part = lax.all_to_all(part_rows, "fsdp", split_axis=0, concat_axis=0, tiled=True)
    returned_rows = returned_part
    expert_sum = from_slots(returned_rows).reshape(token_count, 2, model_width)
    block_out = (middle + jnp.sum(gates[..., None] * expert_sum, 1)).astype(jnp.bfloat16)
    grad_out = cotangent.reshape(token_count, model_width).astype(jnp.float32)
    weights = layer_weights()
    inner_use, outer_use = expert_weights()
    normed_low, unit_first, factor_first, query_matrix, gathered = attention_front(weights)
    mixed_low = attend_values(query_matrix, gathered, block_masks, key_tile_block, running_totals)
    middle, unit_second, factor_second, expert_low, logits = middle_part(weights, mixed_low)
    gates = gates_for(logits)
    sent = to_slots(jnp.repeat(expert_low, 2, axis=0))
    grad_sent = to_slots(
        (gates[..., None] * grad_out[:, None, :])
        .astype(jnp.bfloat16)
        .reshape(2 * token_count, model_width)
    )
    rows_in = lax.all_to_all(sent, "fsdp", split_axis=0, concat_axis=0, tiled=True)
    rows_grad = lax.all_to_all(grad_sent, "fsdp", split_axis=0, concat_axis=0, tiled=True)
    row_shape = rows_in.shape
    hidden_flat, grad_pre_flat, grad_in_flat = expert_back(
        inner_use, outer_use, rows_in.reshape(-1, model_width), rows_grad.reshape(-1, model_width)
    )
    part_rows = jnp.dot(hidden_flat, outer_use, preferred_element_type=jnp.float32).astype(
        jnp.bfloat16
    )
    grad_home = lax.all_to_all(
        grad_in_flat.reshape(row_shape), "fsdp", split_axis=0, concat_axis=0, tiled=True
    )
    part_home = lax.all_to_all(
        part_rows.reshape(row_shape), "fsdp", split_axis=0, concat_axis=0, tiled=True
    )
    item_shape = row_shape[:2]
    grad_pre = grad_pre_flat.reshape(item_shape + (-1,))
    hidden_rows = hidden_flat.reshape(item_shape + (-1,))
    expert_sum = from_slots(part_home).reshape(token_count, 2, model_width)
    rows_flat = rows_in.reshape(-1, model_width)
    row_total = rows_flat.shape[0]
    inner_grad_all = jnp.dot(
        rows_flat.T, grad_pre.reshape(row_total, -1), preferred_element_type=jnp.float32
    )
    outer_grad_all = jnp.dot(
        hidden_rows.reshape(row_total, -1).T,
        rows_grad.reshape(row_total, model_width),
        preferred_element_type=jnp.float32,
    )
    inner_grad, outer_grad = (
        lax.psum_scatter(
            inner_grad_all.reshape(model_width, 2, -1).astype(jnp.bfloat16),
            "dp",
            scatter_dimension=0,
            tiled=True,
        ).astype(jnp.float32),
        lax.psum_scatter(
            outer_grad_all.astype(jnp.bfloat16), "dp", scatter_dimension=1, tiled=True
        ).astype(jnp.float32),
    )
    grad_gates = jnp.sum(grad_out[:, None, :] * expert_sum, -1)
    grad_choice = gates * (grad_gates - jnp.sum(gates * grad_gates, -1, keepdims=True))
    grad_logits = jnp.sum(jnp.where(chosen_mask, grad_choice[..., None], 0.0), 1)
    router_grad_all = jnp.dot(
        expert_low.astype(jnp.float32).T, grad_logits, precision=HIGHEST_PRECISION
    )
    grad_expert_in = jnp.sum(from_slots(grad_home).reshape(token_count, 2, model_width), 1)
    grad_expert_in = grad_expert_in + jnp.dot(
        grad_logits, weights[3].astype(jnp.float32).T, precision=HIGHEST_PRECISION
    )
    grad_norm_second, middle_gain_grad = normalize_back(
        grad_expert_in, unit_second, factor_second, weights[5]
    )
    grad_middle = grad_out + grad_norm_second
    grad_branch = grad_middle.astype(jnp.bfloat16)
    output_grad_all = jnp.dot(mixed_low.T, grad_branch, preferred_element_type=jnp.float32)
    mixed_gradient = jnp.dot(grad_branch, weights[2].T, preferred_element_type=jnp.float32).astype(
        jnp.bfloat16
    )
    mixed_gradient = mixed_gradient.reshape(
        sequence_count, resident_rows, KEY_VALUE_HEADS, QUERY_HEADS // KEY_VALUE_HEADS, HEAD_SIZE
    )
    grad_queries, key_terms, delta = attend_back(
        query_matrix, mixed_gradient, gathered, block_masks, key_tile_block, running_totals
    )
    key_grads = lax.psum_scatter(
        key_terms.astype(jnp.bfloat16), "fsdp", scatter_dimension=1, tiled=True
    ).reshape(token_count, -1)
    query_low = grad_queries.reshape(token_count, -1).astype(jnp.bfloat16)
    grad_normed = jnp.dot(query_low, weights[0].T, preferred_element_type=jnp.float32) + jnp.dot(
        key_grads, weights[1].T, preferred_element_type=jnp.float32
    )
    query_grad_all = jnp.dot(normed_low.T, query_low, preferred_element_type=jnp.float32)
    keyval_grad_all = jnp.dot(normed_low.T, key_grads, preferred_element_type=jnp.float32)
    grad_norm_first, before_gain_grad = normalize_back(
        grad_normed, unit_first, factor_first, weights[4]
    )
    tokens_grad = grad_middle + grad_norm_first
    summed_grads = (
        lax.psum_scatter(query_grad_all, ("dp", "fsdp"), scatter_dimension=0, tiled=True),
        lax.psum_scatter(keyval_grad_all, ("dp", "fsdp"), scatter_dimension=0, tiled=True),
        lax.psum_scatter(output_grad_all, ("dp", "fsdp"), scatter_dimension=1, tiled=True),
        lax.psum_scatter(router_grad_all, ("dp", "fsdp"), scatter_dimension=0, tiled=True),
        lax.psum_scatter(before_gain_grad, ("dp", "fsdp"), scatter_dimension=0, tiled=True),
        lax.psum_scatter(middle_gain_grad, ("dp", "fsdp"), scatter_dimension=0, tiled=True),
    )
    return (
        block_out.reshape(sequence_count, resident_rows, model_width),
        tokens_grad.reshape(sequence_count, resident_rows, model_width),
        summed_grads[0],
        summed_grads[1],
        summed_grads[2],
        summed_grads[3],
        summed_grads[4],
        summed_grads[5],
        inner_grad,
        outer_grad,
    )


def attend_kernel(spans, q_ref, k_ref, v_ref, segr_ref, segc_ref, o_ref, ot_ref, lse_ref):
    step = pl.program_id(0)
    block = q_ref.shape[0]
    heads = q_ref.shape[1] // HEAD_SIZE
    queries = q_ref[...] * jnp.bfloat16(HEAD_SIZE ** (-0.5))
    stacked = jnp.concatenate(
        [queries[:, h * HEAD_SIZE : (h + 1) * HEAD_SIZE] for h in range(heads)], 0
    )
    seg_row = segr_ref[...]

    def scores_of(j):
        keys = k_ref[pl.ds(pl.multiple_of(j * block, block), block), :]
        return lax.dot_general(
            keys, stacked, (((1,), (1,)), ((), ())), preferred_element_type=jnp.float32
        )

    def same_doc(j):
        seg_col = segc_ref[pl.ds(pl.multiple_of(j * block, block), block), :]
        return seg_col == seg_row

    def fold(j, scores, carry):
        top, total, out = carry
        values = v_ref[pl.ds(pl.multiple_of(j * block, block), block), :]
        new_top = jnp.maximum(top, jnp.max(scores, 0, keepdims=True))
        probs = jnp.exp(scores - new_top)
        decay = jnp.exp(top - new_top)
        total = total * decay + jnp.sum(probs, 0, keepdims=True)
        out = out * decay + lax.dot_general(
            values,
            probs.astype(jnp.bfloat16),
            (((0,), (0,)), ((), ())),
            preferred_element_type=jnp.float32,
        )
        return (new_top, total, out)

    def masked(j, carry):
        allowed = jnp.concatenate([same_doc(j)] * heads, 1)
        return fold(j, jnp.where(allowed, scores_of(j), NEGATIVE_LARGE), carry)

    def whole(j, carry):
        return fold(j, scores_of(j), carry)

    columns = heads * block
    carry = (
        jnp.full((1, columns), NEGATIVE_LARGE, jnp.float32),
        jnp.zeros((1, columns), jnp.float32),
        jnp.zeros((HEAD_SIZE, columns), jnp.float32),
    )
    first, full = spans[0, step], spans[1, step]
    carry = lax.fori_loop(first, full, masked, carry)
    carry = lax.fori_loop(full, step, whole, carry)
    key_spot = lax.broadcasted_iota(jnp.int32, (block, block), 0)
    query_spot = lax.broadcasted_iota(jnp.int32, (block, block), 1)
    allowed = same_doc(step) & (key_spot <= query_spot)
    allowed = jnp.concatenate([allowed] * heads, 1)
    top, total, out = fold(step, jnp.where(allowed, scores_of(step), NEGATIVE_LARGE), carry)
    out = out / total
    totals = top + jnp.log(total)
    for h in range(heads):
        part = out[:, h * block : (h + 1) * block]
        ot_ref[h * HEAD_SIZE : (h + 1) * HEAD_SIZE, :] = part
        lse_ref[h : h + 1, :] = totals[:, h * block : (h + 1) * block]
    o_ref[...] = jnp.concatenate(
        [out[:, h * block : (h + 1) * block].T for h in range(heads)], 1
    ).astype(jnp.bfloat16)


def attend_back_kernel(
    spans, q_ref, g_ref, k_ref, v_ref, segr_ref, segc_ref, ot_ref, lse_ref,
    dq_ref, dkv_ref, dk_sum, dv_sum,
):
    step = pl.program_id(0)
    block = q_ref.shape[0]
    heads = q_ref.shape[1] // HEAD_SIZE
    queries = q_ref[...] * jnp.bfloat16(HEAD_SIZE ** (-0.5))
    grads = g_ref[...]
    cuts = [slice(h * HEAD_SIZE, (h + 1) * HEAD_SIZE) for h in range(heads)]
    stacked = jnp.concatenate([queries[:, cut] for cut in cuts], 0)
    stacked_grad = jnp.concatenate([grads[:, cut] for cut in cuts], 0)
    delta = jnp.concatenate(
        [
            jnp.sum(grads[:, cut].astype(jnp.float32).T * ot_ref[cut, :], 0, keepdims=True)
            for cut in cuts
        ],
        1,
    )
    totals = jnp.concatenate([lse_ref[h : h + 1, :] for h in range(heads)], 1)
    seg_row = segr_ref[...]

    @pl.when(step == 0)
    def _():
        dk_sum[...] = jnp.zeros_like(dk_sum)
        dv_sum[...] = jnp.zeros_like(dv_sum)

    def turn(j, query_sum, allowed):
        rows = pl.ds(pl.multiple_of(j * block, block), block)
        keys, values = k_ref[rows, :], v_ref[rows, :]
        scores = lax.dot_general(
            keys, stacked, (((1,), (1,)), ((), ())), preferred_element_type=jnp.float32
        )
        probs = jnp.exp(scores - totals)
        if allowed is not None:
            probs = jnp.where(jnp.concatenate([allowed] * heads, 1), probs, 0.0)
        grad_probs = lax.dot_general(
            values, stacked_grad, (((1,), (1,)), ((), ())), preferred_element_type=jnp.float32
        )
        grad_scores = (probs * (grad_probs - delta)).astype(jnp.bfloat16)
        dv_sum[rows, :] += jnp.dot(
            probs.astype(jnp.bfloat16), stacked_grad, preferred_element_type=jnp.float32
        )
        dk_sum[rows, :] += jnp.dot(grad_scores, stacked, preferred_element_type=jnp.float32)
        return query_sum + lax.dot_general(
            keys, grad_scores, (((0,), (0,)), ((), ())), preferred_element_type=jnp.float32
        )

    def same_doc(j):
        seg_col = segc_ref[pl.ds(pl.multiple_of(j * block, block), block), :]
        return seg_col == seg_row

    query_sum = jnp.zeros((HEAD_SIZE, heads * block), jnp.float32)
    first, full = spans[0, step], spans[1, step]
    query_sum = lax.fori_loop(first, full, lambda j, c: turn(j, c, same_doc(j)), query_sum)
    query_sum = lax.fori_loop(full, step, lambda j, c: turn(j, c, None), query_sum)
    key_spot = lax.broadcasted_iota(jnp.int32, (block, block), 0)
    query_spot = lax.broadcasted_iota(jnp.int32, (block, block), 1)
    query_sum = turn(step, query_sum, same_doc(step) & (key_spot <= query_spot))
    query_sum = query_sum * HEAD_SIZE ** (-0.5)
    dq_ref[...] = jnp.concatenate(
        [query_sum[:, h * block : (h + 1) * block].T for h in range(heads)], 1
    ).astype(jnp.bfloat16)

    @pl.when(step == pl.num_programs(0) - 1)
    def _():
        dkv_ref[...] = jnp.concatenate([dk_sum[...], dv_sum[...]], 1).astype(jnp.bfloat16)


def attention_specs(length, block, wide):
    along = lambda width: pl.BlockSpec((block, width), lambda i, spans: (i, 0))
    across = lambda height: pl.BlockSpec((height, block), lambda i, spans: (0, i))
    fixed = lambda width: pl.BlockSpec((length, width), lambda i, spans: (0, 0))
    return along, across, fixed


def attend(spans, queries, keys, values, seg_row, seg_col, block):
    length, wide = queries.shape
    along, across, fixed = attention_specs(length, block, wide)
    return pl.pallas_call(
        attend_kernel,
        grid_spec=pltpu.PrefetchScalarGridSpec(
            num_scalar_prefetch=1,
            grid=(length // block,),
            in_specs=[along(wide), fixed(HEAD_SIZE), fixed(HEAD_SIZE), across(1), fixed(1)],
            out_specs=[along(wide), across(wide), across(8)],
        ),
        out_shape=[
            jax.ShapeDtypeStruct((length, wide), jnp.bfloat16),
            jax.ShapeDtypeStruct((wide, length), jnp.float32),
            jax.ShapeDtypeStruct((8, length), jnp.float32),
        ],
        compiler_params=pltpu.CompilerParams(vmem_limit_bytes=48 * 2**20),
        name="attend",
    )(spans, queries, keys, values, seg_row, seg_col)


def attend_backward(
    spans, queries, grads, keys, values, seg_row, seg_col, mixed_t, totals, block
):
    length, wide = queries.shape
    along, across, fixed = attention_specs(length, block, wide)
    return pl.pallas_call(
        attend_back_kernel,
        grid_spec=pltpu.PrefetchScalarGridSpec(
            num_scalar_prefetch=1,
            grid=(length // block,),
            in_specs=[
                along(wide), along(wide), fixed(HEAD_SIZE), fixed(HEAD_SIZE), across(1), fixed(1),
                across(wide), across(8),
            ],
            out_specs=[along(wide), fixed(2 * HEAD_SIZE)],
            scratch_shapes=[
                pltpu.VMEM((length, HEAD_SIZE), jnp.float32),
                pltpu.VMEM((length, HEAD_SIZE), jnp.float32),
            ],
        ),
        out_shape=[
            jax.ShapeDtypeStruct((length, wide), jnp.bfloat16),
            jax.ShapeDtypeStruct((length, 2 * HEAD_SIZE), jnp.bfloat16),
        ],
        compiler_params=pltpu.CompilerParams(vmem_limit_bytes=48 * 2**20),
        name="attend_backward",
    )(spans, queries, grads, keys, values, seg_row, seg_col, mixed_t, totals)


def flip_exchange(block, axis, flip):
    count = lax.axis_size(axis)
    return lax.ppermute(block, axis, [(i, i ^ flip) for i in range(count)])


def swap_blocks(blocks, axis):
    return [blocks[0]] + [flip_exchange(blocks[k], axis, k) for k in range(1, len(blocks))]


def line_gather(own):
    count = lax.axis_size("fsdp")
    chips = count // 2
    place = lax.axis_index("fsdp") // 2
    ups, downs = [own], [own]
    for step in range(1, chips):
        ups.append(
            lax.ppermute(ups[-1], "fsdp", [(i, i + 2) for i in range(2 * (step - 1), count - 2)])
        )
        downs.append(
            lax.ppermute(
                downs[-1], "fsdp", [(i, i - 2) for i in range(2, count - 2 * (step - 1))]
            )
        )
    return [own] + [
        jnp.where(place >= step, ups[step], downs[chips - step]) for step in range(1, chips)
    ]


def gather_tokens(own):
    count = lax.axis_size("fsdp")
    chips = count // 2
    index = lax.axis_index("fsdp")
    place, core = index // 2, index % 2
    rows, width = own.shape
    mine = line_gather(own)
    theirs = [flip_exchange(block, "fsdp", 1) for block in mine]
    whole = jnp.zeros((count * rows, width), own.dtype)
    for step in range(chips):
        chip = lax.rem(place - step + chips, chips)
        whole = lax.dynamic_update_slice_in_dim(whole, mine[step], (2 * chip + core) * rows, 0)
        whole = lax.dynamic_update_slice_in_dim(whole, theirs[step], (2 * chip + 1 - core) * rows, 0)
    return whole


def gather_over_dp(block, order):
    other = 3 - order
    near = flip_exchange(block, "dp", order)
    side = flip_exchange(block, "dp", other)
    far = flip_exchange(near, "dp", other)
    parts = [block, None, None, None]
    parts[order], parts[other], parts[3] = near, side, far
    return parts


def scatter_over_dp(parts, order):
    other = 3 - order
    near = flip_exchange(parts[order].astype(jnp.bfloat16), "dp", order)
    far = flip_exchange(parts[3].astype(jnp.bfloat16), "dp", order)
    passed = (parts[other] + far.astype(jnp.float32)).astype(jnp.bfloat16)
    side = flip_exchange(passed, "dp", other)
    return parts[0] + near.astype(jnp.float32) + side.astype(jnp.float32)


def in_order(parts, axis):
    stacked = jnp.stack(parts)
    index = lax.axis_index(axis)
    return jnp.stack(
        [
            lax.dynamic_index_in_dim(stacked, jnp.bitwise_xor(index, j), 0, keepdims=False)
            for j in range(len(parts))
        ]
    )


def split_low(value, pieces):
    parts = []
    for _ in range(pieces):
        part = value.astype(jnp.bfloat16)
        parts.append(part)
        value = value - part.astype(jnp.float32)
    return parts


def all_to_all(blocks):
    return lax.all_to_all(blocks, "fsdp", split_axis=0, concat_axis=0, tiled=True)


def per_device_heads(
    tokens,
    segment_ids,
    routes,
    query_weight,
    key_value_weight,
    output_weight,
    router_weight,
    gain_before,
    gain_middle,
    inner_weight,
    outer_weight,
    cotangent,
):
    f32, low = jnp.float32, jnp.bfloat16
    _, rows, width = tokens.shape
    count = lax.axis_size("fsdp")
    experts = router_weight.shape[1]
    index, group = lax.axis_index("fsdp"), lax.axis_index("dp")
    capacity = 3 * rows // 8
    length = count * rows
    shard = query_weight.shape[0]
    share = QUERY_HEADS // KEY_VALUE_HEADS * HEAD_SIZE
    cols = share + 2 * HEAD_SIZE
    half = KEY_VALUE_HEADS * HEAD_SIZE
    ff = outer_weight.shape[0]

    start_low = tokens.reshape(rows, width)
    cot_low = cotangent.reshape(rows, width)

    route = routes.reshape(rows, 2)
    route_flat = route.reshape(rows * 2)
    picks = route_flat[:, None] == jnp.arange(experts, dtype=jnp.int32)[None, :]
    before = jnp.dot(
        jnp.tril(jnp.ones((rows * 2, rows * 2), low), -1),
        picks.astype(low),
        preferred_element_type=f32,
    )
    rank = jnp.sum(jnp.where(picks, before, 0.0), 1).astype(jnp.int32).reshape(rows, 2)
    slots = jnp.arange(experts * capacity, dtype=jnp.int32)
    slot_near = jnp.bitwise_xor(route, index) * capacity + rank
    hit = [slot_near[:, c][None, :] == slots[:, None] for c in range(2)]
    to_slots = (hit[0] | hit[1]).astype(low)
    slot_named = route * capacity + rank
    named = [slot_named[:, c][None, :] == slots[:, None] for c in range(2)]
    other_route = jnp.sum(
        jnp.where(named[0], route[:, 1][None, :], 0) + jnp.where(named[1], route[:, 0][None, :], 0),
        1,
    )

    by_head = jnp.concatenate(
        [
            query_weight.reshape(shard, count, share),
            key_value_weight[:, :half].reshape(shard, count, HEAD_SIZE),
            key_value_weight[:, half:].reshape(shard, count, HEAD_SIZE),
        ],
        2,
    )
    lanes = 128 * -(-(cols + 2 + experts) // 128)
    extras = jnp.concatenate([gain_before[:, None], gain_middle[:, None], router_weight], 1)
    extras = jnp.broadcast_to(extras[None], (count, shard, 2 + experts))
    head_block = jnp.concatenate([by_head.transpose(1, 0, 2), extras], 2)
    head_block = jnp.pad(head_block, ((0, 0), (0, 0), (0, lanes - cols - 2 - experts)))
    seg_line = jnp.broadcast_to(segment_ids.reshape(1, 1, rows), (count, 1, rows)).astype(low)
    seg_line = jnp.pad(seg_line, ((0, 0), (0, 0), (0, lanes - rows)))
    other_line = other_route.reshape(experts, 1, capacity).astype(low)
    other_line = jnp.pad(other_line, ((0, 0), (0, 14), (0, lanes - capacity)))
    arrived = all_to_all(jnp.concatenate([head_block, seg_line, other_line], 1))
    segments = arrived[:, shard, :rows].reshape(length).astype(jnp.int32)
    other_expert = arrived[:, shard + 1, :capacity].astype(jnp.int32)
    other_expert = jnp.concatenate(
        [
            lax.dynamic_index_in_dim(other_expert, jnp.bitwise_xor(index, k), 0, keepdims=False)
            for k in range(count)
        ]
    )
    head_rows = arrived[:, :shard].reshape(count * shard, lanes)
    head_weights = in_order(gather_over_dp(head_rows, 1), "dp").reshape(width, lanes)
    head_weight = head_weights[:, :cols]
    gain_first = head_weights[:, cols].astype(f32)
    gain_second = head_weights[:, cols + 1].astype(f32)
    router = head_weights[:, cols + 2 : cols + 2 + experts]

    inner_parts = gather_over_dp(inner_weight.reshape(inner_weight.shape[0], 2 * ff), 1)
    outer_parts = gather_over_dp(outer_weight, 2)
    inner_all = in_order(inner_parts, "dp").reshape(width, 2 * ff)
    outer_all = in_order(outer_parts, "dp").transpose(1, 0, 2).reshape(ff, width)

    output_all = lax.all_gather(output_weight.T, ("dp", "fsdp"), axis=0, tiled=True)
    project_all = lax.all_gather(
        by_head.reshape(shard, count * cols), ("dp", "fsdp"), axis=0, tiled=True
    )

    tokens_all = gather_tokens(start_low)
    normed, _, _ = normalize(tokens_all.astype(f32), gain_first)
    normed_low = normed.astype(low)
    projected = jnp.dot(normed_low, head_weight, preferred_element_type=f32).astype(low)
    queries = projected[:, :share]
    keys = projected[:, share : share + HEAD_SIZE]
    values = projected[:, share + HEAD_SIZE :]
    block = rows
    firsts = segments.reshape(length // block, block)
    starts = jnp.sum(segments[None, :] < firsts[:, :1], 1) // block
    wholes = (jnp.sum(segments[None, :] < firsts[:, -1:], 1) + block - 1) // block
    wholes = jnp.minimum(wholes, jnp.arange(length // block))
    spans = jnp.stack([starts, wholes]).astype(jnp.int32)
    seg_row, seg_col = segments.reshape(1, length), segments.reshape(length, 1)
    mixed_head, mixed_t, totals = attend(spans, queries, keys, values, seg_row, seg_col, block)
    mixed_low = (
        all_to_all(mixed_head.reshape(count, rows, share)).transpose(1, 0, 2).reshape(rows, width)
    )

    start = start_low.astype(f32)
    middle = start + lax.dot_general(
        mixed_low, output_all, (((1,), (1,)), ((), ())), preferred_element_type=f32
    )
    expert_in, unit_second, factor_second = normalize(middle, gain_second)
    expert_low = expert_in.astype(low)
    logits = jnp.dot(expert_low, router, preferred_element_type=f32)
    chosen = picks.reshape(rows, 2, experts)
    gates = jax.nn.softmax(jnp.sum(jnp.where(chosen, logits[:, None, :], 0.0), -1), -1)

    def by_slot(source):
        return [
            jnp.dot(
                to_slots[k * capacity : (k + 1) * capacity], source, preferred_element_type=f32
            ).astype(low)
            for k in range(experts)
        ]

    cot_in = jnp.concatenate(swap_blocks(by_slot(cot_low), "fsdp"))
    rows_in = jnp.concatenate(swap_blocks(by_slot(expert_low), "fsdp"))
    slot_logits = jnp.dot(rows_in, router, preferred_element_type=f32)
    own_hot = jnp.arange(experts) == index
    other_hot = other_expert[:, None] == jnp.arange(experts)[None, :]
    own_logit = jnp.sum(jnp.where(own_hot[None, :], slot_logits, 0.0), 1)
    other_logit = jnp.sum(jnp.where(other_hot, slot_logits, 0.0), 1)
    slot_gates = jax.nn.softmax(jnp.stack([own_logit, other_logit], 1), -1)
    cot_rows = cot_in.astype(f32)
    grad_in = (slot_gates[:, :1] * cot_rows).astype(low)
    hidden, grad_pre, grad_rows = expert_back(inner_all, outer_all, rows_in, grad_in)
    part = jnp.dot(hidden, outer_all, preferred_element_type=f32).astype(low)
    grad_gate = jnp.sum(cot_rows * part.astype(f32), 1)
    slope = slot_gates[:, 0] * slot_gates[:, 1] * grad_gate
    sides = own_hot[None, :].astype(f32) - other_hot.astype(f32)
    logit_grads = jnp.concatenate(split_low(slope[:, None] * sides, 2), 1)
    grad_rows = grad_rows.astype(f32) + jnp.dot(
        logit_grads, jnp.concatenate([router, router], 1).T, preferred_element_type=f32
    )
    grad_rows = grad_rows.astype(low)
    router_parts = lax.dot_general(
        rows_in, logit_grads, (((0,), (0,)), ((), ())), preferred_element_type=f32
    )
    router_part = router_parts[:, :experts] + router_parts[:, experts:]

    def cut(value, k, size):
        at = jnp.bitwise_xor(group, k) * size
        return lax.dynamic_slice_in_dim(value, at, size, 1)

    def pieces(value, blocks):
        return [value[k * capacity : (k + 1) * capacity] for k in range(blocks)]

    grad_home = jnp.concatenate(swap_blocks(pieces(grad_rows, experts), "fsdp"))
    part_home = jnp.concatenate(swap_blocks(pieces(part, experts), "fsdp"))
    size = inner_weight.shape[0]
    inner_terms = [
        lax.dot_general(
            cut(rows_in, k, size), grad_pre, (((0,), (0,)), ((), ())), preferred_element_type=f32
        )
        for k in range(4)
    ]
    outer_terms = [
        lax.dot_general(
            hidden, cut(grad_in, k, size), (((0,), (0,)), ((), ())), preferred_element_type=f32
        )
        for k in range(4)
    ]
    inner_grad = scatter_over_dp(inner_terms, 1).reshape(size, 2, ff)
    outer_grad = scatter_over_dp(outer_terms, 2)

    grad_out = cot_low.astype(f32)
    grad_expert_in = lax.dot_general(
        to_slots, grad_home, (((0,), (0,)), ((), ())), preferred_element_type=f32
    )
    inner_back, middle_part = normalize_back(
        grad_expert_in, unit_second, factor_second, gain_second
    )
    grad_middle = grad_out + inner_back
    grad_branch = grad_middle.astype(low)
    mixed_grad = jnp.dot(grad_branch, output_all, preferred_element_type=f32).astype(low)
    mixed_grad = all_to_all(mixed_grad.reshape(rows, count, share).transpose(1, 0, 2)).reshape(
        length, share
    )
    output_part = lax.dot_general(
        grad_branch, mixed_low, (((0,), (0,)), ((), ())), preferred_element_type=f32
    )
    output_grad = lax.psum_scatter(
        output_part, ("dp", "fsdp"), scatter_dimension=0, tiled=True
    ).T
    gate_terms = split_low(gates, 3)
    combine = [
        jnp.where(hit[0], gate[:, 0][None, :], 0) + jnp.where(hit[1], gate[:, 1][None, :], 0)
        for gate in gate_terms
    ]
    mixture = sum(
        lax.dot_general(term, part_home, (((0,), (0,)), ((), ())), preferred_element_type=f32)
        for term in combine
    )
    block_out = (middle + mixture).astype(low)

    grad_queries, grad_keyvals = attend_backward(
        spans, queries, mixed_grad, keys, values, seg_row, seg_col, mixed_t, totals, block
    )
    grad_heads = jnp.concatenate([grad_queries, grad_keyvals], 1)
    weight_part = lax.dot_general(
        normed_low, grad_heads, (((0,), (0,)), ((), ())), preferred_element_type=f32
    )
    weight_part = jnp.concatenate([weight_part, middle_part[:, None], router_part], 1)
    weight_part = jnp.pad(weight_part, ((0, 0), (0, lanes - cols - 1 - experts)))
    span = count * shard
    terms = [
        lax.dynamic_slice_in_dim(weight_part, jnp.bitwise_xor(group, k) * span, span, 0)
        for k in range(4)
    ]
    weight_sum = scatter_over_dp(terms, 1).astype(low)
    weight_home = all_to_all(weight_sum.reshape(count, shard, lanes)).astype(f32)
    query_grad = weight_home[:, :, :share].transpose(1, 0, 2).reshape(shard, count * share)
    key_grad = weight_home[:, :, share : share + HEAD_SIZE].transpose(1, 0, 2)
    value_grad = weight_home[:, :, share + HEAD_SIZE : cols].transpose(1, 0, 2)
    keyval_grad = jnp.concatenate(
        [key_grad.reshape(shard, half), value_grad.reshape(shard, half)], 1
    )
    small = jnp.sum(weight_home[:, :, cols : cols + 1 + experts], 0)
    middle_grad, router_grad = small[:, 0], small[:, 1:]
    before_grad = (
        jnp.sum(query_grad * query_weight.astype(f32), 1)
        + jnp.sum(keyval_grad * key_value_weight.astype(f32), 1)
    ) / gain_before.astype(f32)

    grad_mine = all_to_all(grad_heads.reshape(count, rows, cols))
    grad_mine = grad_mine.transpose(1, 0, 2).reshape(rows, count * cols)
    grad_normed = lax.dot_general(
        grad_mine, project_all, (((1,), (1,)), ((), ())), preferred_element_type=f32
    )
    _, unit_first, factor_first = normalize(start, gain_first)
    outer_back, _ = normalize_back(grad_normed, unit_first, factor_first, gain_first)
    tokens_grad = grad_middle + outer_back
    return (
        block_out[None],
        tokens_grad[None],
        query_grad,
        keyval_grad,
        output_grad,
        router_grad,
        before_grad,
        middle_grad,
        inner_grad,
        outer_grad,
    )


def solution(mesh):
    by_heads = (mesh.shape["dp"], mesh.shape["fsdp"]) == (4, KEY_VALUE_HEADS)
    in_specs = (
        P("dp", "fsdp", None),
        P("dp", "fsdp"),
        P("dp", "fsdp", None),
        P(("dp", "fsdp"), None),
        P(("dp", "fsdp"), None),
        P(None, ("dp", "fsdp")),
        P(("dp", "fsdp"), None),
        P(("dp", "fsdp")),
        P(("dp", "fsdp")),
        P("dp", None, "fsdp"),
        P("fsdp", "dp"),
        P("dp", "fsdp", None),
    )
    out_specs = (
        P("dp", "fsdp", None),
        P("dp", "fsdp", None),
        P(("dp", "fsdp"), None),
        P(("dp", "fsdp"), None),
        P(None, ("dp", "fsdp")),
        P(("dp", "fsdp"), None),
        P(("dp", "fsdp")),
        P(("dp", "fsdp")),
        P("dp", None, "fsdp"),
        P("fsdp", "dp"),
    )
    return jax.shard_map(
        per_device_heads if by_heads else per_device, mesh=mesh, in_specs=in_specs, out_specs=out_specs, check_vma=False
    )
```

```python
import functools

import jax
import jax.numpy as jnp
from jax import lax
from jax.experimental import pallas as pl
from jax.experimental.pallas import tpu as pltpu
from jax.sharding import PartitionSpec as P

QUERY_HEADS = 24
KEY_VALUE_HEADS = 8
HEAD_SIZE = 64


HIGHEST_PRECISION = lax.Precision.HIGHEST
EPSILON = 1e-05
NEGATIVE_LARGE = -1e30


def normalize(hidden, gain_vec):
    factor = lax.rsqrt(jnp.mean(hidden * hidden, -1, keepdims=True) + EPSILON)
    unit_rows = hidden * factor
    return (unit_rows * gain_vec.astype(jnp.float32), unit_rows, factor)


def normalize_back(grad_rows, unit_rows, factor, gain_vec):
    scaled = grad_rows * gain_vec.astype(jnp.float32)
    inner_part = factor * (scaled - unit_rows * jnp.mean(scaled * unit_rows, -1, keepdims=True))
    return (inner_part, jnp.sum(grad_rows * unit_rows, 0))


def split_block(gathered, offset, key_tile_block):
    sequence_count = gathered.shape[0]
    portion_rows = lax.slice_in_dim(gathered, offset, offset + key_tile_block, axis=1)
    half_columns = KEY_VALUE_HEADS * HEAD_SIZE
    key_portion = portion_rows[..., :half_columns].reshape(
        sequence_count, key_tile_block, KEY_VALUE_HEADS, HEAD_SIZE
    )
    value_portion = portion_rows[..., half_columns:].reshape(
        sequence_count, key_tile_block, KEY_VALUE_HEADS, HEAD_SIZE
    )
    return (key_portion, value_portion)


def block_scores(query_matrix, key_portion, allowed):
    raw_scores = jnp.einsum(
        "sikgd,sjkd->skgij", query_matrix, key_portion, preferred_element_type=jnp.float32
    ) * HEAD_SIZE ** (-0.5)
    return jnp.where(allowed[:, None, None], raw_scores, NEGATIVE_LARGE)


def mask_for(seg_all, seg_mine, positions, offset, key_tile_block):
    key_seg = lax.slice_in_dim(seg_all, offset, offset + key_tile_block, axis=1)
    key_spots = offset + jnp.arange(key_tile_block, dtype=jnp.int32)
    same_doc = seg_mine[:, :, None] == key_seg[:, None, :]
    causal = key_spots[None, None, :] <= positions[None, :, None]
    return same_doc & causal


def log_totals(query_matrix, gathered, block_masks, key_tile_block):
    sequence_count, resident_rows = (query_matrix.shape[0], query_matrix.shape[1])
    running_totals = jnp.full(
        (sequence_count, KEY_VALUE_HEADS, QUERY_HEADS // KEY_VALUE_HEADS, resident_rows),
        NEGATIVE_LARGE,
        jnp.float32,
    )
    for block_index, allowed in enumerate(block_masks):
        key_portion, value_portion = split_block(
            gathered, block_index * key_tile_block, key_tile_block
        )

        def log_live(present_value, key_portion=key_portion, allowed=allowed):
            scores = block_scores(query_matrix, key_portion, allowed)
            return jnp.logaddexp(present_value, jax.nn.logsumexp(scores, -1))

        running_totals = lax.cond(
            jnp.any(allowed), log_live, lambda present_value: present_value, running_totals
        )
    return running_totals


def attend_values(query_matrix, gathered, block_masks, key_tile_block, running_totals):
    result = jnp.zeros(query_matrix.shape, jnp.float32)
    for block_index, allowed in enumerate(block_masks):
        key_portion, value_portion = split_block(
            gathered, block_index * key_tile_block, key_tile_block
        )

        def attend_live(
            present_value, key_portion=key_portion, value_portion=value_portion, allowed=allowed
        ):
            probs = jnp.exp(
                block_scores(query_matrix, key_portion, allowed) - running_totals[..., None]
            ).astype(jnp.bfloat16)
            return present_value + jnp.einsum(
                "skgij,sjkd->sikgd", probs, value_portion, preferred_element_type=jnp.float32
            )

        result = lax.cond(
            jnp.any(allowed), attend_live, lambda present_value: present_value, result
        )
    token_count = query_matrix.shape[0] * query_matrix.shape[1]
    return result.reshape(token_count, -1).astype(jnp.bfloat16)


def attend_back(
    query_matrix, mixed_gradient, gathered, block_masks, key_tile_block, running_totals
):
    sequence_count = query_matrix.shape[0]
    delta = jnp.zeros(running_totals.shape, jnp.float32)
    for block_index, allowed in enumerate(block_masks):
        key_portion, value_portion = split_block(
            gathered, block_index * key_tile_block, key_tile_block
        )

        def live_delta(
            present_value, key_portion=key_portion, value_portion=value_portion, allowed=allowed
        ):
            probs = jnp.exp(
                block_scores(query_matrix, key_portion, allowed) - running_totals[..., None]
            )
            grad_probs = jnp.einsum(
                "sikgd,sjkd->skgij",
                mixed_gradient,
                value_portion,
                preferred_element_type=jnp.float32,
            )
            return present_value + jnp.sum(probs * grad_probs, -1)

        delta = lax.cond(jnp.any(allowed), live_delta, lambda present_value: present_value, delta)
    grad_queries = jnp.zeros(query_matrix.shape, jnp.float32)
    key_terms = []
    for block_index, allowed in enumerate(block_masks):
        key_portion, value_portion = split_block(
            gathered, block_index * key_tile_block, key_tile_block
        )

        def live_grad(
            present_value, key_portion=key_portion, value_portion=value_portion, allowed=allowed
        ):
            probs = jnp.exp(
                block_scores(query_matrix, key_portion, allowed) - running_totals[..., None]
            )
            grad_probs = jnp.einsum(
                "sikgd,sjkd->skgij",
                mixed_gradient,
                value_portion,
                preferred_element_type=jnp.float32,
            )
            grad_scores = (probs * (grad_probs - delta[..., None])).astype(jnp.bfloat16)
            updated = present_value + jnp.einsum(
                "skgij,sjkd->sikgd", grad_scores, key_portion, preferred_element_type=jnp.float32
            ) * HEAD_SIZE ** (-0.5)
            grad_keys = jnp.einsum(
                "skgij,sikgd->sjkd", grad_scores, query_matrix, preferred_element_type=jnp.float32
            ) * HEAD_SIZE ** (-0.5)
            grad_values = jnp.einsum(
                "skgij,sikgd->sjkd",
                probs.astype(jnp.bfloat16),
                mixed_gradient,
                preferred_element_type=jnp.float32,
            )
            both_parts = jnp.concatenate(
                [
                    grad_keys.reshape(sequence_count, key_tile_block, -1),
                    grad_values.reshape(sequence_count, key_tile_block, -1),
                ],
                -1,
            )
            return (updated, both_parts)

        def dead_grad(present_value):
            return (
                present_value,
                jnp.zeros(
                    (sequence_count, key_tile_block, 2 * KEY_VALUE_HEADS * HEAD_SIZE), jnp.float32
                ),
            )

        grad_queries, block_term = lax.cond(jnp.any(allowed), live_grad, dead_grad, grad_queries)
        key_terms.append(block_term)
    return (grad_queries, jnp.concatenate(key_terms, 1), delta)


def expert_forward(inner_use, outer_use, received):
    model_width = received.shape[-1]
    rows_in = received.reshape(-1, model_width)
    pre_rows = jnp.dot(rows_in, inner_use, preferred_element_type=jnp.float32)
    slab_width = outer_use.shape[0]
    hidden_rows = (jax.nn.silu(pre_rows[:, :slab_width]) * pre_rows[:, slab_width:]).astype(
        jnp.bfloat16
    )
    part_rows = jnp.dot(hidden_rows, outer_use, preferred_element_type=jnp.float32).astype(
        jnp.bfloat16
    )
    return part_rows.reshape(received.shape)


def expert_back(inner_use, outer_use, rows_flat, grad_flat):
    pre_rows = jnp.dot(rows_flat, inner_use, preferred_element_type=jnp.float32)
    slab_width = outer_use.shape[0]
    gate_pre = pre_rows[:, :slab_width]
    up_pre = pre_rows[:, slab_width:]
    sigma = jax.nn.sigmoid(gate_pre)
    swish = gate_pre * sigma
    hidden_rows = (swish * up_pre).astype(jnp.bfloat16)
    grad_hidden = jnp.dot(grad_flat, outer_use.T, preferred_element_type=jnp.float32)
    grad_gate = grad_hidden * up_pre * sigma * (1.0 + gate_pre * (1.0 - sigma))
    grad_up = grad_hidden * swish
    grad_pre = jnp.concatenate([grad_gate, grad_up], 1).astype(jnp.bfloat16)
    grad_in = jnp.dot(grad_pre, inner_use.T, preferred_element_type=jnp.float32).astype(
        jnp.bfloat16
    )
    return (hidden_rows, grad_pre, grad_in)


def per_device(
    tokens,
    segment_ids,
    routes,
    query_weight,
    key_value_weight,
    output_weight,
    router_weight,
    gain_before,
    gain_middle,
    inner_weight,
    outer_weight,
    cotangent,
):
    sequence_count, resident_rows, model_width = tokens.shape
    token_count = sequence_count * resident_rows
    experts = router_weight.shape[1]
    copies = lax.axis_size("fsdp") // experts
    capacity = 3 * token_count // 8
    seg_all = lax.all_gather(segment_ids, "fsdp", axis=1, tiled=True)
    seq_length = seg_all.shape[1]
    key_tile_block = min(256, seq_length)
    positions = lax.axis_index("fsdp") * resident_rows + jnp.arange(resident_rows, dtype=jnp.int32)
    block_masks = [
        mask_for(seg_all, segment_ids, positions, offset, key_tile_block)
        for offset in range(0, seq_length, key_tile_block)
    ]
    start_rows = tokens.reshape(token_count, model_width).astype(jnp.float32)
    route_flat = routes.reshape(token_count * 2)
    picks = route_flat[:, None] == jnp.arange(experts, dtype=jnp.int32)[None, :]
    marks = picks.astype(jnp.int32)
    slot_index = route_flat * capacity + jnp.sum((jnp.cumsum(marks, 0) - marks) * marks, 1)
    chosen_mask = picks.reshape(token_count, 2, experts)

    def layer_weights():
        return (
            lax.all_gather(query_weight, ("dp", "fsdp"), axis=0, tiled=True),
            lax.all_gather(key_value_weight, ("dp", "fsdp"), axis=0, tiled=True),
            lax.all_gather(output_weight, ("dp", "fsdp"), axis=1, tiled=True),
            lax.all_gather(router_weight, ("dp", "fsdp"), axis=0, tiled=True),
            lax.all_gather(gain_before, ("dp", "fsdp"), axis=0, tiled=True),
            lax.all_gather(gain_middle, ("dp", "fsdp"), axis=0, tiled=True),
        )

    def expert_weights():
        inner_full, outer_full = (
            lax.all_gather(inner_weight, "dp", axis=0, tiled=True),
            lax.all_gather(outer_weight, "dp", axis=1, tiled=True),
        )
        return (inner_full.reshape(model_width, -1), outer_full)

    def attention_front(weights):
        normed, unit_rows, factor = normalize(start_rows, weights[4])
        normed_low = normed.astype(jnp.bfloat16)
        query_matrix = jnp.dot(normed_low, weights[0], preferred_element_type=jnp.float32).astype(
            jnp.bfloat16
        )
        query_matrix = query_matrix.reshape(
            sequence_count,
            resident_rows,
            KEY_VALUE_HEADS,
            QUERY_HEADS // KEY_VALUE_HEADS,
            HEAD_SIZE,
        )
        key_value_rows = jnp.dot(normed_low, weights[1], preferred_element_type=jnp.float32).astype(
            jnp.bfloat16
        )
        gathered = lax.all_gather(
            key_value_rows.reshape(sequence_count, resident_rows, -1), "fsdp", axis=1, tiled=True
        )
        return (normed_low, unit_rows, factor, query_matrix, gathered)

    def middle_part(weights, mixed_low):
        middle = start_rows + jnp.dot(mixed_low, weights[2], preferred_element_type=jnp.float32)
        expert_in, unit_rows, factor = normalize(middle, weights[5])
        expert_low = expert_in.astype(jnp.bfloat16)
        logits = jnp.dot(
            expert_low.astype(jnp.float32),
            weights[3].astype(jnp.float32),
            precision=HIGHEST_PRECISION,
        )
        return (middle, unit_rows, factor, expert_low, logits)

    def gates_for(logits):
        chosen_logits = jnp.sum(jnp.where(chosen_mask, logits[:, None, :], 0.0), -1)
        return jax.nn.softmax(chosen_logits, -1)

    def to_slots(pair_rows):
        packed = (
            jnp.zeros((experts * capacity, model_width), pair_rows.dtype)
            .at[slot_index]
            .set(pair_rows)
        )
        return jnp.repeat(packed.reshape(experts, capacity, model_width), copies, axis=0)

    def from_slots(returned_rows):
        summed = jnp.sum(
            returned_rows.reshape(experts, copies, capacity, model_width).astype(jnp.float32), 1
        )
        return summed.reshape(experts * capacity, model_width)[slot_index]

    weights = layer_weights()
    inner_all, outer_all = expert_weights()
    normed_low, unit_first, factor_first, query_matrix, gathered = attention_front(weights)
    running_totals = log_totals(query_matrix, gathered, block_masks, key_tile_block)
    mixed_low = attend_values(query_matrix, gathered, block_masks, key_tile_block, running_totals)
    middle, unit_second, factor_second, expert_low, logits = middle_part(weights, mixed_low)
    gates = gates_for(logits)
    sent = to_slots(jnp.repeat(expert_low, 2, axis=0))
    part_rows = expert_forward(
        inner_all, outer_all, lax.all_to_all(sent, "fsdp", split_axis=0, concat_axis=0, tiled=True)
    )
    returned_part = lax.all_to_all(part_rows, "fsdp", split_axis=0, concat_axis=0, tiled=True)
    returned_rows = returned_part
    expert_sum = from_slots(returned_rows).reshape(token_count, 2, model_width)
    block_out = (middle + jnp.sum(gates[..., None] * expert_sum, 1)).astype(jnp.bfloat16)
    grad_out = cotangent.reshape(token_count, model_width).astype(jnp.float32)
    weights = layer_weights()
    inner_use, outer_use = expert_weights()
    normed_low, unit_first, factor_first, query_matrix, gathered = attention_front(weights)
    mixed_low = attend_values(query_matrix, gathered, block_masks, key_tile_block, running_totals)
    middle, unit_second, factor_second, expert_low, logits = middle_part(weights, mixed_low)
    gates = gates_for(logits)
    sent = to_slots(jnp.repeat(expert_low, 2, axis=0))
    grad_sent = to_slots(
        (gates[..., None] * grad_out[:, None, :])
        .astype(jnp.bfloat16)
        .reshape(2 * token_count, model_width)
    )
    rows_in = lax.all_to_all(sent, "fsdp", split_axis=0, concat_axis=0, tiled=True)
    rows_grad = lax.all_to_all(grad_sent, "fsdp", split_axis=0, concat_axis=0, tiled=True)
    row_shape = rows_in.shape
    hidden_flat, grad_pre_flat, grad_in_flat = expert_back(
        inner_use, outer_use, rows_in.reshape(-1, model_width), rows_grad.reshape(-1, model_width)
    )
    part_rows = jnp.dot(hidden_flat, outer_use, preferred_element_type=jnp.float32).astype(
        jnp.bfloat16
    )
    grad_home = lax.all_to_all(
        grad_in_flat.reshape(row_shape), "fsdp", split_axis=0, concat_axis=0, tiled=True
    )
    part_home = lax.all_to_all(
        part_rows.reshape(row_shape), "fsdp", split_axis=0, concat_axis=0, tiled=True
    )
    item_shape = row_shape[:2]
    grad_pre = grad_pre_flat.reshape(item_shape + (-1,))
    hidden_rows = hidden_flat.reshape(item_shape + (-1,))
    expert_sum = from_slots(part_home).reshape(token_count, 2, model_width)
    rows_flat = rows_in.reshape(-1, model_width)
    row_total = rows_flat.shape[0]
    inner_grad_all = jnp.dot(
        rows_flat.T, grad_pre.reshape(row_total, -1), preferred_element_type=jnp.float32
    )
    outer_grad_all = jnp.dot(
        hidden_rows.reshape(row_total, -1).T,
        rows_grad.reshape(row_total, model_width),
        preferred_element_type=jnp.float32,
    )
    inner_grad, outer_grad = (
        lax.psum_scatter(
            inner_grad_all.reshape(model_width, 2, -1).astype(jnp.bfloat16),
            "dp",
            scatter_dimension=0,
            tiled=True,
        ).astype(jnp.float32),
        lax.psum_scatter(
            outer_grad_all.astype(jnp.bfloat16), "dp", scatter_dimension=1, tiled=True
        ).astype(jnp.float32),
    )
    grad_gates = jnp.sum(grad_out[:, None, :] * expert_sum, -1)
    grad_choice = gates * (grad_gates - jnp.sum(gates * grad_gates, -1, keepdims=True))
    grad_logits = jnp.sum(jnp.where(chosen_mask, grad_choice[..., None], 0.0), 1)
    router_grad_all = jnp.dot(
        expert_low.astype(jnp.float32).T, grad_logits, precision=HIGHEST_PRECISION
    )
    grad_expert_in = jnp.sum(from_slots(grad_home).reshape(token_count, 2, model_width), 1)
    grad_expert_in = grad_expert_in + jnp.dot(
        grad_logits, weights[3].astype(jnp.float32).T, precision=HIGHEST_PRECISION
    )
    grad_norm_second, middle_gain_grad = normalize_back(
        grad_expert_in, unit_second, factor_second, weights[5]
    )
    grad_middle = grad_out + grad_norm_second
    grad_branch = grad_middle.astype(jnp.bfloat16)
    output_grad_all = jnp.dot(mixed_low.T, grad_branch, preferred_element_type=jnp.float32)
    mixed_gradient = jnp.dot(grad_branch, weights[2].T, preferred_element_type=jnp.float32).astype(
        jnp.bfloat16
    )
    mixed_gradient = mixed_gradient.reshape(
        sequence_count, resident_rows, KEY_VALUE_HEADS, QUERY_HEADS // KEY_VALUE_HEADS, HEAD_SIZE
    )
    grad_queries, key_terms, delta = attend_back(
        query_matrix, mixed_gradient, gathered, block_masks, key_tile_block, running_totals
    )
    key_grads = lax.psum_scatter(
        key_terms.astype(jnp.bfloat16), "fsdp", scatter_dimension=1, tiled=True
    ).reshape(token_count, -1)
    query_low = grad_queries.reshape(token_count, -1).astype(jnp.bfloat16)
    grad_normed = jnp.dot(query_low, weights[0].T, preferred_element_type=jnp.float32) + jnp.dot(
        key_grads, weights[1].T, preferred_element_type=jnp.float32
    )
    query_grad_all = jnp.dot(normed_low.T, query_low, preferred_element_type=jnp.float32)
    keyval_grad_all = jnp.dot(normed_low.T, key_grads, preferred_element_type=jnp.float32)
    grad_norm_first, before_gain_grad = normalize_back(
        grad_normed, unit_first, factor_first, weights[4]
    )
    tokens_grad = grad_middle + grad_norm_first
    summed_grads = (
        lax.psum_scatter(query_grad_all, ("dp", "fsdp"), scatter_dimension=0, tiled=True),
        lax.psum_scatter(keyval_grad_all, ("dp", "fsdp"), scatter_dimension=0, tiled=True),
        lax.psum_scatter(output_grad_all, ("dp", "fsdp"), scatter_dimension=1, tiled=True),
        lax.psum_scatter(router_grad_all, ("dp", "fsdp"), scatter_dimension=0, tiled=True),
        lax.psum_scatter(before_gain_grad, ("dp", "fsdp"), scatter_dimension=0, tiled=True),
        lax.psum_scatter(middle_gain_grad, ("dp", "fsdp"), scatter_dimension=0, tiled=True),
    )
    return (
        block_out.reshape(sequence_count, resident_rows, model_width),
        tokens_grad.reshape(sequence_count, resident_rows, model_width),
        summed_grads[0],
        summed_grads[1],
        summed_grads[2],
        summed_grads[3],
        summed_grads[4],
        summed_grads[5],
        inner_grad,
        outer_grad,
    )


def contract(left, right, left_axis, right_axis):
    return lax.dot_general(
        left, right, (((left_axis,), (right_axis,)), ((), ())), preferred_element_type=jnp.float32
    )


def unit_of(rows):
    factor = lax.rsqrt(jnp.mean(rows * rows, -1, keepdims=True) + EPSILON)
    return (rows * factor, factor)


def column_as_row(table, lane):
    pick = (lax.broadcasted_iota(jnp.int32, (8, table.shape[1]), 1) == lane).astype(jnp.bfloat16)
    return contract(pick, table, 1, 1)[:1]


def split_low(value):
    high = value.astype(jnp.bfloat16)
    return (high, (value - high.astype(jnp.float32)).astype(jnp.bfloat16))


def project_kernel(lane, rows_ref, weight_ref, table_ref, normed_ref, heads_ref, gain):
    @pl.when(pl.program_id(0) == 0)
    def _():
        gain[...] = column_as_row(table_ref[...], lane)

    unit, _ = unit_of(rows_ref[...].astype(jnp.float32))
    normed = (unit * gain[...]).astype(jnp.bfloat16)
    normed_ref[...] = normed
    heads = jnp.dot(normed, weight_ref[...], preferred_element_type=jnp.float32)
    heads_ref[0] = heads.T[: heads_ref.shape[1]].astype(jnp.bfloat16)


def project(rows, head_weights, wide, lane, block):
    length, width = rows.shape
    lanes = head_weights.shape[1]
    blocks = length // block
    return pl.pallas_call(
        functools.partial(project_kernel, lane),
        grid=(blocks,),
        in_specs=[
            pl.BlockSpec((block, width), lambda i: (i, 0)),
            pl.BlockSpec((width, lanes), lambda i: (0, 0)),
            pl.BlockSpec((width, 128), lambda i: (0, lanes // 128 - 1)),
        ],
        out_specs=[
            pl.BlockSpec((block, width), lambda i: (i, 0)),
            pl.BlockSpec((1, wide, block), lambda i: (i, 0, 0)),
        ],
        out_shape=[
            jax.ShapeDtypeStruct((length, width), jnp.bfloat16),
            jax.ShapeDtypeStruct((blocks, wide, block), jnp.bfloat16),
        ],
        scratch_shapes=[pltpu.VMEM((1, width), jnp.float32)],
        compiler_params=pltpu.CompilerParams(vmem_limit_bytes=40 * 2**20),
        name="project",
    )(rows, head_weights, head_weights)


def beside(rows, block, heads):
    return jnp.concatenate([rows[h * HEAD_SIZE : (h + 1) * HEAD_SIZE] for h in range(heads)], 1)


def attend_kernel(spans, q_ref, heads_ref, segr_ref, segc_ref, low_ref, mixed_ref, totals_ref):
    step = pl.program_id(0)
    block = q_ref.shape[2]
    heads = QUERY_HEADS // KEY_VALUE_HEADS
    share = heads * HEAD_SIZE
    queries = beside(q_ref[0, :share, :] * jnp.bfloat16(HEAD_SIZE ** (-0.5)), block, heads)
    seg_row = segr_ref[...]

    def scores_of(j):
        return contract(heads_ref[j, share : share + HEAD_SIZE, :], queries, 0, 0)

    def same_doc(j):
        return segc_ref[pl.ds(pl.multiple_of(j * block, block), block), :] == seg_row

    def fold(j, scores, carry):
        top, total, out = carry
        values = heads_ref[j, share + HEAD_SIZE : share + 2 * HEAD_SIZE, :]
        new_top = jnp.maximum(top, jnp.max(scores, 0, keepdims=True))
        probs = jnp.exp(scores - new_top)
        decay = jnp.exp(top - new_top)
        total = total * decay + jnp.sum(probs, 0, keepdims=True)
        out = out * decay + jnp.dot(
            values, probs.astype(jnp.bfloat16), preferred_element_type=jnp.float32
        )
        return (new_top, total, out)

    def masked(j, carry):
        allowed = jnp.concatenate([same_doc(j)] * heads, 1)
        return fold(j, jnp.where(allowed, scores_of(j), NEGATIVE_LARGE), carry)

    columns = heads * block
    carry = (
        jnp.full((1, columns), NEGATIVE_LARGE, jnp.float32),
        jnp.zeros((1, columns), jnp.float32),
        jnp.zeros((HEAD_SIZE, columns), jnp.float32),
    )
    first, full = spans[0, step], spans[1, step]
    carry = lax.fori_loop(first, full, masked, carry)
    carry = lax.fori_loop(full, step, lambda j, kept: fold(j, scores_of(j), kept), carry)
    key_spot = lax.broadcasted_iota(jnp.int32, (block, block), 0)
    query_spot = lax.broadcasted_iota(jnp.int32, (block, block), 1)
    allowed = same_doc(step) & (key_spot <= query_spot)
    allowed = jnp.concatenate([allowed] * heads, 1)
    top, total, out = fold(step, jnp.where(allowed, scores_of(step), NEGATIVE_LARGE), carry)
    out = out / total
    totals = top + jnp.log(total)
    for h in range(heads):
        part = out[:, h * block : (h + 1) * block]
        mixed_ref[0, h * HEAD_SIZE : (h + 1) * HEAD_SIZE, :] = part
        low_ref[0, h * HEAD_SIZE : (h + 1) * HEAD_SIZE, :] = part.astype(jnp.bfloat16)
        totals_ref[0, h : h + 1, :] = totals[:, h * block : (h + 1) * block]


def attend(spans, projected, seg_row, seg_col):
    blocks, wide, block = projected.shape
    share = wide - 2 * HEAD_SIZE
    length = blocks * block
    each = lambda height: pl.BlockSpec((1, height, block), lambda i, spans: (i, 0, 0))
    return pl.pallas_call(
        attend_kernel,
        grid_spec=pltpu.PrefetchScalarGridSpec(
            num_scalar_prefetch=1,
            grid=(blocks,),
            in_specs=[
                pl.BlockSpec((1, wide, block), lambda i, spans: (i, 0, 0)),
                pl.BlockSpec((blocks, wide, block), lambda i, spans: (0, 0, 0)),
                pl.BlockSpec((1, block), lambda i, spans: (0, i)),
                pl.BlockSpec((length, 1), lambda i, spans: (0, 0)),
            ],
            out_specs=[each(share), each(share), each(8)],
        ),
        out_shape=[
            jax.ShapeDtypeStruct((blocks, share, block), jnp.bfloat16),
            jax.ShapeDtypeStruct((blocks, share, block), jnp.float32),
            jax.ShapeDtypeStruct((blocks, 8, block), jnp.float32),
        ],
        compiler_params=pltpu.CompilerParams(vmem_limit_bytes=40 * 2**20),
        name="attend",
    )(spans, projected, projected, seg_row, seg_col)


def attend_back_kernel(
    spans, q_ref, g_ref, heads_ref, segr_ref, segc_ref, mixed_ref, totals_ref,
    blocks_ref, line_ref, dk_sum, dv_sum,
):
    step = pl.program_id(0)
    blocks, _, block = heads_ref.shape
    heads = QUERY_HEADS // KEY_VALUE_HEADS
    share = heads * HEAD_SIZE
    queries = beside(q_ref[0, :share, :] * jnp.bfloat16(HEAD_SIZE ** (-0.5)), block, heads)
    grads = beside(g_ref[0], block, heads)
    delta = jnp.sum(
        grads.astype(jnp.float32) * beside(mixed_ref[0], block, heads), 0, keepdims=True
    )
    totals = jnp.concatenate([totals_ref[0, h : h + 1, :] for h in range(heads)], 1)
    seg_row = segr_ref[...]

    @pl.when(step == 0)
    def _():
        dk_sum[...] = jnp.zeros_like(dk_sum)
        dv_sum[...] = jnp.zeros_like(dv_sum)

    def turn(j, query_sum, allowed):
        keys = heads_ref[j, share : share + HEAD_SIZE, :]
        values = heads_ref[j, share + HEAD_SIZE : share + 2 * HEAD_SIZE, :]
        probs = jnp.exp(contract(keys, queries, 0, 0) - totals)
        if allowed is not None:
            probs = jnp.where(jnp.concatenate([allowed] * heads, 1), probs, 0.0)
        grad_scores = (probs * (contract(values, grads, 0, 0) - delta)).astype(jnp.bfloat16)
        dv_sum[j] += contract(grads, probs.astype(jnp.bfloat16), 1, 1)
        dk_sum[j] += contract(queries, grad_scores, 1, 1)
        return query_sum + jnp.dot(keys, grad_scores, preferred_element_type=jnp.float32)

    def same_doc(j):
        return segc_ref[pl.ds(pl.multiple_of(j * block, block), block), :] == seg_row

    query_sum = jnp.zeros((HEAD_SIZE, heads * block), jnp.float32)
    first, full = spans[0, step], spans[1, step]
    query_sum = lax.fori_loop(first, full, lambda j, c: turn(j, c, same_doc(j)), query_sum)
    query_sum = lax.fori_loop(full, step, lambda j, c: turn(j, c, None), query_sum)
    key_spot = lax.broadcasted_iota(jnp.int32, (block, block), 0)
    query_spot = lax.broadcasted_iota(jnp.int32, (block, block), 1)
    query_sum = turn(step, query_sum, same_doc(step) & (key_spot <= query_spot))
    query_sum = (query_sum * HEAD_SIZE ** (-0.5)).astype(jnp.bfloat16)

    def spread(j, at, size, value):
        blocks_ref[j, at : at + size, :] = value
        there = pl.ds(pl.multiple_of(j * block, block), block)
        line_ref[at : at + size, there] = value

    for h in range(heads):
        spread(step, h * HEAD_SIZE, HEAD_SIZE, query_sum[:, h * block : (h + 1) * block])

    @pl.when(step == pl.num_programs(0) - 1)
    def _():
        for j in range(blocks):
            spread(j, share, HEAD_SIZE, dk_sum[j].astype(jnp.bfloat16))
            spread(j, share + HEAD_SIZE, HEAD_SIZE, dv_sum[j].astype(jnp.bfloat16))


def attend_backward(spans, projected, grads, seg_row, seg_col, mixed, totals):
    blocks, wide, block = projected.shape
    share = wide - 2 * HEAD_SIZE
    length = blocks * block
    each = lambda height: pl.BlockSpec((1, height, block), lambda i, spans: (i, 0, 0))
    return pl.pallas_call(
        attend_back_kernel,
        grid_spec=pltpu.PrefetchScalarGridSpec(
            num_scalar_prefetch=1,
            grid=(blocks,),
            in_specs=[
                pl.BlockSpec((1, wide, block), lambda i, spans: (i, 0, 0)),
                each(share),
                pl.BlockSpec((blocks, wide, block), lambda i, spans: (0, 0, 0)),
                pl.BlockSpec((1, block), lambda i, spans: (0, i)),
                pl.BlockSpec((length, 1), lambda i, spans: (0, 0)),
                each(share),
                each(8),
            ],
            out_specs=[
                pl.BlockSpec((blocks, wide, block), lambda i, spans: (0, 0, 0)),
                pl.BlockSpec((wide, length), lambda i, spans: (0, 0)),
            ],
            scratch_shapes=[
                pltpu.VMEM((blocks, HEAD_SIZE, block), jnp.float32),
                pltpu.VMEM((blocks, HEAD_SIZE, block), jnp.float32),
            ],
        ),
        out_shape=[
            jax.ShapeDtypeStruct((blocks, wide, block), jnp.bfloat16),
            jax.ShapeDtypeStruct((wide, length), jnp.bfloat16),
        ],
        compiler_params=pltpu.CompilerParams(vmem_limit_bytes=40 * 2**20),
        name="attend_backward",
    )(spans, projected, grads, projected, seg_row, seg_col, mixed, totals)


def hits(slots, height):
    spot = lax.broadcasted_iota(jnp.int32, (height, slots.shape[1]), 0)
    return (spot == slots[0:1, :], spot == slots[1:2, :])


def spread_kernel(slots_ref, rows_ref, *out_refs):
    size = out_refs[0].shape[0]
    first, second = hits(slots_ref[...], size * len(out_refs))
    chosen = (first | second).astype(jnp.bfloat16)
    for k, out_ref in enumerate(out_refs):
        out_ref[...] = jnp.dot(
            chosen[k * size : (k + 1) * size], rows_ref[...], preferred_element_type=jnp.float32
        ).astype(jnp.bfloat16)


def spread_rows(slots, rows, size, blocks):
    return pl.pallas_call(
        spread_kernel,
        out_shape=[jax.ShapeDtypeStruct((size, rows.shape[1]), jnp.bfloat16)] * blocks,
        compiler_params=pltpu.CompilerParams(vmem_limit_bytes=40 * 2**20),
        name="spread_rows",
    )(slots, rows)


def middle_kernel(
    lane, router_lane, start_ref, mixed_ref, weight_ref, table_ref, slots_ref, routes_ref,
    middle_ref, sent_ref, gates_ref,
):
    table = table_ref[...]
    middle = start_ref[...].astype(jnp.float32) + contract(mixed_ref[...].T, weight_ref[...], 1, 1)
    middle_ref[...] = middle
    unit, _ = unit_of(middle)
    expert_low = (unit * column_as_row(table, lane)).astype(jnp.bfloat16)
    first, second = hits(slots_ref[...], sent_ref.shape[0])
    sent_ref[...] = jnp.dot(
        (first | second).astype(jnp.bfloat16), expert_low, preferred_element_type=jnp.float32
    ).astype(jnp.bfloat16)
    logits = jnp.dot(expert_low, table, preferred_element_type=jnp.float32).T
    spot = lax.broadcasted_iota(jnp.int32, logits.shape, 0) - router_lane
    chosen = [
        jnp.sum(jnp.where(spot == routes_ref[c : c + 1, :], logits, 0.0), 0, keepdims=True)
        for c in range(2)
    ]
    top = jnp.maximum(chosen[0], chosen[1])
    parts = [jnp.exp(value - top) for value in chosen]
    gates_ref[...] = jnp.concatenate([part / (parts[0] + parts[1]) for part in parts], 0)


def middle_part(start, mixed, weight, head_weights, slots, routes, lane, router_lane, height):
    rows, width = start.shape
    lanes = head_weights.shape[1]
    whole = lambda shape: pl.BlockSpec(shape, lambda i: (0, 0))
    return pl.pallas_call(
        functools.partial(middle_kernel, lane, router_lane),
        grid=(1,),
        in_specs=[
            whole(start.shape),
            whole(mixed.shape),
            whole(weight.shape),
            pl.BlockSpec((width, 128), lambda i: (0, lanes // 128 - 1)),
            whole(slots.shape),
            whole(routes.shape),
        ],
        out_specs=[whole((rows, width)), whole((height, width)), whole((2, rows))],
        out_shape=[
            jax.ShapeDtypeStruct((rows, width), jnp.float32),
            jax.ShapeDtypeStruct((height, width), jnp.bfloat16),
            jax.ShapeDtypeStruct((2, rows), jnp.float32),
        ],
        compiler_params=pltpu.CompilerParams(vmem_limit_bytes=40 * 2**20),
        name="middle",
    )(start, mixed, weight, head_weights, slots, routes)


def block_place(own_ref, axis, k, size):
    return pl.ds(pl.multiple_of(jnp.bitwise_xor(own_ref[axis], k) * size, size), size)


def assemble_weights(own_ref, part_refs, gate, up, outer):
    count = len(part_refs) // 3
    for k in range(count):
        size = part_refs[k].shape[0]
        place = block_place(own_ref, 1, k, size)
        gate[place, :] = part_refs[k][...]
        up[place, :] = part_refs[count + k][...]
        outer[:, place] = part_refs[2 * count + k][...]


def expert_kernel(router_lane, blocks, own_ref, rows_ref, *refs):
    weight_refs, (table_ref, other_ref) = refs[:12], refs[12:14]
    pre_gate_ref, pre_up_ref, hidden_ref, gates_ref = refs[14:18]
    part_refs, (part_sum, gate, up, outer) = refs[18 : 18 + blocks], refs[18 + blocks :]
    step = pl.program_id(0)
    size = part_refs[0].shape[0]
    rows = rows_ref[...]
    assemble_weights(own_ref, weight_refs, gate, up, outer)

    @pl.when(step == 0)
    def _():
        lane = lax.broadcasted_iota(jnp.int32, (rows.shape[0], 128), 1) - router_lane
        logits = jnp.dot(rows, table_ref[...], preferred_element_type=jnp.float32)
        own = jnp.sum(jnp.where(lane == own_ref[0], logits, 0.0), 1, keepdims=True)
        other = jnp.sum(jnp.where(lane == other_ref[...], logits, 0.0), 1, keepdims=True)
        top = jnp.maximum(own, other)
        own, other = jnp.exp(own - top), jnp.exp(other - top)
        gates_ref[:, 0:1] = own / (own + other)
        gates_ref[:, 1:2] = other / (own + other)
        part_sum[...] = jnp.zeros_like(part_sum)

    gate_pre = jnp.dot(rows, gate[...], preferred_element_type=jnp.float32)
    up_pre = jnp.dot(rows, up[...], preferred_element_type=jnp.float32)
    pre_gate_ref[...] = gate_pre
    pre_up_ref[...] = up_pre
    hidden = (gate_pre / (1.0 + jnp.exp(-gate_pre)) * up_pre).astype(jnp.bfloat16)
    hidden_ref[...] = hidden
    part_sum[...] += jnp.dot(hidden, outer[...], preferred_element_type=jnp.float32)

    @pl.when(step == pl.num_programs(0) - 1)
    def _():
        for k, ref in enumerate(part_refs):
            ref[...] = part_sum[block_place(own_ref, 0, k, size), :].astype(jnp.bfloat16)


def weight_specs(inner, outer, tile, steps):
    size = inner[0].shape[0]
    return (
        [pl.BlockSpec((size, tile), lambda i, own: (0, i))] * len(inner)
        + [pl.BlockSpec((size, tile), lambda i, own: (0, steps + i))] * len(inner)
        + [pl.BlockSpec((tile, size), lambda i, own: (i, 0))] * len(outer)
    )


def expert_forward_pass(own, rows, inner, outer, head_weights, other, router_lane, tile, blocks):
    height, width = rows.shape
    units = outer[0].shape[0]
    steps = units // tile
    lanes = head_weights.shape[1]
    whole = lambda shape: pl.BlockSpec(shape, lambda i, own: (0, 0))
    tiled = lambda rows, off: pl.BlockSpec((rows, tile), lambda i, own: (0, off + i))
    shape = jax.ShapeDtypeStruct
    low, f32 = jnp.bfloat16, jnp.float32
    outcome = pl.pallas_call(
        functools.partial(expert_kernel, router_lane, blocks),
        grid_spec=pltpu.PrefetchScalarGridSpec(
            num_scalar_prefetch=1,
            grid=(steps,),
            in_specs=[whole(rows.shape)]
            + weight_specs(inner, outer, tile, steps)
            + [
                pl.BlockSpec((width, 128), lambda i, own: (0, lanes // 128 - 1)),
                whole(other.shape),
            ],
            out_specs=[tiled(height, 0)] * 3
            + [whole((height, 128))]
            + [whole((height // blocks, width))] * blocks,
            scratch_shapes=[
                pltpu.VMEM((height, width), f32),
                pltpu.VMEM((width, tile), low),
                pltpu.VMEM((width, tile), low),
                pltpu.VMEM((tile, width), low),
            ],
        ),
        out_shape=[shape((height, units), f32)] * 2
        + [shape((height, units), low), shape((height, 128), f32)]
        + [shape((height // blocks, width), low)] * blocks,
        compiler_params=pltpu.CompilerParams(vmem_limit_bytes=56 * 2**20),
        name="expert",
    )(own, rows, *inner, *inner, *outer, head_weights, other)
    return outcome[:4], list(outcome[4:])


def expert_back_kernel(router_lane, blocks, own_ref, *refs):
    cot_refs, part_refs, refs = refs[:blocks], refs[blocks : 2 * blocks], refs[2 * blocks :]
    rows_ref, gates_ref, pre_gate_ref, pre_up_ref = refs[:4]
    weight_refs, refs = refs[4:16], refs[16:]
    table_ref, other_ref, pre_ref, grad_ref, back_ref, router_ref = refs[:6]
    cot, back_sum, gate, up, outer = refs[6:]
    step = pl.program_id(0)
    tile = gate.shape[1]
    assemble_weights(own_ref, weight_refs, gate, up, outer)
    units = tile * pl.num_programs(0)
    size = cot_refs[0].shape[0]
    gates = gates_ref[...]

    @pl.when(step == 0)
    def _():
        for k, ref in enumerate(cot_refs):
            cot[block_place(own_ref, 0, k, size), :] = ref[...]
        grad_ref[...] = (gates[:, 0:1] * cot[...].astype(jnp.float32)).astype(jnp.bfloat16)
        back_sum[...] = jnp.zeros_like(back_sum)

    gate_pre, up_pre = pre_gate_ref[...], pre_up_ref[...]
    grad_hidden = contract(grad_ref[...], outer[...], 1, 1)
    sigma = 1.0 / (1.0 + jnp.exp(-gate_pre))
    grad_gate = grad_hidden * up_pre * sigma * (1.0 + gate_pre * (1.0 - sigma))
    grad_gate = grad_gate.astype(jnp.bfloat16)
    grad_up = (grad_hidden * (gate_pre * sigma)).astype(jnp.bfloat16)
    at = pl.multiple_of(step * tile, tile)
    pre_ref[:, pl.ds(at, tile)] = grad_gate
    pre_ref[:, pl.ds(pl.multiple_of(units + at, tile), tile)] = grad_up
    back_sum[...] += contract(grad_gate, gate[...], 1, 1) + contract(grad_up, up[...], 1, 1)

    @pl.when(step == pl.num_programs(0) - 1)
    def _():
        table = table_ref[...]
        total = jnp.zeros(router_ref.shape, jnp.float32)
        for k in range(blocks):
            place = block_place(own_ref, 0, k, size)
            grad_gates = jnp.sum(
                cot_refs[k][...].astype(jnp.float32) * part_refs[k][...].astype(jnp.float32),
                1,
                keepdims=True,
            )
            gates_k = gates_ref[place, :]
            lane_k = lax.broadcasted_iota(jnp.int32, (size, 128), 1) - router_lane
            sides_k = (lane_k == own_ref[0]).astype(jnp.float32) - (
                lane_k == other_ref[place, :]
            ).astype(jnp.float32)
            high, rest = split_low(gates_k[:, 0:1] * gates_k[:, 1:2] * grad_gates * sides_k)
            routed = contract(high, table, 1, 1) + contract(rest, table, 1, 1)
            back = back_sum[place, :].astype(jnp.bfloat16).astype(jnp.float32)
            back_ref[place, :] = (back + routed).astype(jnp.bfloat16)
            rows_k = rows_ref[place, :]
            total = total + contract(high, rows_k, 0, 0) + contract(rest, rows_k, 0, 0)
        router_ref[...] = total


def expert_backward_pass(
    own, cot_blocks, part_blocks, rows, gates, pre_gate, pre_up, inner, outer, head_weights, other,
    router_lane, tile,
):
    height, width = rows.shape
    units = outer[0].shape[0]
    steps = units // tile
    lanes = head_weights.shape[1]
    blocks = len(cot_blocks)
    whole = lambda shape: pl.BlockSpec(shape, lambda i, own: (0, 0))
    tiled = lambda rows, off: pl.BlockSpec((rows, tile), lambda i, own: (0, off + i))
    low, f32 = jnp.bfloat16, jnp.float32
    return pl.pallas_call(
        functools.partial(expert_back_kernel, router_lane, blocks),
        grid_spec=pltpu.PrefetchScalarGridSpec(
            num_scalar_prefetch=1,
            grid=(steps,),
            in_specs=[whole((height // blocks, width))] * (2 * blocks)
            + [
                whole(rows.shape),
                whole(gates.shape),
                tiled(height, 0),
                tiled(height, 0),
            ]
            + weight_specs(inner, outer, tile, steps)
            + [
                pl.BlockSpec((width, 128), lambda i, own: (0, lanes // 128 - 1)),
                whole(other.shape),
            ],
            out_specs=[
                whole((height, 2 * units)),
                whole((height, width)),
                whole((height, width)),
                whole((128, width)),
            ],
            scratch_shapes=[
                pltpu.VMEM((height, width), low),
                pltpu.VMEM((height, width), f32),
                pltpu.VMEM((width, tile), low),
                pltpu.VMEM((width, tile), low),
                pltpu.VMEM((tile, width), low),
            ],
        ),
        out_shape=[
            jax.ShapeDtypeStruct((height, 2 * units), low),
            jax.ShapeDtypeStruct((height, width), low),
            jax.ShapeDtypeStruct((height, width), low),
            jax.ShapeDtypeStruct((128, width), f32),
        ],
        compiler_params=pltpu.CompilerParams(vmem_limit_bytes=56 * 2**20),
        name="expert_backward",
    )(
        own, *cot_blocks, *part_blocks, rows, gates, pre_gate, pre_up, *inner, *inner, *outer,
        head_weights, other,
    )


def back_kernel(
    lane, middle_ref, cot_ref, home_ref, weight_ref, table_ref, slots_ref,
    grad_ref, branch_ref, gain_ref, mixed_ref,
):
    first, second = hits(slots_ref[...], home_ref.shape[0])
    grad_in = contract((first | second).astype(jnp.bfloat16), home_ref[...], 0, 0)
    unit, factor = unit_of(middle_ref[...])
    gain_ref[...] = jnp.sum(grad_in * unit, 0, keepdims=True)
    scaled = grad_in * column_as_row(table_ref[...], lane)
    inner_part = factor * (scaled - unit * jnp.mean(scaled * unit, -1, keepdims=True))
    grad_middle = cot_ref[...].astype(jnp.float32) + inner_part
    grad_ref[...] = grad_middle
    branch = grad_middle.astype(jnp.bfloat16)
    branch_ref[...] = branch
    mixed = jnp.dot(branch, weight_ref[...], preferred_element_type=jnp.float32)
    mixed_ref[...] = mixed.T.astype(jnp.bfloat16)


def back_part(middle, cot, home, weight, head_weights, slots, lane):
    rows, width = middle.shape
    lanes = head_weights.shape[1]
    whole = lambda shape: pl.BlockSpec(shape, lambda i: (0, 0))
    return pl.pallas_call(
        functools.partial(back_kernel, lane),
        grid=(1,),
        in_specs=[
            whole((rows, width)),
            whole((rows, width)),
            whole(home.shape),
            whole(weight.shape),
            pl.BlockSpec((width, 128), lambda i: (0, lanes // 128 - 1)),
            whole(slots.shape),
        ],
        out_specs=[
            whole((rows, width)),
            whole((rows, width)),
            whole((1, width)),
            whole((weight.shape[1], rows)),
        ],
        out_shape=[
            jax.ShapeDtypeStruct((rows, width), jnp.float32),
            jax.ShapeDtypeStruct((rows, width), jnp.bfloat16),
            jax.ShapeDtypeStruct((1, width), jnp.float32),
            jax.ShapeDtypeStruct((weight.shape[1], rows), jnp.bfloat16),
        ],
        compiler_params=pltpu.CompilerParams(vmem_limit_bytes=48 * 2**20),
        name="back",
    )(middle, cot, home, weight, head_weights, slots)


def weight_kernel(place, normed_ref, grads_ref, extra_ref, out_ref):
    total = jnp.dot(grads_ref[...], normed_ref[...], preferred_element_type=jnp.float32)
    out_ref[0] = jnp.concatenate([total, extra_ref[...]], 0).T.astype(jnp.bfloat16)


def weight_terms(place, normed, grads, extra, parts):
    length, width = normed.shape
    wide = grads.shape[0]
    span = width // parts
    lanes = wide + extra.shape[0]
    near = lambda k, place: (0, jnp.bitwise_xor(place[0], k))
    return pl.pallas_call(
        weight_kernel,
        grid_spec=pltpu.PrefetchScalarGridSpec(
            num_scalar_prefetch=1,
            grid=(parts,),
            in_specs=[
                pl.BlockSpec((length, span), near),
                pl.BlockSpec((wide, length), lambda k, place: (0, 0)),
                pl.BlockSpec((extra.shape[0], span), near),
            ],
            out_specs=pl.BlockSpec((1, span, lanes), lambda k, place: (k, 0, 0)),
        ),
        out_shape=jax.ShapeDtypeStruct((parts, span, lanes), jnp.bfloat16),
        compiler_params=pltpu.CompilerParams(vmem_limit_bytes=40 * 2**20),
        name="weight_terms",
    )(place, normed, grads, extra)


def mixture_kernel(slots_ref, gates_ref, middle_ref, *refs):
    part_refs, out_ref = refs[:-1], refs[-1]
    size = part_refs[0].shape[0]
    first, second = hits(slots_ref[...], size * len(part_refs))
    total = middle_ref[...]
    shares = gates_ref[...]
    for _ in range(3):
        piece = shares.astype(jnp.bfloat16)
        shares = shares - piece.astype(jnp.float32)
        piece = piece.astype(jnp.float32)
        weights = jnp.where(first, piece[0:1], 0.0) + jnp.where(second, piece[1:2], 0.0)
        weights = weights.astype(jnp.bfloat16)
        for k, ref in enumerate(part_refs):
            total = total + contract(weights[k * size : (k + 1) * size], ref[...], 0, 0)
    out_ref[...] = total.astype(jnp.bfloat16)


def mixture(slots, gates, middle, parts):
    return pl.pallas_call(
        mixture_kernel,
        out_shape=jax.ShapeDtypeStruct(middle.shape, jnp.bfloat16),
        compiler_params=pltpu.CompilerParams(vmem_limit_bytes=40 * 2**20),
        name="mixture",
    )(slots, gates, middle, *parts)


def weight_grads_kernel(
    share, home_ref, query_weight_ref, keyval_weight_ref, gain_ref,
    query_ref, keyval_ref, router_ref, gains_ref,
):
    count = home_ref.shape[0]
    cols = share + 2 * HEAD_SIZE
    half = count * HEAD_SIZE
    experts = router_ref.shape[1]
    small = jnp.zeros((home_ref.shape[1], home_ref.shape[2] - cols), jnp.float32)
    for e in range(count):
        part = home_ref[e].astype(jnp.float32)
        query_ref[:, e * share : (e + 1) * share] = part[:, :share]
        at = e * HEAD_SIZE
        keyval_ref[:, at : at + HEAD_SIZE] = part[:, share : share + HEAD_SIZE]
        keyval_ref[:, half + at : half + at + HEAD_SIZE] = part[:, share + HEAD_SIZE : cols]
        small = small + part[:, cols:]
    router_ref[...] = small[:, :experts]
    products = jnp.sum(
        query_ref[...] * query_weight_ref[...].astype(jnp.float32), 1, keepdims=True
    ) + jnp.sum(keyval_ref[...] * keyval_weight_ref[...].astype(jnp.float32), 1, keepdims=True)
    gains_ref[:, 0:1] = products / gain_ref[...].astype(jnp.float32)
    gains_ref[:, 1:2] = small[:, experts : experts + 1]


def weight_grads(home, query_weight, keyval_weight, gain, share, experts):
    shape = lambda width: jax.ShapeDtypeStruct((query_weight.shape[0], width), jnp.float32)
    return pl.pallas_call(
        functools.partial(weight_grads_kernel, share),
        out_shape=[
            shape(query_weight.shape[1]),
            shape(keyval_weight.shape[1]),
            shape(experts),
            shape(2),
        ],
        compiler_params=pltpu.CompilerParams(vmem_limit_bytes=40 * 2**20),
        name="weight_grads",
    )(home, query_weight, keyval_weight, gain)


def after(values, *earlier):
    return lax.optimization_barrier((values, earlier))[0]


def flip_exchange(block, axis, flip):
    count = lax.axis_size(axis)
    return lax.ppermute(block, axis, [(i, i ^ flip) for i in range(count)])


def swap_near_blocks(blocks, flips):
    return [flip_exchange(blocks[flip], "fsdp", flip) for flip in flips]


def swap_near(block, axis, flips):
    return [flip_exchange(block, axis, flip) for flip in flips]


def in_order(parts, axis):
    stacked = jnp.stack(parts)
    index = lax.axis_index(axis)
    return jnp.stack(
        [
            lax.dynamic_index_in_dim(stacked, jnp.bitwise_xor(index, j), 0, keepdims=False)
            for j in range(len(parts))
        ]
    )


def all_to_all(blocks):
    return lax.all_to_all(blocks, "fsdp", split_axis=0, concat_axis=0, tiled=True)


def gather(block, axis):
    return lax.all_gather(block, axis, axis=0, tiled=True)


def per_device_heads(
    tokens,
    segment_ids,
    routes,
    query_weight,
    key_value_weight,
    output_weight,
    router_weight,
    gain_before,
    gain_middle,
    inner_weight,
    outer_weight,
    cotangent,
):
    f32, low = jnp.float32, jnp.bfloat16
    _, rows, width = tokens.shape
    count = lax.axis_size("fsdp")
    experts = router_weight.shape[1]
    index, group = lax.axis_index("fsdp"), lax.axis_index("dp")
    core = index % 2
    capacity = 3 * rows // 8
    height = experts * capacity
    length = count * rows
    shard = query_weight.shape[0]
    share = QUERY_HEADS // KEY_VALUE_HEADS * HEAD_SIZE
    cols = share + 2 * HEAD_SIZE
    half = KEY_VALUE_HEADS * HEAD_SIZE
    ff = outer_weight.shape[0]
    size = inner_weight.shape[0]

    start_low = tokens.reshape(rows, width)
    cot_low = cotangent.reshape(rows, width)

    route = routes.reshape(rows, 2)
    route_flat = route.reshape(rows * 2)
    picks = route_flat[:, None] == jnp.arange(experts, dtype=jnp.int32)[None, :]
    before = jnp.dot(
        jnp.tril(jnp.ones((rows * 2, rows * 2), low), -1),
        picks.astype(low),
        preferred_element_type=f32,
    )
    rank = jnp.sum(jnp.where(picks, before, 0.0), 1).astype(jnp.int32).reshape(rows, 2)
    route_lines = route.T
    slots = (route * capacity + rank).T
    slots_near = (jnp.bitwise_xor(route, index) * capacity + rank).T
    spots = jnp.arange(height, dtype=jnp.int32)[:, None]
    other_route = jnp.sum(
        jnp.where(slots[0:1] == spots, route_lines[1:2], 0)
        + jnp.where(slots[1:2] == spots, route_lines[0:1], 0),
        1,
    )

    by_head = jnp.concatenate(
        [
            query_weight.reshape(shard, count, share),
            key_value_weight[:, :half].reshape(shard, count, HEAD_SIZE),
            key_value_weight[:, half:].reshape(shard, count, HEAD_SIZE),
        ],
        2,
    )
    lanes = 128 * -(-(cols + 2 + experts) // 128)
    table_lane = lanes - 128
    router_lane = cols - table_lane
    first_lane, second_lane = router_lane + experts, router_lane + experts + 1
    extras = jnp.concatenate([router_weight, gain_before[:, None], gain_middle[:, None]], 1)
    extras = jnp.broadcast_to(extras[None], (count, shard, 2 + experts))
    head_block = jnp.concatenate([by_head.transpose(1, 0, 2), extras], 2)
    head_block = jnp.pad(head_block, ((0, 0), (0, 0), (0, lanes - cols - 2 - experts)))
    seg_line = jnp.broadcast_to(segment_ids.reshape(1, 1, rows), (count, 1, rows)).astype(low)
    seg_line = jnp.pad(seg_line, ((0, 0), (0, 0), (0, lanes - rows)))
    other_line = other_route.reshape(experts, 1, capacity).astype(low)
    other_line = jnp.pad(other_line, ((0, 0), (0, 14), (0, lanes - capacity)))
    head_block = jnp.concatenate([head_block, seg_line, other_line], 1)
    chip = index // 2
    tokens_all = gather(start_low, "fsdp")
    arrived = all_to_all(head_block)

    inner_own = inner_weight.reshape(size, 2 * ff)
    inner_x, inner_y = swap_near(inner_own, "dp", (1, 2))
    outer_x, outer_y = swap_near(outer_weight, "dp", (1, 2))
    arrived, inner_x, inner_y, outer_x, outer_y = after(
        (arrived, inner_x, inner_y, outer_x, outer_y)
    )
    inner_far = flip_exchange(inner_x, "dp", 2)
    outer_far = flip_exchange(outer_y, "dp", 1)
    segments = arrived[:, shard, :rows].reshape(length).astype(jnp.int32)
    other_expert = arrived[:, shard + 1, :capacity].reshape(height, 1).astype(jnp.int32)
    head_rows = arrived[:, :shard].reshape(count * shard, lanes)
    head_near = swap_near(head_rows, "dp", (1, 2, 3))
    head_weights = in_order([head_rows] + head_near, "dp").reshape(width, lanes)
    cot_sent = spread_rows(slots_near, cot_low, capacity, experts)

    by_head_line = by_head.reshape(shard, count * cols)
    tokens_all, cot_sent, head_weights, by_head_line, output_own = after(
        (tokens_all, cot_sent, head_weights, by_head_line, output_weight.T)
    )
    output_all = gather(output_own, ("dp", "fsdp"))
    normed, projected = project(tokens_all, head_weights, cols, first_lane, rows)
    cot_first = swap_near_blocks(cot_sent, (4, 6, 2))
    firsts = segments.reshape(count, rows)
    starts = jnp.sum(segments[None, :] < firsts[:, :1], 1) // rows
    wholes = (jnp.sum(segments[None, :] < firsts[:, -1:], 1) + rows - 1) // rows
    wholes = jnp.minimum(wholes, jnp.arange(count))
    spans = jnp.stack([starts, wholes]).astype(jnp.int32)
    seg_row, seg_col = segments.reshape(1, length), segments.reshape(length, 1)
    mixed_head, mixed_exact, totals = attend(spans, projected, seg_row, seg_col)
    mixed_head, cot_first, inner_far, outer_far, by_head_line = after(
        (mixed_head, cot_first, inner_far, outer_far, by_head_line)
    )
    project_line = gather(by_head_line, "fsdp")
    inner_parts = [inner_own, inner_x, inner_y, inner_far]
    outer_parts = [outer_weight, outer_x, outer_y, outer_far]
    mixed = all_to_all(mixed_head).reshape(count * share, rows)

    middle, sent, gates = middle_part(
        start_low, mixed, output_all, head_weights, slots, route_lines,
        second_lane, router_lane, height,
    )

    rows_in = all_to_all(sent)
    rows_in, cot_sent, project_line = after((rows_in, cot_sent, project_line))
    project_all = gather(project_line, "dp")
    cot_last = swap_near_blocks(cot_sent, (5, 7, 3, 1))
    own_expert = jnp.stack([index, group]).astype(jnp.int32)
    (pre_gate, pre_up, hidden, slot_gates), parts = expert_forward_pass(
        own_expert, rows_in, inner_parts, outer_parts, head_weights, other_expert,
        router_lane, 256, experts,
    )
    hidden, parts, cot_last = after((hidden, parts, cot_last))
    part_first = swap_near_blocks(parts, (4, 6, 2, 1))
    cot_in = [cot_sent[0], cot_last[3], cot_first[2], cot_last[2]]
    cot_in = cot_in + [cot_first[0], cot_last[0], cot_first[1], cot_last[1]]
    grad_pre, grad_in, grad_rows, router_part = expert_backward_pass(
        own_expert, cot_in, parts, rows_in, slot_gates, pre_gate, pre_up, inner_parts, outer_parts,
        head_weights, other_expert, router_lane, 256,
    )
    grad_rows, part_first, grad_pre, grad_in = after((grad_rows, part_first, grad_pre, grad_in))
    grad_home = all_to_all(grad_rows)

    def cut(value, k):
        return lax.dynamic_slice_in_dim(value, jnp.bitwise_xor(group, k) * size, size, 1)

    inner_terms = [contract(cut(rows_in, k), grad_pre, 0, 0).astype(low) for k in range(4)]
    outer_term = contract(grad_in, hidden, 0, 0).astype(low)
    half_size = size // 2
    inner_a = [term[:half_size] for term in inner_terms]
    inner_b = [term[half_size:] for term in inner_terms]
    near_a, far_a = [flip_exchange(inner_a[k], "dp", 1) for k in (1, 3)]
    near_b, far_b = [flip_exchange(inner_b[k], "dp", 2) for k in (2, 3)]
    grad_home, outer_term, near_a, far_a, near_b, far_b, project_all = after(
        (grad_home, outer_term, near_a, far_a, near_b, far_b, project_all)
    )
    passed_a = (inner_a[2].astype(f32) + far_a.astype(f32)).astype(low)
    passed_b = (inner_b[1].astype(f32) + far_b.astype(f32)).astype(low)
    side_a, side_b = flip_exchange(passed_a, "dp", 2), flip_exchange(passed_b, "dp", 1)

    grad_middle, grad_branch, gain_part, mixed_grad = back_part(
        middle, cot_low, grad_home, output_all, head_weights, slots, second_lane
    )
    mixed_grad = all_to_all(mixed_grad.reshape(count, share, rows))

    branch_near = jnp.concatenate([cut(grad_branch, k) for k in range(4)], 1)
    half_width = width // 2

    def half_terms(side):
        heads = lax.dynamic_slice_in_dim(mixed, side * half_width, half_width, 0)
        return contract(branch_near, heads, 0, 1).astype(low)

    from_core = flip_exchange(half_terms(1 - core), "fsdp", 1)
    output_part = half_terms(core).astype(f32) + from_core.astype(f32)
    output_part = output_part.astype(low).reshape(4, size, half_width)
    mixed_grad, output_part, parts, side_a, side_b, outer_term = after(
        (mixed_grad, output_part, parts, side_a, side_b, outer_term)
    )
    outer_sum = lax.psum_scatter(outer_term, "dp", scatter_dimension=0, tiled=True)
    part_last = swap_near_blocks(parts, (5, 7, 3))
    output_near = [flip_exchange(output_part[k], "dp", k) for k in (1, 2)]

    grads_blocks, grads_line = attend_backward(
        spans, projected, mixed_grad, seg_row, seg_col, mixed_exact, totals
    )
    grads_blocks, grads_line, output_part, output_near, part_last = after(
        (grads_blocks, grads_line, output_part, output_near, part_last)
    )
    part_home = [parts[0], part_first[3], part_first[2], part_last[2]]
    part_home = part_home + [part_first[0], part_last[0], part_first[1], part_last[1]]
    grad_mine = all_to_all(grads_blocks).reshape(count * cols, rows)
    extra = jnp.concatenate(
        [router_part[router_lane : router_lane + experts], gain_part,
         jnp.zeros((lanes - cols - experts - 1, width), f32)]
    )
    output_near = output_near + [flip_exchange(output_part[3], "dp", 3)]
    own_group = group.reshape(1).astype(jnp.int32)
    terms = weight_terms(own_group, normed, grads_line, extra, 4)
    weight_sum = terms[0].astype(f32)
    for k in range(1, 4):
        weight_sum = weight_sum + flip_exchange(terms[k], "dp", k).astype(f32)
    inner_grad = jnp.concatenate(
        [
            inner_a[0].astype(f32) + near_a.astype(f32) + side_a.astype(f32),
            inner_b[0].astype(f32) + near_b.astype(f32) + side_b.astype(f32),
        ]
    ).reshape(size, 2, ff)
    outer_grad = outer_sum.astype(f32).T
    block_out = mixture(slots_near, gates, middle, part_home)
    output_sum = output_part[0].astype(f32)
    for near in output_near:
        output_sum = output_sum + near.astype(f32)
    weight_sum, output_sum = after((weight_sum.astype(low), output_sum), grad_mine)
    weight_home = all_to_all(weight_sum.reshape(count, shard, lanes))
    query_grad, keyval_grad, router_grad, gains = weight_grads(
        weight_home, query_weight, key_value_weight, gain_before[:, None], share, experts
    )
    before_grad, middle_grad = gains[:, 0], gains[:, 1]
    chips, pair = count // 2, 2 * shard
    output_low = output_sum.astype(low)

    def line_part(value, k):
        at = jnp.bitwise_xor(index // 2, k) * pair
        return lax.dynamic_slice_in_dim(value, at, pair, 0)

    output_grad = line_part(output_sum, 0)
    for k in range(1, chips):
        output_grad = output_grad + flip_exchange(line_part(output_low, k), "fsdp", 2 * k).astype(f32)
    own_half = lax.dynamic_slice_in_dim(output_grad, core * shard, shard, 0)
    other_half = flip_exchange(
        lax.dynamic_slice_in_dim(output_grad, (1 - core) * shard, shard, 0), "fsdp", 1
    )
    output_grad = jnp.where(
        core == 0,
        jnp.concatenate([own_half, other_half], 1),
        jnp.concatenate([other_half, own_half], 1),
    ).T
    grad_normed = contract(grad_mine, project_all, 0, 1)
    gain_first = head_weights[:, table_lane + first_lane]
    _, unit_first, factor_first = normalize(start_low.astype(f32), gain_first)
    outer_back, _ = normalize_back(grad_normed, unit_first, factor_first, gain_first)
    tokens_grad = grad_middle + outer_back
    return (
        block_out[None],
        tokens_grad[None],
        query_grad,
        keyval_grad,
        output_grad,
        router_grad,
        before_grad,
        middle_grad,
        inner_grad,
        outer_grad,
    )


def solution(mesh):
    by_heads = (mesh.shape["dp"], mesh.shape["fsdp"]) == (4, KEY_VALUE_HEADS)
    in_specs = (
        P("dp", "fsdp", None),
        P("dp", "fsdp"),
        P("dp", "fsdp", None),
        P(("dp", "fsdp"), None),
        P(("dp", "fsdp"), None),
        P(None, ("dp", "fsdp")),
        P(("dp", "fsdp"), None),
        P(("dp", "fsdp")),
        P(("dp", "fsdp")),
        P("dp", None, "fsdp"),
        P("fsdp", "dp"),
        P("dp", "fsdp", None),
    )
    out_specs = (
        P("dp", "fsdp", None),
        P("dp", "fsdp", None),
        P(("dp", "fsdp"), None),
        P(("dp", "fsdp"), None),
        P(None, ("dp", "fsdp")),
        P(("dp", "fsdp"), None),
        P(("dp", "fsdp")),
        P(("dp", "fsdp")),
        P("dp", None, "fsdp"),
        P("fsdp", "dp"),
    )
    return jax.shard_map(
        per_device_heads if by_heads else per_device, mesh=mesh, in_specs=in_specs, out_specs=out_specs, check_vma=False
    )
```

```python
import functools

import jax
import jax.numpy as jnp
from jax import lax
from jax.experimental import pallas as pl
from jax.experimental.pallas import tpu as pltpu
from jax.sharding import PartitionSpec as P

QUERY_HEADS = 24
KEY_VALUE_HEADS = 8
HEAD_SIZE = 64


HIGHEST_PRECISION = lax.Precision.HIGHEST
EPSILON = 1e-05
NEGATIVE_LARGE = -1e30


def normalize(hidden, gain_vec):
    factor = lax.rsqrt(jnp.mean(hidden * hidden, -1, keepdims=True) + EPSILON)
    unit_rows = hidden * factor
    return (unit_rows * gain_vec.astype(jnp.float32), unit_rows, factor)


def normalize_back(grad_rows, unit_rows, factor, gain_vec):
    scaled = grad_rows * gain_vec.astype(jnp.float32)
    inner_part = factor * (scaled - unit_rows * jnp.mean(scaled * unit_rows, -1, keepdims=True))
    return (inner_part, jnp.sum(grad_rows * unit_rows, 0))


def split_block(gathered, offset, key_tile_block):
    sequence_count = gathered.shape[0]
    portion_rows = lax.slice_in_dim(gathered, offset, offset + key_tile_block, axis=1)
    half_columns = KEY_VALUE_HEADS * HEAD_SIZE
    key_portion = portion_rows[..., :half_columns].reshape(
        sequence_count, key_tile_block, KEY_VALUE_HEADS, HEAD_SIZE
    )
    value_portion = portion_rows[..., half_columns:].reshape(
        sequence_count, key_tile_block, KEY_VALUE_HEADS, HEAD_SIZE
    )
    return (key_portion, value_portion)


def block_scores(query_matrix, key_portion, allowed):
    raw_scores = jnp.einsum(
        "sikgd,sjkd->skgij", query_matrix, key_portion, preferred_element_type=jnp.float32
    ) * HEAD_SIZE ** (-0.5)
    return jnp.where(allowed[:, None, None], raw_scores, NEGATIVE_LARGE)


def mask_for(seg_all, seg_mine, positions, offset, key_tile_block):
    key_seg = lax.slice_in_dim(seg_all, offset, offset + key_tile_block, axis=1)
    key_spots = offset + jnp.arange(key_tile_block, dtype=jnp.int32)
    same_doc = seg_mine[:, :, None] == key_seg[:, None, :]
    causal = key_spots[None, None, :] <= positions[None, :, None]
    return same_doc & causal


def log_totals(query_matrix, gathered, block_masks, key_tile_block):
    sequence_count, resident_rows = (query_matrix.shape[0], query_matrix.shape[1])
    running_totals = jnp.full(
        (sequence_count, KEY_VALUE_HEADS, QUERY_HEADS // KEY_VALUE_HEADS, resident_rows),
        NEGATIVE_LARGE,
        jnp.float32,
    )
    for block_index, allowed in enumerate(block_masks):
        key_portion, value_portion = split_block(
            gathered, block_index * key_tile_block, key_tile_block
        )

        def log_live(present_value, key_portion=key_portion, allowed=allowed):
            scores = block_scores(query_matrix, key_portion, allowed)
            return jnp.logaddexp(present_value, jax.nn.logsumexp(scores, -1))

        running_totals = lax.cond(
            jnp.any(allowed), log_live, lambda present_value: present_value, running_totals
        )
    return running_totals


def attend_values(query_matrix, gathered, block_masks, key_tile_block, running_totals):
    result = jnp.zeros(query_matrix.shape, jnp.float32)
    for block_index, allowed in enumerate(block_masks):
        key_portion, value_portion = split_block(
            gathered, block_index * key_tile_block, key_tile_block
        )

        def attend_live(
            present_value, key_portion=key_portion, value_portion=value_portion, allowed=allowed
        ):
            probs = jnp.exp(
                block_scores(query_matrix, key_portion, allowed) - running_totals[..., None]
            ).astype(jnp.bfloat16)
            return present_value + jnp.einsum(
                "skgij,sjkd->sikgd", probs, value_portion, preferred_element_type=jnp.float32
            )

        result = lax.cond(
            jnp.any(allowed), attend_live, lambda present_value: present_value, result
        )
    token_count = query_matrix.shape[0] * query_matrix.shape[1]
    return result.reshape(token_count, -1).astype(jnp.bfloat16)


def attend_back(
    query_matrix, mixed_gradient, gathered, block_masks, key_tile_block, running_totals
):
    sequence_count = query_matrix.shape[0]
    delta = jnp.zeros(running_totals.shape, jnp.float32)
    for block_index, allowed in enumerate(block_masks):
        key_portion, value_portion = split_block(
            gathered, block_index * key_tile_block, key_tile_block
        )

        def live_delta(
            present_value, key_portion=key_portion, value_portion=value_portion, allowed=allowed
        ):
            probs = jnp.exp(
                block_scores(query_matrix, key_portion, allowed) - running_totals[..., None]
            )
            grad_probs = jnp.einsum(
                "sikgd,sjkd->skgij",
                mixed_gradient,
                value_portion,
                preferred_element_type=jnp.float32,
            )
            return present_value + jnp.sum(probs * grad_probs, -1)

        delta = lax.cond(jnp.any(allowed), live_delta, lambda present_value: present_value, delta)
    grad_queries = jnp.zeros(query_matrix.shape, jnp.float32)
    key_terms = []
    for block_index, allowed in enumerate(block_masks):
        key_portion, value_portion = split_block(
            gathered, block_index * key_tile_block, key_tile_block
        )

        def live_grad(
            present_value, key_portion=key_portion, value_portion=value_portion, allowed=allowed
        ):
            probs = jnp.exp(
                block_scores(query_matrix, key_portion, allowed) - running_totals[..., None]
            )
            grad_probs = jnp.einsum(
                "sikgd,sjkd->skgij",
                mixed_gradient,
                value_portion,
                preferred_element_type=jnp.float32,
            )
            grad_scores = (probs * (grad_probs - delta[..., None])).astype(jnp.bfloat16)
            updated = present_value + jnp.einsum(
                "skgij,sjkd->sikgd", grad_scores, key_portion, preferred_element_type=jnp.float32
            ) * HEAD_SIZE ** (-0.5)
            grad_keys = jnp.einsum(
                "skgij,sikgd->sjkd", grad_scores, query_matrix, preferred_element_type=jnp.float32
            ) * HEAD_SIZE ** (-0.5)
            grad_values = jnp.einsum(
                "skgij,sikgd->sjkd",
                probs.astype(jnp.bfloat16),
                mixed_gradient,
                preferred_element_type=jnp.float32,
            )
            both_parts = jnp.concatenate(
                [
                    grad_keys.reshape(sequence_count, key_tile_block, -1),
                    grad_values.reshape(sequence_count, key_tile_block, -1),
                ],
                -1,
            )
            return (updated, both_parts)

        def dead_grad(present_value):
            return (
                present_value,
                jnp.zeros(
                    (sequence_count, key_tile_block, 2 * KEY_VALUE_HEADS * HEAD_SIZE), jnp.float32
                ),
            )

        grad_queries, block_term = lax.cond(jnp.any(allowed), live_grad, dead_grad, grad_queries)
        key_terms.append(block_term)
    return (grad_queries, jnp.concatenate(key_terms, 1), delta)


def expert_forward(inner_use, outer_use, received):
    model_width = received.shape[-1]
    rows_in = received.reshape(-1, model_width)
    pre_rows = jnp.dot(rows_in, inner_use, preferred_element_type=jnp.float32)
    slab_width = outer_use.shape[0]
    hidden_rows = (jax.nn.silu(pre_rows[:, :slab_width]) * pre_rows[:, slab_width:]).astype(
        jnp.bfloat16
    )
    part_rows = jnp.dot(hidden_rows, outer_use, preferred_element_type=jnp.float32).astype(
        jnp.bfloat16
    )
    return part_rows.reshape(received.shape)


def expert_back(inner_use, outer_use, rows_flat, grad_flat):
    pre_rows = jnp.dot(rows_flat, inner_use, preferred_element_type=jnp.float32)
    slab_width = outer_use.shape[0]
    gate_pre = pre_rows[:, :slab_width]
    up_pre = pre_rows[:, slab_width:]
    sigma = jax.nn.sigmoid(gate_pre)
    swish = gate_pre * sigma
    hidden_rows = (swish * up_pre).astype(jnp.bfloat16)
    grad_hidden = jnp.dot(grad_flat, outer_use.T, preferred_element_type=jnp.float32)
    grad_gate = grad_hidden * up_pre * sigma * (1.0 + gate_pre * (1.0 - sigma))
    grad_up = grad_hidden * swish
    grad_pre = jnp.concatenate([grad_gate, grad_up], 1).astype(jnp.bfloat16)
    grad_in = jnp.dot(grad_pre, inner_use.T, preferred_element_type=jnp.float32).astype(
        jnp.bfloat16
    )
    return (hidden_rows, grad_pre, grad_in)


def per_device(
    tokens,
    segment_ids,
    routes,
    query_weight,
    key_value_weight,
    output_weight,
    router_weight,
    gain_before,
    gain_middle,
    inner_weight,
    outer_weight,
    cotangent,
):
    sequence_count, resident_rows, model_width = tokens.shape
    token_count = sequence_count * resident_rows
    experts = router_weight.shape[1]
    copies = lax.axis_size("fsdp") // experts
    capacity = 3 * token_count // 8
    seg_all = lax.all_gather(segment_ids, "fsdp", axis=1, tiled=True)
    seq_length = seg_all.shape[1]
    key_tile_block = min(256, seq_length)
    positions = lax.axis_index("fsdp") * resident_rows + jnp.arange(resident_rows, dtype=jnp.int32)
    block_masks = [
        mask_for(seg_all, segment_ids, positions, offset, key_tile_block)
        for offset in range(0, seq_length, key_tile_block)
    ]
    start_rows = tokens.reshape(token_count, model_width).astype(jnp.float32)
    route_flat = routes.reshape(token_count * 2)
    picks = route_flat[:, None] == jnp.arange(experts, dtype=jnp.int32)[None, :]
    marks = picks.astype(jnp.int32)
    slot_index = route_flat * capacity + jnp.sum((jnp.cumsum(marks, 0) - marks) * marks, 1)
    chosen_mask = picks.reshape(token_count, 2, experts)

    def layer_weights():
        return (
            lax.all_gather(query_weight, ("dp", "fsdp"), axis=0, tiled=True),
            lax.all_gather(key_value_weight, ("dp", "fsdp"), axis=0, tiled=True),
            lax.all_gather(output_weight, ("dp", "fsdp"), axis=1, tiled=True),
            lax.all_gather(router_weight, ("dp", "fsdp"), axis=0, tiled=True),
            lax.all_gather(gain_before, ("dp", "fsdp"), axis=0, tiled=True),
            lax.all_gather(gain_middle, ("dp", "fsdp"), axis=0, tiled=True),
        )

    def expert_weights():
        inner_full, outer_full = (
            lax.all_gather(inner_weight, "dp", axis=0, tiled=True),
            lax.all_gather(outer_weight, "dp", axis=1, tiled=True),
        )
        return (inner_full.reshape(model_width, -1), outer_full)

    def attention_front(weights):
        normed, unit_rows, factor = normalize(start_rows, weights[4])
        normed_low = normed.astype(jnp.bfloat16)
        query_matrix = jnp.dot(normed_low, weights[0], preferred_element_type=jnp.float32).astype(
            jnp.bfloat16
        )
        query_matrix = query_matrix.reshape(
            sequence_count,
            resident_rows,
            KEY_VALUE_HEADS,
            QUERY_HEADS // KEY_VALUE_HEADS,
            HEAD_SIZE,
        )
        key_value_rows = jnp.dot(normed_low, weights[1], preferred_element_type=jnp.float32).astype(
            jnp.bfloat16
        )
        gathered = lax.all_gather(
            key_value_rows.reshape(sequence_count, resident_rows, -1), "fsdp", axis=1, tiled=True
        )
        return (normed_low, unit_rows, factor, query_matrix, gathered)

    def middle_part(weights, mixed_low):
        middle = start_rows + jnp.dot(mixed_low, weights[2], preferred_element_type=jnp.float32)
        expert_in, unit_rows, factor = normalize(middle, weights[5])
        expert_low = expert_in.astype(jnp.bfloat16)
        logits = jnp.dot(
            expert_low.astype(jnp.float32),
            weights[3].astype(jnp.float32),
            precision=HIGHEST_PRECISION,
        )
        return (middle, unit_rows, factor, expert_low, logits)

    def gates_for(logits):
        chosen_logits = jnp.sum(jnp.where(chosen_mask, logits[:, None, :], 0.0), -1)
        return jax.nn.softmax(chosen_logits, -1)

    def to_slots(pair_rows):
        packed = (
            jnp.zeros((experts * capacity, model_width), pair_rows.dtype)
            .at[slot_index]
            .set(pair_rows)
        )
        return jnp.repeat(packed.reshape(experts, capacity, model_width), copies, axis=0)

    def from_slots(returned_rows):
        summed = jnp.sum(
            returned_rows.reshape(experts, copies, capacity, model_width).astype(jnp.float32), 1
        )
        return summed.reshape(experts * capacity, model_width)[slot_index]

    weights = layer_weights()
    inner_all, outer_all = expert_weights()
    normed_low, unit_first, factor_first, query_matrix, gathered = attention_front(weights)
    running_totals = log_totals(query_matrix, gathered, block_masks, key_tile_block)
    mixed_low = attend_values(query_matrix, gathered, block_masks, key_tile_block, running_totals)
    middle, unit_second, factor_second, expert_low, logits = middle_part(weights, mixed_low)
    gates = gates_for(logits)
    sent = to_slots(jnp.repeat(expert_low, 2, axis=0))
    part_rows = expert_forward(
        inner_all, outer_all, lax.all_to_all(sent, "fsdp", split_axis=0, concat_axis=0, tiled=True)
    )
    returned_part = lax.all_to_all(part_rows, "fsdp", split_axis=0, concat_axis=0, tiled=True)
    returned_rows = returned_part
    expert_sum = from_slots(returned_rows).reshape(token_count, 2, model_width)
    block_out = (middle + jnp.sum(gates[..., None] * expert_sum, 1)).astype(jnp.bfloat16)
    grad_out = cotangent.reshape(token_count, model_width).astype(jnp.float32)
    weights = layer_weights()
    inner_use, outer_use = expert_weights()
    normed_low, unit_first, factor_first, query_matrix, gathered = attention_front(weights)
    mixed_low = attend_values(query_matrix, gathered, block_masks, key_tile_block, running_totals)
    middle, unit_second, factor_second, expert_low, logits = middle_part(weights, mixed_low)
    gates = gates_for(logits)
    sent = to_slots(jnp.repeat(expert_low, 2, axis=0))
    grad_sent = to_slots(
        (gates[..., None] * grad_out[:, None, :])
        .astype(jnp.bfloat16)
        .reshape(2 * token_count, model_width)
    )
    rows_in = lax.all_to_all(sent, "fsdp", split_axis=0, concat_axis=0, tiled=True)
    rows_grad = lax.all_to_all(grad_sent, "fsdp", split_axis=0, concat_axis=0, tiled=True)
    row_shape = rows_in.shape
    hidden_flat, grad_pre_flat, grad_in_flat = expert_back(
        inner_use, outer_use, rows_in.reshape(-1, model_width), rows_grad.reshape(-1, model_width)
    )
    part_rows = jnp.dot(hidden_flat, outer_use, preferred_element_type=jnp.float32).astype(
        jnp.bfloat16
    )
    grad_home = lax.all_to_all(
        grad_in_flat.reshape(row_shape), "fsdp", split_axis=0, concat_axis=0, tiled=True
    )
    part_home = lax.all_to_all(
        part_rows.reshape(row_shape), "fsdp", split_axis=0, concat_axis=0, tiled=True
    )
    item_shape = row_shape[:2]
    grad_pre = grad_pre_flat.reshape(item_shape + (-1,))
    hidden_rows = hidden_flat.reshape(item_shape + (-1,))
    expert_sum = from_slots(part_home).reshape(token_count, 2, model_width)
    rows_flat = rows_in.reshape(-1, model_width)
    row_total = rows_flat.shape[0]
    inner_grad_all = jnp.dot(
        rows_flat.T, grad_pre.reshape(row_total, -1), preferred_element_type=jnp.float32
    )
    outer_grad_all = jnp.dot(
        hidden_rows.reshape(row_total, -1).T,
        rows_grad.reshape(row_total, model_width),
        preferred_element_type=jnp.float32,
    )
    inner_grad, outer_grad = (
        lax.psum_scatter(
            inner_grad_all.reshape(model_width, 2, -1).astype(jnp.bfloat16),
            "dp",
            scatter_dimension=0,
            tiled=True,
        ).astype(jnp.float32),
        lax.psum_scatter(
            outer_grad_all.astype(jnp.bfloat16), "dp", scatter_dimension=1, tiled=True
        ).astype(jnp.float32),
    )
    grad_gates = jnp.sum(grad_out[:, None, :] * expert_sum, -1)
    grad_choice = gates * (grad_gates - jnp.sum(gates * grad_gates, -1, keepdims=True))
    grad_logits = jnp.sum(jnp.where(chosen_mask, grad_choice[..., None], 0.0), 1)
    router_grad_all = jnp.dot(
        expert_low.astype(jnp.float32).T, grad_logits, precision=HIGHEST_PRECISION
    )
    grad_expert_in = jnp.sum(from_slots(grad_home).reshape(token_count, 2, model_width), 1)
    grad_expert_in = grad_expert_in + jnp.dot(
        grad_logits, weights[3].astype(jnp.float32).T, precision=HIGHEST_PRECISION
    )
    grad_norm_second, middle_gain_grad = normalize_back(
        grad_expert_in, unit_second, factor_second, weights[5]
    )
    grad_middle = grad_out + grad_norm_second
    grad_branch = grad_middle.astype(jnp.bfloat16)
    output_grad_all = jnp.dot(mixed_low.T, grad_branch, preferred_element_type=jnp.float32)
    mixed_gradient = jnp.dot(grad_branch, weights[2].T, preferred_element_type=jnp.float32).astype(
        jnp.bfloat16
    )
    mixed_gradient = mixed_gradient.reshape(
        sequence_count, resident_rows, KEY_VALUE_HEADS, QUERY_HEADS // KEY_VALUE_HEADS, HEAD_SIZE
    )
    grad_queries, key_terms, delta = attend_back(
        query_matrix, mixed_gradient, gathered, block_masks, key_tile_block, running_totals
    )
    key_grads = lax.psum_scatter(
        key_terms.astype(jnp.bfloat16), "fsdp", scatter_dimension=1, tiled=True
    ).reshape(token_count, -1)
    query_low = grad_queries.reshape(token_count, -1).astype(jnp.bfloat16)
    grad_normed = jnp.dot(query_low, weights[0].T, preferred_element_type=jnp.float32) + jnp.dot(
        key_grads, weights[1].T, preferred_element_type=jnp.float32
    )
    query_grad_all = jnp.dot(normed_low.T, query_low, preferred_element_type=jnp.float32)
    keyval_grad_all = jnp.dot(normed_low.T, key_grads, preferred_element_type=jnp.float32)
    grad_norm_first, before_gain_grad = normalize_back(
        grad_normed, unit_first, factor_first, weights[4]
    )
    tokens_grad = grad_middle + grad_norm_first
    summed_grads = (
        lax.psum_scatter(query_grad_all, ("dp", "fsdp"), scatter_dimension=0, tiled=True),
        lax.psum_scatter(keyval_grad_all, ("dp", "fsdp"), scatter_dimension=0, tiled=True),
        lax.psum_scatter(output_grad_all, ("dp", "fsdp"), scatter_dimension=1, tiled=True),
        lax.psum_scatter(router_grad_all, ("dp", "fsdp"), scatter_dimension=0, tiled=True),
        lax.psum_scatter(before_gain_grad, ("dp", "fsdp"), scatter_dimension=0, tiled=True),
        lax.psum_scatter(middle_gain_grad, ("dp", "fsdp"), scatter_dimension=0, tiled=True),
    )
    return (
        block_out.reshape(sequence_count, resident_rows, model_width),
        tokens_grad.reshape(sequence_count, resident_rows, model_width),
        summed_grads[0],
        summed_grads[1],
        summed_grads[2],
        summed_grads[3],
        summed_grads[4],
        summed_grads[5],
        inner_grad,
        outer_grad,
    )


def contract(left, right, left_axis, right_axis):
    return lax.dot_general(
        left, right, (((left_axis,), (right_axis,)), ((), ())), preferred_element_type=jnp.float32
    )


def unit_of(rows):
    factor = lax.rsqrt(jnp.mean(rows * rows, -1, keepdims=True) + EPSILON)
    return (rows * factor, factor)


def column_as_row(table, lane):
    pick = (lax.broadcasted_iota(jnp.int32, (8, table.shape[1]), 1) == lane).astype(jnp.bfloat16)
    return contract(pick, table, 1, 1)[:1]


def split_low(value):
    high = value.astype(jnp.bfloat16)
    return (high, (value - high.astype(jnp.float32)).astype(jnp.bfloat16))


def project_kernel(lane, rows_ref, weight_ref, table_ref, normed_ref, heads_ref, gain):
    @pl.when(pl.program_id(0) == 0)
    def _():
        gain[...] = column_as_row(table_ref[...], lane)

    unit, _ = unit_of(rows_ref[...].astype(jnp.float32))
    normed = (unit * gain[...]).astype(jnp.bfloat16)
    normed_ref[...] = normed
    heads = jnp.dot(normed, weight_ref[...], preferred_element_type=jnp.float32)
    heads_ref[0] = heads.T[: heads_ref.shape[1]].astype(jnp.bfloat16)


def project(rows, head_weights, wide, lane, block):
    length, width = rows.shape
    lanes = head_weights.shape[1]
    blocks = length // block
    return pl.pallas_call(
        functools.partial(project_kernel, lane),
        grid=(blocks,),
        in_specs=[
            pl.BlockSpec((block, width), lambda i: (i, 0)),
            pl.BlockSpec((width, lanes), lambda i: (0, 0)),
            pl.BlockSpec((width, 128), lambda i: (0, lanes // 128 - 1)),
        ],
        out_specs=[
            pl.BlockSpec((block, width), lambda i: (i, 0)),
            pl.BlockSpec((1, wide, block), lambda i: (i, 0, 0)),
        ],
        out_shape=[
            jax.ShapeDtypeStruct((length, width), jnp.bfloat16),
            jax.ShapeDtypeStruct((blocks, wide, block), jnp.bfloat16),
        ],
        scratch_shapes=[pltpu.VMEM((1, width), jnp.float32)],
        compiler_params=pltpu.CompilerParams(vmem_limit_bytes=60 * 2**20),
        name="project",
    )(rows, head_weights, head_weights)


def beside(rows, block, heads):
    return jnp.concatenate([rows[h * HEAD_SIZE : (h + 1) * HEAD_SIZE] for h in range(heads)], 1)


def attend_kernel(spans, q_ref, heads_ref, segr_ref, segc_ref, low_ref, mixed_ref, totals_ref):
    step = pl.program_id(0)
    block = q_ref.shape[2]
    heads = QUERY_HEADS // KEY_VALUE_HEADS
    share = heads * HEAD_SIZE
    queries = beside(q_ref[0, :share, :] * jnp.bfloat16(HEAD_SIZE ** (-0.5)), block, heads)
    seg_row = segr_ref[...]

    def scores_of(j):
        return contract(heads_ref[j, share : share + HEAD_SIZE, :], queries, 0, 0)

    def same_doc(j):
        return segc_ref[pl.ds(pl.multiple_of(j * block, block), block), :] == seg_row

    def fold(j, scores, carry):
        top, total, out = carry
        values = heads_ref[j, share + HEAD_SIZE : share + 2 * HEAD_SIZE, :]
        new_top = jnp.maximum(top, jnp.max(scores, 0, keepdims=True))
        probs = jnp.exp(scores - new_top)
        decay = jnp.exp(top - new_top)
        total = total * decay + jnp.sum(probs, 0, keepdims=True)
        out = out * decay + jnp.dot(
            values, probs.astype(jnp.bfloat16), preferred_element_type=jnp.float32
        )
        return (new_top, total, out)

    def masked(j, carry):
        allowed = jnp.concatenate([same_doc(j)] * heads, 1)
        return fold(j, jnp.where(allowed, scores_of(j), NEGATIVE_LARGE), carry)

    columns = heads * block
    carry = (
        jnp.full((1, columns), NEGATIVE_LARGE, jnp.float32),
        jnp.zeros((1, columns), jnp.float32),
        jnp.zeros((HEAD_SIZE, columns), jnp.float32),
    )
    first, full = spans[0, step], spans[1, step]
    carry = lax.fori_loop(first, full, masked, carry)
    carry = lax.fori_loop(full, step, lambda j, kept: fold(j, scores_of(j), kept), carry)
    key_spot = lax.broadcasted_iota(jnp.int32, (block, block), 0)
    query_spot = lax.broadcasted_iota(jnp.int32, (block, block), 1)
    allowed = same_doc(step) & (key_spot <= query_spot)
    allowed = jnp.concatenate([allowed] * heads, 1)
    top, total, out = fold(step, jnp.where(allowed, scores_of(step), NEGATIVE_LARGE), carry)
    out = out / total
    totals = top + jnp.log(total)
    for h in range(heads):
        part = out[:, h * block : (h + 1) * block]
        mixed_ref[0, h * HEAD_SIZE : (h + 1) * HEAD_SIZE, :] = part
        low_ref[0, h * HEAD_SIZE : (h + 1) * HEAD_SIZE, :] = part.astype(jnp.bfloat16)
        totals_ref[0, h : h + 1, :] = totals[:, h * block : (h + 1) * block]


def attend(spans, projected, seg_row, seg_col):
    blocks, wide, block = projected.shape
    share = wide - 2 * HEAD_SIZE
    length = blocks * block
    each = lambda height: pl.BlockSpec((1, height, block), lambda i, spans: (i, 0, 0))
    return pl.pallas_call(
        attend_kernel,
        grid_spec=pltpu.PrefetchScalarGridSpec(
            num_scalar_prefetch=1,
            grid=(blocks,),
            in_specs=[
                pl.BlockSpec((1, wide, block), lambda i, spans: (i, 0, 0)),
                pl.BlockSpec((blocks, wide, block), lambda i, spans: (0, 0, 0)),
                pl.BlockSpec((1, block), lambda i, spans: (0, i)),
                pl.BlockSpec((length, 1), lambda i, spans: (0, 0)),
            ],
            out_specs=[each(share), each(share), each(8)],
        ),
        out_shape=[
            jax.ShapeDtypeStruct((blocks, share, block), jnp.bfloat16),
            jax.ShapeDtypeStruct((blocks, share, block), jnp.float32),
            jax.ShapeDtypeStruct((blocks, 8, block), jnp.float32),
        ],
        compiler_params=pltpu.CompilerParams(vmem_limit_bytes=40 * 2**20),
        name="attend",
    )(spans, projected, projected, seg_row, seg_col)


def attend_back_kernel(
    spans, q_ref, g_ref, heads_ref, segr_ref, segc_ref, mixed_ref, totals_ref,
    blocks_ref, line_ref, dk_sum, dv_sum,
):
    step = pl.program_id(0)
    blocks, _, block = heads_ref.shape
    heads = QUERY_HEADS // KEY_VALUE_HEADS
    share = heads * HEAD_SIZE
    queries = beside(q_ref[0, :share, :] * jnp.bfloat16(HEAD_SIZE ** (-0.5)), block, heads)
    grads = beside(g_ref[0], block, heads)
    delta = jnp.sum(
        grads.astype(jnp.float32) * beside(mixed_ref[0], block, heads), 0, keepdims=True
    )
    totals = jnp.concatenate([totals_ref[0, h : h + 1, :] for h in range(heads)], 1)
    seg_row = segr_ref[...]

    @pl.when(step == 0)
    def _():
        dk_sum[...] = jnp.zeros_like(dk_sum)
        dv_sum[...] = jnp.zeros_like(dv_sum)

    def turn(j, query_sum, allowed):
        keys = heads_ref[j, share : share + HEAD_SIZE, :]
        values = heads_ref[j, share + HEAD_SIZE : share + 2 * HEAD_SIZE, :]
        probs = jnp.exp(contract(keys, queries, 0, 0) - totals)
        if allowed is not None:
            probs = jnp.where(jnp.concatenate([allowed] * heads, 1), probs, 0.0)
        grad_scores = (probs * (contract(values, grads, 0, 0) - delta)).astype(jnp.bfloat16)
        dv_sum[j] += contract(grads, probs.astype(jnp.bfloat16), 1, 1)
        dk_sum[j] += contract(queries, grad_scores, 1, 1)
        return query_sum + jnp.dot(keys, grad_scores, preferred_element_type=jnp.float32)

    def same_doc(j):
        return segc_ref[pl.ds(pl.multiple_of(j * block, block), block), :] == seg_row

    query_sum = jnp.zeros((HEAD_SIZE, heads * block), jnp.float32)
    first, full = spans[0, step], spans[1, step]
    query_sum = lax.fori_loop(first, full, lambda j, c: turn(j, c, same_doc(j)), query_sum)
    query_sum = lax.fori_loop(full, step, lambda j, c: turn(j, c, None), query_sum)
    key_spot = lax.broadcasted_iota(jnp.int32, (block, block), 0)
    query_spot = lax.broadcasted_iota(jnp.int32, (block, block), 1)
    query_sum = turn(step, query_sum, same_doc(step) & (key_spot <= query_spot))
    query_sum = (query_sum * HEAD_SIZE ** (-0.5)).astype(jnp.bfloat16)

    def spread(j, at, size, value):
        blocks_ref[j, at : at + size, :] = value
        there = pl.ds(pl.multiple_of(j * block, block), block)
        line_ref[at : at + size, there] = value

    for h in range(heads):
        spread(step, h * HEAD_SIZE, HEAD_SIZE, query_sum[:, h * block : (h + 1) * block])

    @pl.when(step == pl.num_programs(0) - 1)
    def _():
        for j in range(blocks):
            spread(j, share, HEAD_SIZE, dk_sum[j].astype(jnp.bfloat16))
            spread(j, share + HEAD_SIZE, HEAD_SIZE, dv_sum[j].astype(jnp.bfloat16))


def attend_backward(spans, projected, grads, seg_row, seg_col, mixed, totals):
    blocks, wide, block = projected.shape
    share = wide - 2 * HEAD_SIZE
    length = blocks * block
    each = lambda height: pl.BlockSpec((1, height, block), lambda i, spans: (i, 0, 0))
    return pl.pallas_call(
        attend_back_kernel,
        grid_spec=pltpu.PrefetchScalarGridSpec(
            num_scalar_prefetch=1,
            grid=(blocks,),
            in_specs=[
                pl.BlockSpec((1, wide, block), lambda i, spans: (i, 0, 0)),
                each(share),
                pl.BlockSpec((blocks, wide, block), lambda i, spans: (0, 0, 0)),
                pl.BlockSpec((1, block), lambda i, spans: (0, i)),
                pl.BlockSpec((length, 1), lambda i, spans: (0, 0)),
                each(share),
                each(8),
            ],
            out_specs=[
                pl.BlockSpec((blocks, wide, block), lambda i, spans: (0, 0, 0)),
                pl.BlockSpec((wide, length), lambda i, spans: (0, 0)),
            ],
            scratch_shapes=[
                pltpu.VMEM((blocks, HEAD_SIZE, block), jnp.float32),
                pltpu.VMEM((blocks, HEAD_SIZE, block), jnp.float32),
            ],
        ),
        out_shape=[
            jax.ShapeDtypeStruct((blocks, wide, block), jnp.bfloat16),
            jax.ShapeDtypeStruct((wide, length), jnp.bfloat16),
        ],
        compiler_params=pltpu.CompilerParams(vmem_limit_bytes=40 * 2**20),
        name="attend_backward",
    )(spans, projected, grads, projected, seg_row, seg_col, mixed, totals)


def hits(slots, height):
    spot = lax.broadcasted_iota(jnp.int32, (height, slots.shape[1]), 0)
    return (spot == slots[0:1, :], spot == slots[1:2, :])


def spread_kernel(slots_ref, rows_ref, *out_refs):
    size = out_refs[0].shape[0]
    first, second = hits(slots_ref[...], size * len(out_refs))
    chosen = (first | second).astype(jnp.bfloat16)
    for k, out_ref in enumerate(out_refs):
        out_ref[...] = jnp.dot(
            chosen[k * size : (k + 1) * size], rows_ref[...], preferred_element_type=jnp.float32
        ).astype(jnp.bfloat16)


def spread_rows(slots, rows, size, blocks):
    return pl.pallas_call(
        spread_kernel,
        out_shape=[jax.ShapeDtypeStruct((size, rows.shape[1]), jnp.bfloat16)] * blocks,
        compiler_params=pltpu.CompilerParams(vmem_limit_bytes=40 * 2**20),
        name="spread_rows",
    )(slots, rows)


def middle_kernel(
    lane, router_lane, start_ref, mixed_ref, weight_ref, table_ref, slots_ref, routes_ref,
    middle_ref, sent_ref, gates_ref,
):
    table = table_ref[...]
    middle = start_ref[...].astype(jnp.float32) + contract(mixed_ref[...].T, weight_ref[...], 1, 1)
    middle_ref[...] = middle
    unit, _ = unit_of(middle)
    expert_low = (unit * column_as_row(table, lane)).astype(jnp.bfloat16)
    first, second = hits(slots_ref[...], sent_ref.shape[0])
    sent_ref[...] = jnp.dot(
        (first | second).astype(jnp.bfloat16), expert_low, preferred_element_type=jnp.float32
    ).astype(jnp.bfloat16)
    logits = jnp.dot(expert_low, table, preferred_element_type=jnp.float32).T
    spot = lax.broadcasted_iota(jnp.int32, logits.shape, 0) - router_lane
    chosen = [
        jnp.sum(jnp.where(spot == routes_ref[c : c + 1, :], logits, 0.0), 0, keepdims=True)
        for c in range(2)
    ]
    top = jnp.maximum(chosen[0], chosen[1])
    parts = [jnp.exp(value - top) for value in chosen]
    gates_ref[...] = jnp.concatenate([part / (parts[0] + parts[1]) for part in parts], 0)


def middle_part(start, mixed, weight, head_weights, slots, routes, lane, router_lane, height):
    rows, width = start.shape
    lanes = head_weights.shape[1]
    whole = lambda shape: pl.BlockSpec(shape, lambda i: (0, 0))
    return pl.pallas_call(
        functools.partial(middle_kernel, lane, router_lane),
        grid=(1,),
        in_specs=[
            whole(start.shape),
            whole(mixed.shape),
            whole(weight.shape),
            pl.BlockSpec((width, 128), lambda i: (0, lanes // 128 - 1)),
            whole(slots.shape),
            whole(routes.shape),
        ],
        out_specs=[whole((rows, width)), whole((height, width)), whole((2, rows))],
        out_shape=[
            jax.ShapeDtypeStruct((rows, width), jnp.float32),
            jax.ShapeDtypeStruct((height, width), jnp.bfloat16),
            jax.ShapeDtypeStruct((2, rows), jnp.float32),
        ],
        compiler_params=pltpu.CompilerParams(vmem_limit_bytes=60 * 2**20),
        name="middle",
    )(start, mixed, weight, head_weights, slots, routes)


def block_place(own_ref, axis, k, size):
    return pl.ds(pl.multiple_of(jnp.bitwise_xor(own_ref[axis], k) * size, size), size)


def assemble_weights(own_ref, part_refs, gate, up, outer):
    count = len(part_refs) // 3
    for k in range(count):
        size = part_refs[k].shape[0]
        place = block_place(own_ref, 1, k, size)
        gate[place, :] = part_refs[k][...]
        up[place, :] = part_refs[count + k][...]
        outer[:, place] = part_refs[2 * count + k][...]


def expert_kernel(router_lane, blocks, own_ref, rows_ref, *refs):
    weight_refs, (table_ref, other_ref) = refs[:12], refs[12:14]
    pre_gate_ref, pre_up_ref, hidden_ref, gates_ref = refs[14:18]
    part_refs, (part_sum, gate, up, outer) = refs[18 : 18 + blocks], refs[18 + blocks :]
    step = pl.program_id(0)
    size = part_refs[0].shape[0]
    rows = rows_ref[...]
    assemble_weights(own_ref, weight_refs, gate, up, outer)

    @pl.when(step == 0)
    def _():
        lane = lax.broadcasted_iota(jnp.int32, (rows.shape[0], 128), 1) - router_lane
        logits = jnp.dot(rows, table_ref[...], preferred_element_type=jnp.float32)
        own = jnp.sum(jnp.where(lane == own_ref[0], logits, 0.0), 1, keepdims=True)
        other = jnp.sum(jnp.where(lane == other_ref[...], logits, 0.0), 1, keepdims=True)
        top = jnp.maximum(own, other)
        own, other = jnp.exp(own - top), jnp.exp(other - top)
        gates_ref[:, 0:1] = own / (own + other)
        gates_ref[:, 1:2] = other / (own + other)
        part_sum[...] = jnp.zeros_like(part_sum)

    gate_pre = jnp.dot(rows, gate[...], preferred_element_type=jnp.float32)
    up_pre = jnp.dot(rows, up[...], preferred_element_type=jnp.float32)
    pre_gate_ref[...] = gate_pre
    pre_up_ref[...] = up_pre
    hidden = (gate_pre / (1.0 + jnp.exp(-gate_pre)) * up_pre).astype(jnp.bfloat16)
    hidden_ref[...] = hidden
    part_sum[...] += jnp.dot(hidden, outer[...], preferred_element_type=jnp.float32)

    @pl.when(step == pl.num_programs(0) - 1)
    def _():
        for k, ref in enumerate(part_refs):
            ref[...] = part_sum[block_place(own_ref, 0, k, size), :].astype(jnp.bfloat16)


def weight_specs(inner, outer, tile, steps):
    size = inner[0].shape[0]
    return (
        [pl.BlockSpec((size, tile), lambda i, own: (0, i))] * len(inner)
        + [pl.BlockSpec((size, tile), lambda i, own: (0, steps + i))] * len(inner)
        + [pl.BlockSpec((tile, size), lambda i, own: (i, 0))] * len(outer)
    )


def expert_forward_pass(own, rows, inner, outer, head_weights, other, router_lane, tile, blocks):
    height, width = rows.shape
    units = outer[0].shape[0]
    steps = units // tile
    lanes = head_weights.shape[1]
    whole = lambda shape: pl.BlockSpec(shape, lambda i, own: (0, 0))
    tiled = lambda rows, off: pl.BlockSpec((rows, tile), lambda i, own: (0, off + i))
    shape = jax.ShapeDtypeStruct
    low, f32 = jnp.bfloat16, jnp.float32
    outcome = pl.pallas_call(
        functools.partial(expert_kernel, router_lane, blocks),
        grid_spec=pltpu.PrefetchScalarGridSpec(
            num_scalar_prefetch=1,
            grid=(steps,),
            in_specs=[whole(rows.shape)]
            + weight_specs(inner, outer, tile, steps)
            + [
                pl.BlockSpec((width, 128), lambda i, own: (0, lanes // 128 - 1)),
                whole(other.shape),
            ],
            out_specs=[tiled(height, 0)] * 3
            + [whole((height, 128))]
            + [whole((height // blocks, width))] * blocks,
            scratch_shapes=[
                pltpu.VMEM((height, width), f32),
                pltpu.VMEM((width, tile), low),
                pltpu.VMEM((width, tile), low),
                pltpu.VMEM((tile, width), low),
            ],
        ),
        out_shape=[shape((height, units), f32)] * 2
        + [shape((height, units), low), shape((height, 128), f32)]
        + [shape((height // blocks, width), low)] * blocks,
        compiler_params=pltpu.CompilerParams(vmem_limit_bytes=56 * 2**20),
        name="expert",
    )(own, rows, *inner, *inner, *outer, head_weights, other)
    return outcome[:4], list(outcome[4:])


def expert_back_kernel(router_lane, blocks, own_ref, *refs):
    cot_refs, part_refs, refs = refs[:blocks], refs[blocks : 2 * blocks], refs[2 * blocks :]
    rows_ref, gates_ref, pre_gate_ref, pre_up_ref = refs[:4]
    weight_refs, refs = refs[4:16], refs[16:]
    table_ref, other_ref, grad_gate_ref, grad_up_ref, grad_ref, back_ref, router_ref = refs[:7]
    cot, back_sum, gate, up, outer = refs[7:]
    step = pl.program_id(0)
    assemble_weights(own_ref, weight_refs, gate, up, outer)
    size = cot_refs[0].shape[0]
    gates = gates_ref[...]

    @pl.when(step == 0)
    def _():
        for k, ref in enumerate(cot_refs):
            cot[block_place(own_ref, 0, k, size), :] = ref[...]
        grad_ref[...] = (gates[:, 0:1] * cot[...].astype(jnp.float32)).astype(jnp.bfloat16)
        back_sum[...] = jnp.zeros_like(back_sum)

    gate_pre, up_pre = pre_gate_ref[...], pre_up_ref[...]
    grad_hidden = contract(grad_ref[...], outer[...], 1, 1)
    sigma = 1.0 / (1.0 + jnp.exp(-gate_pre))
    grad_gate = grad_hidden * up_pre * sigma * (1.0 + gate_pre * (1.0 - sigma))
    grad_gate = grad_gate.astype(jnp.bfloat16)
    grad_up = (grad_hidden * (gate_pre * sigma)).astype(jnp.bfloat16)
    grad_gate_ref[...] = grad_gate
    grad_up_ref[...] = grad_up
    back_sum[...] += contract(grad_gate, gate[...], 1, 1) + contract(grad_up, up[...], 1, 1)

    @pl.when(step == pl.num_programs(0) - 1)
    def _():
        table = table_ref[...]
        total = jnp.zeros(router_ref.shape, jnp.float32)
        for k in range(blocks):
            place = block_place(own_ref, 0, k, size)
            grad_gates = jnp.sum(
                cot_refs[k][...].astype(jnp.float32) * part_refs[k][...].astype(jnp.float32),
                1,
                keepdims=True,
            )
            gates_k = gates_ref[place, :]
            lane_k = lax.broadcasted_iota(jnp.int32, (size, 128), 1) - router_lane
            sides_k = (lane_k == own_ref[0]).astype(jnp.float32) - (
                lane_k == other_ref[place, :]
            ).astype(jnp.float32)
            high, rest = split_low(gates_k[:, 0:1] * gates_k[:, 1:2] * grad_gates * sides_k)
            routed = contract(high, table, 1, 1) + contract(rest, table, 1, 1)
            back = back_sum[place, :].astype(jnp.bfloat16).astype(jnp.float32)
            back_ref[place, :] = (back + routed).astype(jnp.bfloat16)
            rows_k = rows_ref[place, :]
            total = total + contract(high, rows_k, 0, 0) + contract(rest, rows_k, 0, 0)
        router_ref[...] = total


def expert_backward_pass(
    own, cot_blocks, part_blocks, rows, gates, pre_gate, pre_up, inner, outer, head_weights, other,
    router_lane, tile,
):
    height, width = rows.shape
    units = outer[0].shape[0]
    steps = units // tile
    lanes = head_weights.shape[1]
    blocks = len(cot_blocks)
    whole = lambda shape: pl.BlockSpec(shape, lambda i, own: (0, 0))
    tiled = lambda rows, off: pl.BlockSpec((rows, tile), lambda i, own: (0, off + i))
    low, f32 = jnp.bfloat16, jnp.float32
    return pl.pallas_call(
        functools.partial(expert_back_kernel, router_lane, blocks),
        grid_spec=pltpu.PrefetchScalarGridSpec(
            num_scalar_prefetch=1,
            grid=(steps,),
            in_specs=[whole((height // blocks, width))] * (2 * blocks)
            + [
                whole(rows.shape),
                whole(gates.shape),
                tiled(height, 0),
                tiled(height, 0),
            ]
            + weight_specs(inner, outer, tile, steps)
            + [
                pl.BlockSpec((width, 128), lambda i, own: (0, lanes // 128 - 1)),
                whole(other.shape),
            ],
            out_specs=[
                tiled(height, 0),
                tiled(height, 0),
                whole((height, width)),
                whole((height, width)),
                whole((128, width)),
            ],
            scratch_shapes=[
                pltpu.VMEM((height, width), low),
                pltpu.VMEM((height, width), f32),
                pltpu.VMEM((width, tile), low),
                pltpu.VMEM((width, tile), low),
                pltpu.VMEM((tile, width), low),
            ],
        ),
        out_shape=[
            jax.ShapeDtypeStruct((height, units), low),
            jax.ShapeDtypeStruct((height, units), low),
            jax.ShapeDtypeStruct((height, width), low),
            jax.ShapeDtypeStruct((height, width), low),
            jax.ShapeDtypeStruct((128, width), f32),
        ],
        compiler_params=pltpu.CompilerParams(vmem_limit_bytes=56 * 2**20),
        name="expert_backward",
    )(
        own, *cot_blocks, *part_blocks, rows, gates, pre_gate, pre_up, *inner, *inner, *outer,
        head_weights, other,
    )


def back_kernel(
    lane, middle_ref, cot_ref, home_ref, weight_ref, table_ref, slots_ref,
    grad_ref, branch_ref, gain_ref, mixed_ref,
):
    first, second = hits(slots_ref[...], home_ref.shape[0])
    grad_in = contract((first | second).astype(jnp.bfloat16), home_ref[...], 0, 0)
    unit, factor = unit_of(middle_ref[...])
    gain_ref[...] = jnp.sum(grad_in * unit, 0, keepdims=True)
    scaled = grad_in * column_as_row(table_ref[...], lane)
    inner_part = factor * (scaled - unit * jnp.mean(scaled * unit, -1, keepdims=True))
    grad_middle = cot_ref[...].astype(jnp.float32) + inner_part
    grad_ref[...] = grad_middle
    branch = grad_middle.astype(jnp.bfloat16)
    branch_ref[...] = branch
    mixed = jnp.dot(branch, weight_ref[...], preferred_element_type=jnp.float32)
    mixed_ref[...] = mixed.T.astype(jnp.bfloat16)


def back_part(middle, cot, home, weight, head_weights, slots, lane):
    rows, width = middle.shape
    lanes = head_weights.shape[1]
    whole = lambda shape: pl.BlockSpec(shape, lambda i: (0, 0))
    return pl.pallas_call(
        functools.partial(back_kernel, lane),
        grid=(1,),
        in_specs=[
            whole((rows, width)),
            whole((rows, width)),
            whole(home.shape),
            whole(weight.shape),
            pl.BlockSpec((width, 128), lambda i: (0, lanes // 128 - 1)),
            whole(slots.shape),
        ],
        out_specs=[
            whole((rows, width)),
            whole((rows, width)),
            whole((1, width)),
            whole((weight.shape[1], rows)),
        ],
        out_shape=[
            jax.ShapeDtypeStruct((rows, width), jnp.float32),
            jax.ShapeDtypeStruct((rows, width), jnp.bfloat16),
            jax.ShapeDtypeStruct((1, width), jnp.float32),
            jax.ShapeDtypeStruct((weight.shape[1], rows), jnp.bfloat16),
        ],
        compiler_params=pltpu.CompilerParams(vmem_limit_bytes=48 * 2**20),
        name="back",
    )(middle, cot, home, weight, head_weights, slots)


def weight_kernel(place, normed_ref, grads_ref, extra_ref, out_ref):
    total = jnp.dot(grads_ref[...], normed_ref[...], preferred_element_type=jnp.float32)
    out_ref[0] = jnp.concatenate([total, extra_ref[...]], 0).T.astype(jnp.bfloat16)


def weight_terms(place, normed, grads, extra, parts):
    length, width = normed.shape
    wide = grads.shape[0]
    span = width // parts
    lanes = wide + extra.shape[0]
    near = lambda k, place: (0, jnp.bitwise_xor(place[0], k))
    return pl.pallas_call(
        weight_kernel,
        grid_spec=pltpu.PrefetchScalarGridSpec(
            num_scalar_prefetch=1,
            grid=(parts,),
            in_specs=[
                pl.BlockSpec((length, span), near),
                pl.BlockSpec((wide, length), lambda k, place: (0, 0)),
                pl.BlockSpec((extra.shape[0], span), near),
            ],
            out_specs=pl.BlockSpec((1, span, lanes), lambda k, place: (k, 0, 0)),
        ),
        out_shape=jax.ShapeDtypeStruct((parts, span, lanes), jnp.bfloat16),
        compiler_params=pltpu.CompilerParams(vmem_limit_bytes=40 * 2**20),
        name="weight_terms",
    )(place, normed, grads, extra)


def mixture_kernel(slots_ref, gates_ref, middle_ref, *refs):
    part_refs, out_ref = refs[:-1], refs[-1]
    size = part_refs[0].shape[0]
    first, second = hits(slots_ref[...], size * len(part_refs))
    total = middle_ref[...]
    shares = gates_ref[...]
    for _ in range(3):
        piece = shares.astype(jnp.bfloat16)
        shares = shares - piece.astype(jnp.float32)
        piece = piece.astype(jnp.float32)
        weights = jnp.where(first, piece[0:1], 0.0) + jnp.where(second, piece[1:2], 0.0)
        weights = weights.astype(jnp.bfloat16)
        for k, ref in enumerate(part_refs):
            total = total + contract(weights[k * size : (k + 1) * size], ref[...], 0, 0)
    out_ref[...] = total.astype(jnp.bfloat16)


def mixture(slots, gates, middle, parts):
    return pl.pallas_call(
        mixture_kernel,
        out_shape=jax.ShapeDtypeStruct(middle.shape, jnp.bfloat16),
        compiler_params=pltpu.CompilerParams(vmem_limit_bytes=40 * 2**20),
        name="mixture",
    )(slots, gates, middle, *parts)


def weight_grads_kernel(
    share, home_ref, query_weight_ref, keyval_weight_ref, gain_ref,
    query_ref, keyval_ref, router_ref, gains_ref,
):
    count = home_ref.shape[0]
    cols = share + 2 * HEAD_SIZE
    half = count * HEAD_SIZE
    experts = router_ref.shape[1]
    small = jnp.zeros((home_ref.shape[1], home_ref.shape[2] - cols), jnp.float32)
    for e in range(count):
        part = home_ref[e].astype(jnp.float32)
        query_ref[:, e * share : (e + 1) * share] = part[:, :share]
        at = e * HEAD_SIZE
        keyval_ref[:, at : at + HEAD_SIZE] = part[:, share : share + HEAD_SIZE]
        keyval_ref[:, half + at : half + at + HEAD_SIZE] = part[:, share + HEAD_SIZE : cols]
        small = small + part[:, cols:]
    router_ref[...] = small[:, :experts]
    products = jnp.sum(
        query_ref[...] * query_weight_ref[...].astype(jnp.float32), 1, keepdims=True
    ) + jnp.sum(keyval_ref[...] * keyval_weight_ref[...].astype(jnp.float32), 1, keepdims=True)
    gains_ref[:, 0:1] = products / gain_ref[...].astype(jnp.float32)
    gains_ref[:, 1:2] = small[:, experts : experts + 1]


def weight_grads(home, query_weight, keyval_weight, gain, share, experts):
    shape = lambda width: jax.ShapeDtypeStruct((query_weight.shape[0], width), jnp.float32)
    return pl.pallas_call(
        functools.partial(weight_grads_kernel, share),
        out_shape=[
            shape(query_weight.shape[1]),
            shape(keyval_weight.shape[1]),
            shape(experts),
            shape(2),
        ],
        compiler_params=pltpu.CompilerParams(vmem_limit_bytes=40 * 2**20),
        name="weight_grads",
    )(home, query_weight, keyval_weight, gain)


def sum_pairs_kernel(*refs):
    out_ref = refs[-1]
    count = len(refs) // 2
    for side in range(2):
        total = sum(ref[...].astype(jnp.float32) for ref in refs[side * count : (side + 1) * count])
        out_ref[:, side, :] = total


def sum_pairs(first, second, tile):
    rows, width = first[0].shape
    return pl.pallas_call(
        sum_pairs_kernel,
        grid=(rows // tile,),
        in_specs=[pl.BlockSpec((tile, width), lambda i: (i, 0))] * (len(first) + len(second)),
        out_specs=pl.BlockSpec((tile, 2, width), lambda i: (i, 0, 0)),
        out_shape=jax.ShapeDtypeStruct((rows, 2, width), jnp.float32),
        compiler_params=pltpu.CompilerParams(vmem_limit_bytes=40 * 2**20),
        name="sum_pairs",
    )(*first, *second)


def after(values, *earlier):
    return lax.optimization_barrier((values, earlier))[0]


def flip_exchange(block, axis, flip):
    count = lax.axis_size(axis)
    return lax.ppermute(block, axis, [(i, i ^ flip) for i in range(count)])


def swap_near_blocks(blocks, flips):
    return [flip_exchange(blocks[flip], "fsdp", flip) for flip in flips]


def swap_near(block, axis, flips):
    return [flip_exchange(block, axis, flip) for flip in flips]


def in_order(parts, axis):
    stacked = jnp.stack(parts)
    index = lax.axis_index(axis)
    return jnp.stack(
        [
            lax.dynamic_index_in_dim(stacked, jnp.bitwise_xor(index, j), 0, keepdims=False)
            for j in range(len(parts))
        ]
    )


def all_to_all(blocks):
    return lax.all_to_all(blocks, "fsdp", split_axis=0, concat_axis=0, tiled=True)


def gather(block, axis):
    return lax.all_gather(block, axis, axis=0, tiled=True)


def per_device_heads(
    tokens,
    segment_ids,
    routes,
    query_weight,
    key_value_weight,
    output_weight,
    router_weight,
    gain_before,
    gain_middle,
    inner_weight,
    outer_weight,
    cotangent,
):
    f32, low = jnp.float32, jnp.bfloat16
    _, rows, width = tokens.shape
    count = lax.axis_size("fsdp")
    experts = router_weight.shape[1]
    index, group = lax.axis_index("fsdp"), lax.axis_index("dp")
    core = index % 2
    capacity = 3 * rows // 8
    height = experts * capacity
    length = count * rows
    shard = query_weight.shape[0]
    share = QUERY_HEADS // KEY_VALUE_HEADS * HEAD_SIZE
    cols = share + 2 * HEAD_SIZE
    half = KEY_VALUE_HEADS * HEAD_SIZE
    ff = outer_weight.shape[0]
    size = inner_weight.shape[0]

    start_low = tokens.reshape(rows, width)
    cot_low = cotangent.reshape(rows, width)

    route = routes.reshape(rows, 2)
    route_flat = route.reshape(rows * 2)
    picks = route_flat[:, None] == jnp.arange(experts, dtype=jnp.int32)[None, :]
    before = jnp.dot(
        jnp.tril(jnp.ones((rows * 2, rows * 2), low), -1),
        picks.astype(low),
        preferred_element_type=f32,
    )
    rank = jnp.sum(jnp.where(picks, before, 0.0), 1).astype(jnp.int32).reshape(rows, 2)
    route_lines = route.T
    slots = (route * capacity + rank).T
    slots_near = (jnp.bitwise_xor(route, index) * capacity + rank).T
    spots = jnp.arange(height, dtype=jnp.int32)[:, None]
    other_route = jnp.sum(
        jnp.where(slots[0:1] == spots, route_lines[1:2], 0)
        + jnp.where(slots[1:2] == spots, route_lines[0:1], 0),
        1,
    )

    by_head = jnp.concatenate(
        [
            query_weight.reshape(shard, count, share),
            key_value_weight[:, :half].reshape(shard, count, HEAD_SIZE),
            key_value_weight[:, half:].reshape(shard, count, HEAD_SIZE),
        ],
        2,
    )
    lanes = 128 * -(-(cols + 2 + experts) // 128)
    table_lane = lanes - 128
    router_lane = cols - table_lane
    first_lane, second_lane = router_lane + experts, router_lane + experts + 1
    extras = jnp.concatenate([router_weight, gain_before[:, None], gain_middle[:, None]], 1)
    extras = jnp.broadcast_to(extras[None], (count, shard, 2 + experts))
    head_block = jnp.concatenate([by_head.transpose(1, 0, 2), extras], 2)
    head_block = jnp.pad(head_block, ((0, 0), (0, 0), (0, lanes - cols - 2 - experts)))
    seg_line = jnp.broadcast_to(segment_ids.reshape(1, 1, rows), (count, 1, rows)).astype(low)
    seg_line = jnp.pad(seg_line, ((0, 0), (0, 0), (0, lanes - rows)))
    other_line = other_route.reshape(experts, 1, capacity).astype(low)
    other_line = jnp.pad(other_line, ((0, 0), (0, 14), (0, lanes - capacity)))
    head_block = jnp.concatenate([head_block, seg_line, other_line], 1)
    chip = index // 2
    tokens_all = gather(start_low, "fsdp")
    arrived = all_to_all(head_block)

    inner_own = inner_weight.reshape(size, 2 * ff)
    inner_x, inner_y = swap_near(inner_own, "dp", (1, 2))
    outer_x, outer_y = swap_near(outer_weight, "dp", (1, 2))
    arrived, inner_x, inner_y, outer_x, outer_y = after(
        (arrived, inner_x, inner_y, outer_x, outer_y)
    )
    segments = arrived[:, shard, :rows].reshape(length).astype(jnp.int32)
    other_expert = arrived[:, shard + 1, :capacity].reshape(height, 1).astype(jnp.int32)
    head_rows = arrived[:, :shard].reshape(count * shard, lanes)
    head_near = swap_near(head_rows, "dp", (1, 2, 3))
    head_weights = in_order([head_rows] + head_near, "dp").reshape(width, lanes)
    cot_sent = spread_rows(slots_near, cot_low, capacity, experts)

    by_head_line = by_head.reshape(shard, count * cols)
    tokens_all, cot_sent, head_weights, by_head_line, output_own = after(
        (tokens_all, cot_sent, head_weights, by_head_line, output_weight.T)
    )
    output_all = gather(output_own, ("dp", "fsdp"))
    normed, projected = project(tokens_all, head_weights, cols, first_lane, rows)
    cot_first = swap_near_blocks(cot_sent, (4, 6, 2))
    firsts = segments.reshape(count, rows)
    starts = jnp.sum(segments[None, :] < firsts[:, :1], 1) // rows
    wholes = (jnp.sum(segments[None, :] < firsts[:, -1:], 1) + rows - 1) // rows
    wholes = jnp.minimum(wholes, jnp.arange(count))
    spans = jnp.stack([starts, wholes]).astype(jnp.int32)
    seg_row, seg_col = segments.reshape(1, length), segments.reshape(length, 1)
    mixed_head, mixed_exact, totals = attend(spans, projected, seg_row, seg_col)
    mixed_head, cot_first, by_head_line = after((mixed_head, cot_first, by_head_line))
    project_line = gather(by_head_line, "fsdp")
    mixed = all_to_all(mixed_head).reshape(count * share, rows)

    middle, sent, gates = middle_part(
        start_low, mixed, output_all, head_weights, slots, route_lines,
        second_lane, router_lane, height,
    )

    rows_in = all_to_all(sent)
    inner_far = flip_exchange(after(inner_x, sent), "dp", 2)
    outer_far = flip_exchange(after(outer_y, sent), "dp", 1)
    rows_in, cot_sent, project_line, inner_far, outer_far = after(
        (rows_in, cot_sent, project_line, inner_far, outer_far)
    )
    inner_parts = [inner_own, inner_x, inner_y, inner_far]
    outer_parts = [outer_weight, outer_x, outer_y, outer_far]
    project_all = gather(project_line, "dp")
    cot_last = swap_near_blocks(cot_sent, (5, 7, 3, 1))
    own_expert = jnp.stack([index, group]).astype(jnp.int32)
    (pre_gate, pre_up, hidden, slot_gates), parts = expert_forward_pass(
        own_expert, rows_in, inner_parts, outer_parts, head_weights, other_expert,
        router_lane, 256, experts,
    )
    hidden, parts, cot_last = after((hidden, parts, cot_last))
    part_first = swap_near_blocks(parts, (4, 6, 2, 1, 3))
    cot_in = [cot_sent[0], cot_last[3], cot_first[2], cot_last[2]]
    cot_in = cot_in + [cot_first[0], cot_last[0], cot_first[1], cot_last[1]]
    grad_gate, grad_up, grad_in, grad_rows, router_part = expert_backward_pass(
        own_expert, cot_in, parts, rows_in, slot_gates, pre_gate, pre_up, inner_parts, outer_parts,
        head_weights, other_expert, router_lane, 512,
    )
    grad_rows, part_first, grad_gate, grad_up, grad_in = after(
        (grad_rows, part_first, grad_gate, grad_up, grad_in)
    )
    grad_home = all_to_all(grad_rows)

    def cut(value, k):
        return lax.dynamic_slice_in_dim(value, jnp.bitwise_xor(group, k) * size, size, 1)

    rows_near = [cut(rows_in, k) for k in range(4)]
    gate_terms = [contract(near, grad_gate, 0, 0).astype(low) for near in rows_near]
    up_terms = [contract(near, grad_up, 0, 0).astype(low) for near in rows_near]
    near_a, far_a = [flip_exchange(gate_terms[k], "dp", 1) for k in (1, 3)]
    near_b, far_b = [flip_exchange(up_terms[k], "dp", 2) for k in (2, 3)]
    passed_a = (gate_terms[2].astype(f32) + far_a.astype(f32)).astype(low)
    passed_b = (up_terms[1].astype(f32) + far_b.astype(f32)).astype(low)
    outer_term = jnp.concatenate(
        [contract(hidden, grad_in[:, k * size : (k + 1) * size], 0, 0) for k in range(4)]
    ).astype(low)
    grad_home, outer_term, passed_a, passed_b, gate_terms, up_terms, near_a, near_b, project_all = after(
        (
            grad_home, outer_term, passed_a, passed_b, gate_terms, up_terms, near_a, near_b,
            project_all,
        )
    )
    side_a, side_b = flip_exchange(passed_a, "dp", 2), flip_exchange(passed_b, "dp", 1)

    grad_middle, grad_branch, gain_part, mixed_grad = back_part(
        middle, cot_low, grad_home, output_all, head_weights, slots, second_lane
    )
    mixed_grad = all_to_all(mixed_grad.reshape(count, share, rows))

    branch_near = jnp.concatenate([cut(grad_branch, k) for k in range(4)], 1)
    half_width = width // 2

    def half_terms(side):
        heads = lax.dynamic_slice_in_dim(mixed, side * half_width, half_width, 0)
        return contract(branch_near, heads, 0, 1).astype(low)

    from_core = flip_exchange(half_terms(1 - core), "fsdp", 1)
    output_part = half_terms(core).astype(f32) + from_core.astype(f32)
    output_part = output_part.astype(low).reshape(4, size, half_width)
    mixed_grad, output_part, parts, side_a, side_b, outer_term = after(
        (mixed_grad, output_part, parts, side_a, side_b, outer_term)
    )
    outer_sum = lax.psum_scatter(outer_term, "dp", scatter_dimension=0, tiled=True)
    output_near = flip_exchange(output_part[2:], "dp", 2)
    part_last = swap_near_blocks(parts, (5, 7))

    grads_blocks, grads_line = attend_backward(
        spans, projected, mixed_grad, seg_row, seg_col, mixed_exact, totals
    )
    grads_blocks, grads_line, output_part, output_near, part_last = after(
        (grads_blocks, grads_line, output_part, output_near, part_last)
    )
    part_home = [parts[0], part_first[3], part_first[2], part_first[4]]
    part_home = part_home + [part_first[0], part_last[0], part_first[1], part_last[1]]
    grad_mine = all_to_all(grads_blocks).reshape(count * cols, rows)
    extra = jnp.concatenate(
        [router_part[router_lane : router_lane + experts], gain_part,
         jnp.zeros((lanes - cols - experts - 1, width), f32)]
    )
    output_sum = output_part[:2].astype(f32) + output_near.astype(f32)
    output_passed = output_sum[1].astype(low)
    output_side = flip_exchange(output_passed, "dp", 1)
    grads_line = after(grads_line, output_passed)
    own_group = group.reshape(1).astype(jnp.int32)
    terms = weight_terms(own_group, normed, grads_line, extra, 4)
    weight_sum = terms[0].astype(f32)
    for k in range(1, 4):
        weight_sum = weight_sum + flip_exchange(terms[k], "dp", k).astype(f32)
    block_out = mixture(slots_near, gates, middle, part_home)
    inner_grad = sum_pairs(
        [gate_terms[0], near_a, side_a], [up_terms[0], near_b, side_b], size // 4
    )
    outer_grad = outer_sum.astype(f32)
    grad_normed = contract(
        after(grad_mine, inner_grad, outer_grad, block_out), project_all, 0, 1
    )
    output_sum = output_sum[0] + output_side.astype(f32)
    weight_sum = after(weight_sum.astype(low), grad_mine)
    weight_home = all_to_all(weight_sum.reshape(count, shard, lanes))
    chips, pair = count // 2, 2 * shard
    output_low = output_sum.astype(low)

    def line_part(value, k):
        at = jnp.bitwise_xor(index // 2, k) * pair
        return lax.dynamic_slice_in_dim(value, at, pair, 0)

    output_line = [
        flip_exchange(line_part(output_low, k), "fsdp", 2 * k) for k in range(1, chips)
    ]
    output_line, weight_home = after((output_line, weight_home), block_out, outer_grad)
    query_grad, keyval_grad, router_grad, gains = weight_grads(
        weight_home, query_weight, key_value_weight, gain_before[:, None], share, experts
    )
    before_grad, middle_grad = gains[:, 0], gains[:, 1]
    output_grad = line_part(output_sum, 0)
    for near in output_line:
        output_grad = output_grad + near.astype(f32)
    own_half = lax.dynamic_slice_in_dim(output_grad, core * shard, shard, 0)
    other_half = flip_exchange(
        lax.dynamic_slice_in_dim(output_grad, (1 - core) * shard, shard, 0), "fsdp", 1
    )
    output_grad = jnp.where(
        core == 0,
        jnp.concatenate([own_half, other_half], 1),
        jnp.concatenate([other_half, own_half], 1),
    ).T
    gain_first = head_weights[:, table_lane + first_lane]
    _, unit_first, factor_first = normalize(start_low.astype(f32), gain_first)
    outer_back, _ = normalize_back(grad_normed, unit_first, factor_first, gain_first)
    tokens_grad = grad_middle + outer_back
    return (
        block_out[None],
        tokens_grad[None],
        query_grad,
        keyval_grad,
        output_grad,
        router_grad,
        before_grad,
        middle_grad,
        inner_grad,
        outer_grad,
    )


def solution(mesh):
    by_heads = (mesh.shape["dp"], mesh.shape["fsdp"]) == (4, KEY_VALUE_HEADS)
    in_specs = (
        P("dp", "fsdp", None),
        P("dp", "fsdp"),
        P("dp", "fsdp", None),
        P(("dp", "fsdp"), None),
        P(("dp", "fsdp"), None),
        P(None, ("dp", "fsdp")),
        P(("dp", "fsdp"), None),
        P(("dp", "fsdp")),
        P(("dp", "fsdp")),
        P("dp", None, "fsdp"),
        P("fsdp", "dp"),
        P("dp", "fsdp", None),
    )
    out_specs = (
        P("dp", "fsdp", None),
        P("dp", "fsdp", None),
        P(("dp", "fsdp"), None),
        P(("dp", "fsdp"), None),
        P(None, ("dp", "fsdp")),
        P(("dp", "fsdp"), None),
        P(("dp", "fsdp")),
        P(("dp", "fsdp")),
        P("dp", None, "fsdp"),
        P("fsdp", "dp"),
    )
    return jax.shard_map(
        per_device_heads if by_heads else per_device, mesh=mesh, in_specs=in_specs, out_specs=out_specs, check_vma=False
    )
```

```python
import functools

import jax
import jax.numpy as jnp
from jax import lax
from jax.experimental import pallas as pl
from jax.experimental.pallas import tpu as pltpu
from jax.sharding import PartitionSpec as P

QUERY_HEADS = 24
KEY_VALUE_HEADS = 8
HEAD_SIZE = 64


HIGHEST_PRECISION = lax.Precision.HIGHEST
EPSILON = 1e-05
NEGATIVE_LARGE = -1e30


def normalize(hidden, gain_vec):
    factor = lax.rsqrt(jnp.mean(hidden * hidden, -1, keepdims=True) + EPSILON)
    unit_rows = hidden * factor
    return (unit_rows * gain_vec.astype(jnp.float32), unit_rows, factor)


def normalize_back(grad_rows, unit_rows, factor, gain_vec):
    scaled = grad_rows * gain_vec.astype(jnp.float32)
    inner_part = factor * (scaled - unit_rows * jnp.mean(scaled * unit_rows, -1, keepdims=True))
    return (inner_part, jnp.sum(grad_rows * unit_rows, 0))


def split_block(gathered, offset, key_tile_block):
    sequence_count = gathered.shape[0]
    portion_rows = lax.slice_in_dim(gathered, offset, offset + key_tile_block, axis=1)
    half_columns = KEY_VALUE_HEADS * HEAD_SIZE
    key_portion = portion_rows[..., :half_columns].reshape(
        sequence_count, key_tile_block, KEY_VALUE_HEADS, HEAD_SIZE
    )
    value_portion = portion_rows[..., half_columns:].reshape(
        sequence_count, key_tile_block, KEY_VALUE_HEADS, HEAD_SIZE
    )
    return (key_portion, value_portion)


def block_scores(query_matrix, key_portion, allowed):
    raw_scores = jnp.einsum(
        "sikgd,sjkd->skgij", query_matrix, key_portion, preferred_element_type=jnp.float32
    ) * HEAD_SIZE ** (-0.5)
    return jnp.where(allowed[:, None, None], raw_scores, NEGATIVE_LARGE)


def mask_for(seg_all, seg_mine, positions, offset, key_tile_block):
    key_seg = lax.slice_in_dim(seg_all, offset, offset + key_tile_block, axis=1)
    key_spots = offset + jnp.arange(key_tile_block, dtype=jnp.int32)
    same_doc = seg_mine[:, :, None] == key_seg[:, None, :]
    causal = key_spots[None, None, :] <= positions[None, :, None]
    return same_doc & causal


def log_totals(query_matrix, gathered, block_masks, key_tile_block):
    sequence_count, resident_rows = (query_matrix.shape[0], query_matrix.shape[1])
    running_totals = jnp.full(
        (sequence_count, KEY_VALUE_HEADS, QUERY_HEADS // KEY_VALUE_HEADS, resident_rows),
        NEGATIVE_LARGE,
        jnp.float32,
    )
    for block_index, allowed in enumerate(block_masks):
        key_portion, value_portion = split_block(
            gathered, block_index * key_tile_block, key_tile_block
        )

        def log_live(present_value, key_portion=key_portion, allowed=allowed):
            scores = block_scores(query_matrix, key_portion, allowed)
            return jnp.logaddexp(present_value, jax.nn.logsumexp(scores, -1))

        running_totals = lax.cond(
            jnp.any(allowed), log_live, lambda present_value: present_value, running_totals
        )
    return running_totals


def attend_values(query_matrix, gathered, block_masks, key_tile_block, running_totals):
    result = jnp.zeros(query_matrix.shape, jnp.float32)
    for block_index, allowed in enumerate(block_masks):
        key_portion, value_portion = split_block(
            gathered, block_index * key_tile_block, key_tile_block
        )

        def attend_live(
            present_value, key_portion=key_portion, value_portion=value_portion, allowed=allowed
        ):
            probs = jnp.exp(
                block_scores(query_matrix, key_portion, allowed) - running_totals[..., None]
            ).astype(jnp.bfloat16)
            return present_value + jnp.einsum(
                "skgij,sjkd->sikgd", probs, value_portion, preferred_element_type=jnp.float32
            )

        result = lax.cond(
            jnp.any(allowed), attend_live, lambda present_value: present_value, result
        )
    token_count = query_matrix.shape[0] * query_matrix.shape[1]
    return result.reshape(token_count, -1).astype(jnp.bfloat16)


def attend_back(
    query_matrix, mixed_gradient, gathered, block_masks, key_tile_block, running_totals
):
    sequence_count = query_matrix.shape[0]
    delta = jnp.zeros(running_totals.shape, jnp.float32)
    for block_index, allowed in enumerate(block_masks):
        key_portion, value_portion = split_block(
            gathered, block_index * key_tile_block, key_tile_block
        )

        def live_delta(
            present_value, key_portion=key_portion, value_portion=value_portion, allowed=allowed
        ):
            probs = jnp.exp(
                block_scores(query_matrix, key_portion, allowed) - running_totals[..., None]
            )
            grad_probs = jnp.einsum(
                "sikgd,sjkd->skgij",
                mixed_gradient,
                value_portion,
                preferred_element_type=jnp.float32,
            )
            return present_value + jnp.sum(probs * grad_probs, -1)

        delta = lax.cond(jnp.any(allowed), live_delta, lambda present_value: present_value, delta)
    grad_queries = jnp.zeros(query_matrix.shape, jnp.float32)
    key_terms = []
    for block_index, allowed in enumerate(block_masks):
        key_portion, value_portion = split_block(
            gathered, block_index * key_tile_block, key_tile_block
        )

        def live_grad(
            present_value, key_portion=key_portion, value_portion=value_portion, allowed=allowed
        ):
            probs = jnp.exp(
                block_scores(query_matrix, key_portion, allowed) - running_totals[..., None]
            )
            grad_probs = jnp.einsum(
                "sikgd,sjkd->skgij",
                mixed_gradient,
                value_portion,
                preferred_element_type=jnp.float32,
            )
            grad_scores = (probs * (grad_probs - delta[..., None])).astype(jnp.bfloat16)
            updated = present_value + jnp.einsum(
                "skgij,sjkd->sikgd", grad_scores, key_portion, preferred_element_type=jnp.float32
            ) * HEAD_SIZE ** (-0.5)
            grad_keys = jnp.einsum(
                "skgij,sikgd->sjkd", grad_scores, query_matrix, preferred_element_type=jnp.float32
            ) * HEAD_SIZE ** (-0.5)
            grad_values = jnp.einsum(
                "skgij,sikgd->sjkd",
                probs.astype(jnp.bfloat16),
                mixed_gradient,
                preferred_element_type=jnp.float32,
            )
            both_parts = jnp.concatenate(
                [
                    grad_keys.reshape(sequence_count, key_tile_block, -1),
                    grad_values.reshape(sequence_count, key_tile_block, -1),
                ],
                -1,
            )
            return (updated, both_parts)

        def dead_grad(present_value):
            return (
                present_value,
                jnp.zeros(
                    (sequence_count, key_tile_block, 2 * KEY_VALUE_HEADS * HEAD_SIZE), jnp.float32
                ),
            )

        grad_queries, block_term = lax.cond(jnp.any(allowed), live_grad, dead_grad, grad_queries)
        key_terms.append(block_term)
    return (grad_queries, jnp.concatenate(key_terms, 1), delta)


def expert_forward(inner_use, outer_use, received):
    model_width = received.shape[-1]
    rows_in = received.reshape(-1, model_width)
    pre_rows = jnp.dot(rows_in, inner_use, preferred_element_type=jnp.float32)
    slab_width = outer_use.shape[0]
    hidden_rows = (jax.nn.silu(pre_rows[:, :slab_width]) * pre_rows[:, slab_width:]).astype(
        jnp.bfloat16
    )
    part_rows = jnp.dot(hidden_rows, outer_use, preferred_element_type=jnp.float32).astype(
        jnp.bfloat16
    )
    return part_rows.reshape(received.shape)


def expert_back(inner_use, outer_use, rows_flat, grad_flat):
    pre_rows = jnp.dot(rows_flat, inner_use, preferred_element_type=jnp.float32)
    slab_width = outer_use.shape[0]
    gate_pre = pre_rows[:, :slab_width]
    up_pre = pre_rows[:, slab_width:]
    sigma = jax.nn.sigmoid(gate_pre)
    swish = gate_pre * sigma
    hidden_rows = (swish * up_pre).astype(jnp.bfloat16)
    grad_hidden = jnp.dot(grad_flat, outer_use.T, preferred_element_type=jnp.float32)
    grad_gate = grad_hidden * up_pre * sigma * (1.0 + gate_pre * (1.0 - sigma))
    grad_up = grad_hidden * swish
    grad_pre = jnp.concatenate([grad_gate, grad_up], 1).astype(jnp.bfloat16)
    grad_in = jnp.dot(grad_pre, inner_use.T, preferred_element_type=jnp.float32).astype(
        jnp.bfloat16
    )
    return (hidden_rows, grad_pre, grad_in)


def per_device(
    tokens,
    segment_ids,
    routes,
    query_weight,
    key_value_weight,
    output_weight,
    router_weight,
    gain_before,
    gain_middle,
    inner_weight,
    outer_weight,
    cotangent,
):
    sequence_count, resident_rows, model_width = tokens.shape
    token_count = sequence_count * resident_rows
    experts = router_weight.shape[1]
    copies = lax.axis_size("fsdp") // experts
    capacity = 3 * token_count // 8
    seg_all = lax.all_gather(segment_ids, "fsdp", axis=1, tiled=True)
    seq_length = seg_all.shape[1]
    key_tile_block = min(256, seq_length)
    positions = lax.axis_index("fsdp") * resident_rows + jnp.arange(resident_rows, dtype=jnp.int32)
    block_masks = [
        mask_for(seg_all, segment_ids, positions, offset, key_tile_block)
        for offset in range(0, seq_length, key_tile_block)
    ]
    start_rows = tokens.reshape(token_count, model_width).astype(jnp.float32)
    route_flat = routes.reshape(token_count * 2)
    picks = route_flat[:, None] == jnp.arange(experts, dtype=jnp.int32)[None, :]
    marks = picks.astype(jnp.int32)
    slot_index = route_flat * capacity + jnp.sum((jnp.cumsum(marks, 0) - marks) * marks, 1)
    chosen_mask = picks.reshape(token_count, 2, experts)

    def layer_weights():
        return (
            lax.all_gather(query_weight, ("dp", "fsdp"), axis=0, tiled=True),
            lax.all_gather(key_value_weight, ("dp", "fsdp"), axis=0, tiled=True),
            lax.all_gather(output_weight, ("dp", "fsdp"), axis=1, tiled=True),
            lax.all_gather(router_weight, ("dp", "fsdp"), axis=0, tiled=True),
            lax.all_gather(gain_before, ("dp", "fsdp"), axis=0, tiled=True),
            lax.all_gather(gain_middle, ("dp", "fsdp"), axis=0, tiled=True),
        )

    def expert_weights():
        inner_full, outer_full = (
            lax.all_gather(inner_weight, "dp", axis=0, tiled=True),
            lax.all_gather(outer_weight, "dp", axis=1, tiled=True),
        )
        return (inner_full.reshape(model_width, -1), outer_full)

    def attention_front(weights):
        normed, unit_rows, factor = normalize(start_rows, weights[4])
        normed_low = normed.astype(jnp.bfloat16)
        query_matrix = jnp.dot(normed_low, weights[0], preferred_element_type=jnp.float32).astype(
            jnp.bfloat16
        )
        query_matrix = query_matrix.reshape(
            sequence_count,
            resident_rows,
            KEY_VALUE_HEADS,
            QUERY_HEADS // KEY_VALUE_HEADS,
            HEAD_SIZE,
        )
        key_value_rows = jnp.dot(normed_low, weights[1], preferred_element_type=jnp.float32).astype(
            jnp.bfloat16
        )
        gathered = lax.all_gather(
            key_value_rows.reshape(sequence_count, resident_rows, -1), "fsdp", axis=1, tiled=True
        )
        return (normed_low, unit_rows, factor, query_matrix, gathered)

    def middle_part(weights, mixed_low):
        middle = start_rows + jnp.dot(mixed_low, weights[2], preferred_element_type=jnp.float32)
        expert_in, unit_rows, factor = normalize(middle, weights[5])
        expert_low = expert_in.astype(jnp.bfloat16)
        logits = jnp.dot(
            expert_low.astype(jnp.float32),
            weights[3].astype(jnp.float32),
            precision=HIGHEST_PRECISION,
        )
        return (middle, unit_rows, factor, expert_low, logits)

    def gates_for(logits):
        chosen_logits = jnp.sum(jnp.where(chosen_mask, logits[:, None, :], 0.0), -1)
        return jax.nn.softmax(chosen_logits, -1)

    def to_slots(pair_rows):
        packed = (
            jnp.zeros((experts * capacity, model_width), pair_rows.dtype)
            .at[slot_index]
            .set(pair_rows)
        )
        return jnp.repeat(packed.reshape(experts, capacity, model_width), copies, axis=0)

    def from_slots(returned_rows):
        summed = jnp.sum(
            returned_rows.reshape(experts, copies, capacity, model_width).astype(jnp.float32), 1
        )
        return summed.reshape(experts * capacity, model_width)[slot_index]

    weights = layer_weights()
    inner_all, outer_all = expert_weights()
    normed_low, unit_first, factor_first, query_matrix, gathered = attention_front(weights)
    running_totals = log_totals(query_matrix, gathered, block_masks, key_tile_block)
    mixed_low = attend_values(query_matrix, gathered, block_masks, key_tile_block, running_totals)
    middle, unit_second, factor_second, expert_low, logits = middle_part(weights, mixed_low)
    gates = gates_for(logits)
    sent = to_slots(jnp.repeat(expert_low, 2, axis=0))
    part_rows = expert_forward(
        inner_all, outer_all, lax.all_to_all(sent, "fsdp", split_axis=0, concat_axis=0, tiled=True)
    )
    returned_part = lax.all_to_all(part_rows, "fsdp", split_axis=0, concat_axis=0, tiled=True)
    returned_rows = returned_part
    expert_sum = from_slots(returned_rows).reshape(token_count, 2, model_width)
    block_out = (middle + jnp.sum(gates[..., None] * expert_sum, 1)).astype(jnp.bfloat16)
    grad_out = cotangent.reshape(token_count, model_width).astype(jnp.float32)
    weights = layer_weights()
    inner_use, outer_use = expert_weights()
    normed_low, unit_first, factor_first, query_matrix, gathered = attention_front(weights)
    mixed_low = attend_values(query_matrix, gathered, block_masks, key_tile_block, running_totals)
    middle, unit_second, factor_second, expert_low, logits = middle_part(weights, mixed_low)
    gates = gates_for(logits)
    sent = to_slots(jnp.repeat(expert_low, 2, axis=0))
    grad_sent = to_slots(
        (gates[..., None] * grad_out[:, None, :])
        .astype(jnp.bfloat16)
        .reshape(2 * token_count, model_width)
    )
    rows_in = lax.all_to_all(sent, "fsdp", split_axis=0, concat_axis=0, tiled=True)
    rows_grad = lax.all_to_all(grad_sent, "fsdp", split_axis=0, concat_axis=0, tiled=True)
    row_shape = rows_in.shape
    hidden_flat, grad_pre_flat, grad_in_flat = expert_back(
        inner_use, outer_use, rows_in.reshape(-1, model_width), rows_grad.reshape(-1, model_width)
    )
    part_rows = jnp.dot(hidden_flat, outer_use, preferred_element_type=jnp.float32).astype(
        jnp.bfloat16
    )
    grad_home = lax.all_to_all(
        grad_in_flat.reshape(row_shape), "fsdp", split_axis=0, concat_axis=0, tiled=True
    )
    part_home = lax.all_to_all(
        part_rows.reshape(row_shape), "fsdp", split_axis=0, concat_axis=0, tiled=True
    )
    item_shape = row_shape[:2]
    grad_pre = grad_pre_flat.reshape(item_shape + (-1,))
    hidden_rows = hidden_flat.reshape(item_shape + (-1,))
    expert_sum = from_slots(part_home).reshape(token_count, 2, model_width)
    rows_flat = rows_in.reshape(-1, model_width)
    row_total = rows_flat.shape[0]
    inner_grad_all = jnp.dot(
        rows_flat.T, grad_pre.reshape(row_total, -1), preferred_element_type=jnp.float32
    )
    outer_grad_all = jnp.dot(
        hidden_rows.reshape(row_total, -1).T,
        rows_grad.reshape(row_total, model_width),
        preferred_element_type=jnp.float32,
    )
    inner_grad, outer_grad = (
        lax.psum_scatter(
            inner_grad_all.reshape(model_width, 2, -1).astype(jnp.bfloat16),
            "dp",
            scatter_dimension=0,
            tiled=True,
        ).astype(jnp.float32),
        lax.psum_scatter(
            outer_grad_all.astype(jnp.bfloat16), "dp", scatter_dimension=1, tiled=True
        ).astype(jnp.float32),
    )
    grad_gates = jnp.sum(grad_out[:, None, :] * expert_sum, -1)
    grad_choice = gates * (grad_gates - jnp.sum(gates * grad_gates, -1, keepdims=True))
    grad_logits = jnp.sum(jnp.where(chosen_mask, grad_choice[..., None], 0.0), 1)
    router_grad_all = jnp.dot(
        expert_low.astype(jnp.float32).T, grad_logits, precision=HIGHEST_PRECISION
    )
    grad_expert_in = jnp.sum(from_slots(grad_home).reshape(token_count, 2, model_width), 1)
    grad_expert_in = grad_expert_in + jnp.dot(
        grad_logits, weights[3].astype(jnp.float32).T, precision=HIGHEST_PRECISION
    )
    grad_norm_second, middle_gain_grad = normalize_back(
        grad_expert_in, unit_second, factor_second, weights[5]
    )
    grad_middle = grad_out + grad_norm_second
    grad_branch = grad_middle.astype(jnp.bfloat16)
    output_grad_all = jnp.dot(mixed_low.T, grad_branch, preferred_element_type=jnp.float32)
    mixed_gradient = jnp.dot(grad_branch, weights[2].T, preferred_element_type=jnp.float32).astype(
        jnp.bfloat16
    )
    mixed_gradient = mixed_gradient.reshape(
        sequence_count, resident_rows, KEY_VALUE_HEADS, QUERY_HEADS // KEY_VALUE_HEADS, HEAD_SIZE
    )
    grad_queries, key_terms, delta = attend_back(
        query_matrix, mixed_gradient, gathered, block_masks, key_tile_block, running_totals
    )
    key_grads = lax.psum_scatter(
        key_terms.astype(jnp.bfloat16), "fsdp", scatter_dimension=1, tiled=True
    ).reshape(token_count, -1)
    query_low = grad_queries.reshape(token_count, -1).astype(jnp.bfloat16)
    grad_normed = jnp.dot(query_low, weights[0].T, preferred_element_type=jnp.float32) + jnp.dot(
        key_grads, weights[1].T, preferred_element_type=jnp.float32
    )
    query_grad_all = jnp.dot(normed_low.T, query_low, preferred_element_type=jnp.float32)
    keyval_grad_all = jnp.dot(normed_low.T, key_grads, preferred_element_type=jnp.float32)
    grad_norm_first, before_gain_grad = normalize_back(
        grad_normed, unit_first, factor_first, weights[4]
    )
    tokens_grad = grad_middle + grad_norm_first
    summed_grads = (
        lax.psum_scatter(query_grad_all, ("dp", "fsdp"), scatter_dimension=0, tiled=True),
        lax.psum_scatter(keyval_grad_all, ("dp", "fsdp"), scatter_dimension=0, tiled=True),
        lax.psum_scatter(output_grad_all, ("dp", "fsdp"), scatter_dimension=1, tiled=True),
        lax.psum_scatter(router_grad_all, ("dp", "fsdp"), scatter_dimension=0, tiled=True),
        lax.psum_scatter(before_gain_grad, ("dp", "fsdp"), scatter_dimension=0, tiled=True),
        lax.psum_scatter(middle_gain_grad, ("dp", "fsdp"), scatter_dimension=0, tiled=True),
    )
    return (
        block_out.reshape(sequence_count, resident_rows, model_width),
        tokens_grad.reshape(sequence_count, resident_rows, model_width),
        summed_grads[0],
        summed_grads[1],
        summed_grads[2],
        summed_grads[3],
        summed_grads[4],
        summed_grads[5],
        inner_grad,
        outer_grad,
    )


def contract(left, right, left_axis, right_axis):
    return lax.dot_general(
        left, right, (((left_axis,), (right_axis,)), ((), ())), preferred_element_type=jnp.float32
    )


def unit_of(rows):
    factor = lax.rsqrt(jnp.mean(rows * rows, -1, keepdims=True) + EPSILON)
    return (rows * factor, factor)


def column_as_row(table, lane):
    pick = (lax.broadcasted_iota(jnp.int32, (8, table.shape[1]), 1) == lane).astype(jnp.bfloat16)
    return contract(pick, table, 1, 1)[:1]


def split_low(value):
    high = value.astype(jnp.bfloat16)
    return (high, (value - high.astype(jnp.float32)).astype(jnp.bfloat16))


def project_kernel(lane, rows_ref, weight_ref, table_ref, normed_ref, heads_ref, gain):
    @pl.when(pl.program_id(0) == 0)
    def _():
        gain[...] = column_as_row(table_ref[...], lane)

    unit, _ = unit_of(rows_ref[...].astype(jnp.float32))
    normed = (unit * gain[...]).astype(jnp.bfloat16)
    normed_ref[...] = normed
    heads = jnp.dot(normed, weight_ref[...], preferred_element_type=jnp.float32)
    heads_ref[0] = heads.T[: heads_ref.shape[1]].astype(jnp.bfloat16)


def project(rows, head_weights, wide, lane, block):
    length, width = rows.shape
    lanes = head_weights.shape[1]
    blocks = length // block
    return pl.pallas_call(
        functools.partial(project_kernel, lane),
        grid=(blocks,),
        in_specs=[
            pl.BlockSpec((block, width), lambda i: (i, 0)),
            pl.BlockSpec((width, lanes), lambda i: (0, 0)),
            pl.BlockSpec((width, 128), lambda i: (0, lanes // 128 - 1)),
        ],
        out_specs=[
            pl.BlockSpec((block, width), lambda i: (i, 0)),
            pl.BlockSpec((1, wide, block), lambda i: (i, 0, 0)),
        ],
        out_shape=[
            jax.ShapeDtypeStruct((length, width), jnp.bfloat16),
            jax.ShapeDtypeStruct((blocks, wide, block), jnp.bfloat16),
        ],
        scratch_shapes=[pltpu.VMEM((1, width), jnp.float32)],
        compiler_params=pltpu.CompilerParams(vmem_limit_bytes=60 * 2**20),
        name="project",
    )(rows, head_weights, head_weights)


def beside(rows, block, heads):
    return jnp.concatenate([rows[h * HEAD_SIZE : (h + 1) * HEAD_SIZE] for h in range(heads)], 1)


def attend_kernel(spans, q_ref, heads_ref, segr_ref, segc_ref, low_ref, mixed_ref, totals_ref):
    step = pl.program_id(0)
    block = q_ref.shape[2]
    heads = QUERY_HEADS // KEY_VALUE_HEADS
    share = heads * HEAD_SIZE
    queries = beside(q_ref[0, :share, :] * jnp.bfloat16(HEAD_SIZE ** (-0.5)), block, heads)
    seg_row = segr_ref[...]

    def scores_of(j):
        return contract(heads_ref[j, share : share + HEAD_SIZE, :], queries, 0, 0)

    def same_doc(j):
        return segc_ref[pl.ds(pl.multiple_of(j * block, block), block), :] == seg_row

    def fold(j, scores, carry):
        top, total, out = carry
        values = heads_ref[j, share + HEAD_SIZE : share + 2 * HEAD_SIZE, :]
        new_top = jnp.maximum(top, jnp.max(scores, 0, keepdims=True))
        probs = jnp.exp(scores - new_top)
        decay = jnp.exp(top - new_top)
        total = total * decay + jnp.sum(probs, 0, keepdims=True)
        out = out * decay + jnp.dot(
            values, probs.astype(jnp.bfloat16), preferred_element_type=jnp.float32
        )
        return (new_top, total, out)

    def masked(j, carry):
        allowed = jnp.concatenate([same_doc(j)] * heads, 1)
        return fold(j, jnp.where(allowed, scores_of(j), NEGATIVE_LARGE), carry)

    columns = heads * block
    carry = (
        jnp.full((1, columns), NEGATIVE_LARGE, jnp.float32),
        jnp.zeros((1, columns), jnp.float32),
        jnp.zeros((HEAD_SIZE, columns), jnp.float32),
    )
    first, full = spans[0, step], spans[1, step]
    carry = lax.fori_loop(first, full, masked, carry)
    carry = lax.fori_loop(full, step, lambda j, kept: fold(j, scores_of(j), kept), carry)
    key_spot = lax.broadcasted_iota(jnp.int32, (block, block), 0)
    query_spot = lax.broadcasted_iota(jnp.int32, (block, block), 1)
    allowed = same_doc(step) & (key_spot <= query_spot)
    allowed = jnp.concatenate([allowed] * heads, 1)
    top, total, out = fold(step, jnp.where(allowed, scores_of(step), NEGATIVE_LARGE), carry)
    out = out / total
    totals = top + jnp.log(total)
    for h in range(heads):
        part = out[:, h * block : (h + 1) * block]
        mixed_ref[0, h * HEAD_SIZE : (h + 1) * HEAD_SIZE, :] = part
        low_ref[0, h * HEAD_SIZE : (h + 1) * HEAD_SIZE, :] = part.astype(jnp.bfloat16)
        totals_ref[0, h : h + 1, :] = totals[:, h * block : (h + 1) * block]


def attend(spans, projected, seg_row, seg_col):
    blocks, wide, block = projected.shape
    share = wide - 2 * HEAD_SIZE
    length = blocks * block
    each = lambda height: pl.BlockSpec((1, height, block), lambda i, spans: (i, 0, 0))
    return pl.pallas_call(
        attend_kernel,
        grid_spec=pltpu.PrefetchScalarGridSpec(
            num_scalar_prefetch=1,
            grid=(blocks,),
            in_specs=[
                pl.BlockSpec((1, wide, block), lambda i, spans: (i, 0, 0)),
                pl.BlockSpec((blocks, wide, block), lambda i, spans: (0, 0, 0)),
                pl.BlockSpec((1, block), lambda i, spans: (0, i)),
                pl.BlockSpec((length, 1), lambda i, spans: (0, 0)),
            ],
            out_specs=[each(share), each(share), each(8)],
        ),
        out_shape=[
            jax.ShapeDtypeStruct((blocks, share, block), jnp.bfloat16),
            jax.ShapeDtypeStruct((blocks, share, block), jnp.float32),
            jax.ShapeDtypeStruct((blocks, 8, block), jnp.float32),
        ],
        compiler_params=pltpu.CompilerParams(vmem_limit_bytes=40 * 2**20),
        name="attend",
    )(spans, projected, projected, seg_row, seg_col)


def attend_back_kernel(
    spans, q_ref, g_ref, heads_ref, segr_ref, segc_ref, mixed_ref, totals_ref,
    blocks_ref, line_ref, dk_sum, dv_sum,
):
    step = pl.program_id(0)
    blocks, _, block = heads_ref.shape
    heads = QUERY_HEADS // KEY_VALUE_HEADS
    share = heads * HEAD_SIZE
    queries = beside(q_ref[0, :share, :] * jnp.bfloat16(HEAD_SIZE ** (-0.5)), block, heads)
    grads = beside(g_ref[0], block, heads)
    delta = jnp.sum(
        grads.astype(jnp.float32) * beside(mixed_ref[0], block, heads), 0, keepdims=True
    )
    totals = jnp.concatenate([totals_ref[0, h : h + 1, :] for h in range(heads)], 1)
    seg_row = segr_ref[...]

    @pl.when(step == 0)
    def _():
        dk_sum[...] = jnp.zeros_like(dk_sum)
        dv_sum[...] = jnp.zeros_like(dv_sum)

    def turn(j, query_sum, allowed):
        keys = heads_ref[j, share : share + HEAD_SIZE, :]
        values = heads_ref[j, share + HEAD_SIZE : share + 2 * HEAD_SIZE, :]
        probs = jnp.exp(contract(keys, queries, 0, 0) - totals)
        if allowed is not None:
            probs = jnp.where(jnp.concatenate([allowed] * heads, 1), probs, 0.0)
        grad_scores = (probs * (contract(values, grads, 0, 0) - delta)).astype(jnp.bfloat16)
        dv_sum[j] += contract(grads, probs.astype(jnp.bfloat16), 1, 1)
        dk_sum[j] += contract(queries, grad_scores, 1, 1)
        return query_sum + jnp.dot(keys, grad_scores, preferred_element_type=jnp.float32)

    def same_doc(j):
        return segc_ref[pl.ds(pl.multiple_of(j * block, block), block), :] == seg_row

    query_sum = jnp.zeros((HEAD_SIZE, heads * block), jnp.float32)
    first, full = spans[0, step], spans[1, step]
    query_sum = lax.fori_loop(first, full, lambda j, c: turn(j, c, same_doc(j)), query_sum)
    query_sum = lax.fori_loop(full, step, lambda j, c: turn(j, c, None), query_sum)
    key_spot = lax.broadcasted_iota(jnp.int32, (block, block), 0)
    query_spot = lax.broadcasted_iota(jnp.int32, (block, block), 1)
    query_sum = turn(step, query_sum, same_doc(step) & (key_spot <= query_spot))
    query_sum = (query_sum * HEAD_SIZE ** (-0.5)).astype(jnp.bfloat16)

    def spread(j, at, size, value):
        blocks_ref[j, at : at + size, :] = value
        there = pl.ds(pl.multiple_of(j * block, block), block)
        line_ref[at : at + size, there] = value

    for h in range(heads):
        spread(step, h * HEAD_SIZE, HEAD_SIZE, query_sum[:, h * block : (h + 1) * block])

    @pl.when(step == pl.num_programs(0) - 1)
    def _():
        for j in range(blocks):
            spread(j, share, HEAD_SIZE, dk_sum[j].astype(jnp.bfloat16))
            spread(j, share + HEAD_SIZE, HEAD_SIZE, dv_sum[j].astype(jnp.bfloat16))


def attend_backward(spans, projected, grads, seg_row, seg_col, mixed, totals):
    blocks, wide, block = projected.shape
    share = wide - 2 * HEAD_SIZE
    length = blocks * block
    each = lambda height: pl.BlockSpec((1, height, block), lambda i, spans: (i, 0, 0))
    return pl.pallas_call(
        attend_back_kernel,
        grid_spec=pltpu.PrefetchScalarGridSpec(
            num_scalar_prefetch=1,
            grid=(blocks,),
            in_specs=[
                pl.BlockSpec((1, wide, block), lambda i, spans: (i, 0, 0)),
                each(share),
                pl.BlockSpec((blocks, wide, block), lambda i, spans: (0, 0, 0)),
                pl.BlockSpec((1, block), lambda i, spans: (0, i)),
                pl.BlockSpec((length, 1), lambda i, spans: (0, 0)),
                each(share),
                each(8),
            ],
            out_specs=[
                pl.BlockSpec((blocks, wide, block), lambda i, spans: (0, 0, 0)),
                pl.BlockSpec((wide, length), lambda i, spans: (0, 0)),
            ],
            scratch_shapes=[
                pltpu.VMEM((blocks, HEAD_SIZE, block), jnp.float32),
                pltpu.VMEM((blocks, HEAD_SIZE, block), jnp.float32),
            ],
        ),
        out_shape=[
            jax.ShapeDtypeStruct((blocks, wide, block), jnp.bfloat16),
            jax.ShapeDtypeStruct((wide, length), jnp.bfloat16),
        ],
        compiler_params=pltpu.CompilerParams(vmem_limit_bytes=40 * 2**20),
        name="attend_backward",
    )(spans, projected, grads, projected, seg_row, seg_col, mixed, totals)


def hits(slots, height):
    spot = lax.broadcasted_iota(jnp.int32, (height, slots.shape[1]), 0)
    return (spot == slots[0:1, :], spot == slots[1:2, :])


def spread_kernel(slots_ref, rows_ref, *out_refs):
    size = out_refs[0].shape[0]
    first, second = hits(slots_ref[...], size * len(out_refs))
    chosen = (first | second).astype(jnp.bfloat16)
    for k, out_ref in enumerate(out_refs):
        out_ref[...] = jnp.dot(
            chosen[k * size : (k + 1) * size], rows_ref[...], preferred_element_type=jnp.float32
        ).astype(jnp.bfloat16)


def spread_rows(slots, rows, size, blocks):
    return pl.pallas_call(
        spread_kernel,
        out_shape=[jax.ShapeDtypeStruct((size, rows.shape[1]), jnp.bfloat16)] * blocks,
        compiler_params=pltpu.CompilerParams(vmem_limit_bytes=40 * 2**20),
        name="spread_rows",
    )(slots, rows)


def middle_kernel(
    lane, router_lane, start_ref, mixed_ref, weight_ref, table_ref, slots_ref, routes_ref,
    middle_ref, sent_ref, gates_ref,
):
    table = table_ref[...]
    middle = start_ref[...].astype(jnp.float32) + contract(mixed_ref[...].T, weight_ref[...], 1, 1)
    middle_ref[...] = middle
    unit, _ = unit_of(middle)
    expert_low = (unit * column_as_row(table, lane)).astype(jnp.bfloat16)
    first, second = hits(slots_ref[...], sent_ref.shape[0])
    sent_ref[...] = jnp.dot(
        (first | second).astype(jnp.bfloat16), expert_low, preferred_element_type=jnp.float32
    ).astype(jnp.bfloat16)
    logits = jnp.dot(expert_low, table, preferred_element_type=jnp.float32).T
    spot = lax.broadcasted_iota(jnp.int32, logits.shape, 0) - router_lane
    chosen = [
        jnp.sum(jnp.where(spot == routes_ref[c : c + 1, :], logits, 0.0), 0, keepdims=True)
        for c in range(2)
    ]
    top = jnp.maximum(chosen[0], chosen[1])
    parts = [jnp.exp(value - top) for value in chosen]
    gates_ref[...] = jnp.concatenate([part / (parts[0] + parts[1]) for part in parts], 0)


def middle_part(start, mixed, weight, head_weights, slots, routes, lane, router_lane, height):
    rows, width = start.shape
    lanes = head_weights.shape[1]
    whole = lambda shape: pl.BlockSpec(shape, lambda i: (0, 0))
    return pl.pallas_call(
        functools.partial(middle_kernel, lane, router_lane),
        grid=(1,),
        in_specs=[
            whole(start.shape),
            whole(mixed.shape),
            whole(weight.shape),
            pl.BlockSpec((width, 128), lambda i: (0, lanes // 128 - 1)),
            whole(slots.shape),
            whole(routes.shape),
        ],
        out_specs=[whole((rows, width)), whole((height, width)), whole((2, rows))],
        out_shape=[
            jax.ShapeDtypeStruct((rows, width), jnp.float32),
            jax.ShapeDtypeStruct((height, width), jnp.bfloat16),
            jax.ShapeDtypeStruct((2, rows), jnp.float32),
        ],
        compiler_params=pltpu.CompilerParams(vmem_limit_bytes=60 * 2**20),
        name="middle",
    )(start, mixed, weight, head_weights, slots, routes)


def block_place(own_ref, axis, k, size):
    return pl.ds(pl.multiple_of(jnp.bitwise_xor(own_ref[axis], k) * size, size), size)


def assemble_weights(own_ref, part_refs, gate, up, outer):
    count = len(part_refs) // 3
    for k in range(count):
        size = part_refs[k].shape[0]
        place = block_place(own_ref, 1, k, size)
        gate[place, :] = part_refs[k][...]
        up[place, :] = part_refs[count + k][...]
        outer[:, place] = part_refs[2 * count + k][...]


def expert_kernel(router_lane, blocks, own_ref, rows_ref, *refs):
    weight_refs, (table_ref, other_ref) = refs[:12], refs[12:14]
    pre_gate_ref, pre_up_ref, hidden_ref, gates_ref = refs[14:18]
    part_refs, (part_sum, gate, up, outer) = refs[18 : 18 + blocks], refs[18 + blocks :]
    step = pl.program_id(0)
    size = part_refs[0].shape[0]
    rows = rows_ref[...]
    assemble_weights(own_ref, weight_refs, gate, up, outer)

    @pl.when(step == 0)
    def _():
        lane = lax.broadcasted_iota(jnp.int32, (rows.shape[0], 128), 1) - router_lane
        logits = jnp.dot(rows, table_ref[...], preferred_element_type=jnp.float32)
        own = jnp.sum(jnp.where(lane == own_ref[0], logits, 0.0), 1, keepdims=True)
        other = jnp.sum(jnp.where(lane == other_ref[...], logits, 0.0), 1, keepdims=True)
        top = jnp.maximum(own, other)
        own, other = jnp.exp(own - top), jnp.exp(other - top)
        gates_ref[:, 0:1] = own / (own + other)
        gates_ref[:, 1:2] = other / (own + other)
        part_sum[...] = jnp.zeros_like(part_sum)

    gate_pre = jnp.dot(rows, gate[...], preferred_element_type=jnp.float32)
    up_pre = jnp.dot(rows, up[...], preferred_element_type=jnp.float32)
    pre_gate_ref[...] = gate_pre
    pre_up_ref[...] = up_pre
    hidden = (gate_pre / (1.0 + jnp.exp(-gate_pre)) * up_pre).astype(jnp.bfloat16)
    hidden_ref[...] = hidden
    part_sum[...] += jnp.dot(hidden, outer[...], preferred_element_type=jnp.float32)

    @pl.when(step == pl.num_programs(0) - 1)
    def _():
        for k, ref in enumerate(part_refs):
            ref[...] = part_sum[block_place(own_ref, 0, k, size), :].astype(jnp.bfloat16)


def weight_specs(inner, outer, tile, steps):
    size = inner[0].shape[0]
    return (
        [pl.BlockSpec((size, tile), lambda i, own: (0, i))] * len(inner)
        + [pl.BlockSpec((size, tile), lambda i, own: (0, steps + i))] * len(inner)
        + [pl.BlockSpec((tile, size), lambda i, own: (i, 0))] * len(outer)
    )


def expert_forward_pass(own, rows, inner, outer, head_weights, other, router_lane, tile, blocks):
    height, width = rows.shape
    units = outer[0].shape[0]
    steps = units // tile
    lanes = head_weights.shape[1]
    whole = lambda shape: pl.BlockSpec(shape, lambda i, own: (0, 0))
    tiled = lambda rows, off: pl.BlockSpec((rows, tile), lambda i, own: (0, off + i))
    shape = jax.ShapeDtypeStruct
    low, f32 = jnp.bfloat16, jnp.float32
    outcome = pl.pallas_call(
        functools.partial(expert_kernel, router_lane, blocks),
        grid_spec=pltpu.PrefetchScalarGridSpec(
            num_scalar_prefetch=1,
            grid=(steps,),
            in_specs=[whole(rows.shape)]
            + weight_specs(inner, outer, tile, steps)
            + [
                pl.BlockSpec((width, 128), lambda i, own: (0, lanes // 128 - 1)),
                whole(other.shape),
            ],
            out_specs=[tiled(height, 0)] * 3
            + [whole((height, 128))]
            + [whole((height // blocks, width))] * blocks,
            scratch_shapes=[
                pltpu.VMEM((height, width), f32),
                pltpu.VMEM((width, tile), low),
                pltpu.VMEM((width, tile), low),
                pltpu.VMEM((tile, width), low),
            ],
        ),
        out_shape=[shape((height, units), f32)] * 2
        + [shape((height, units), low), shape((height, 128), f32)]
        + [shape((height // blocks, width), low)] * blocks,
        compiler_params=pltpu.CompilerParams(vmem_limit_bytes=56 * 2**20),
        name="expert",
    )(own, rows, *inner, *inner, *outer, head_weights, other)
    return outcome[:4], list(outcome[4:])


def expert_back_kernel(router_lane, blocks, own_ref, *refs):
    cot_refs, part_refs, refs = refs[:blocks], refs[blocks : 2 * blocks], refs[2 * blocks :]
    rows_ref, gates_ref, pre_gate_ref, pre_up_ref = refs[:4]
    weight_refs, refs = refs[4:16], refs[16:]
    table_ref, other_ref, grad_gate_ref, grad_up_ref, grad_ref, back_ref, router_ref = refs[:7]
    cot, back_sum, gate, up, outer = refs[7:]
    step = pl.program_id(0)
    assemble_weights(own_ref, weight_refs, gate, up, outer)
    size = cot_refs[0].shape[0]
    gates = gates_ref[...]

    @pl.when(step == 0)
    def _():
        for k, ref in enumerate(cot_refs):
            cot[block_place(own_ref, 0, k, size), :] = ref[...]
        grad_ref[...] = (gates[:, 0:1] * cot[...].astype(jnp.float32)).astype(jnp.bfloat16)
        back_sum[...] = jnp.zeros_like(back_sum)

    gate_pre, up_pre = pre_gate_ref[...], pre_up_ref[...]
    grad_hidden = contract(grad_ref[...], outer[...], 1, 1)
    sigma = 1.0 / (1.0 + jnp.exp(-gate_pre))
    grad_gate = grad_hidden * up_pre * sigma * (1.0 + gate_pre * (1.0 - sigma))
    grad_gate = grad_gate.astype(jnp.bfloat16)
    grad_up = (grad_hidden * (gate_pre * sigma)).astype(jnp.bfloat16)
    grad_gate_ref[...] = grad_gate
    grad_up_ref[...] = grad_up
    back_sum[...] += contract(grad_gate, gate[...], 1, 1) + contract(grad_up, up[...], 1, 1)

    @pl.when(step == pl.num_programs(0) - 1)
    def _():
        table = table_ref[...]
        total = jnp.zeros(router_ref.shape, jnp.float32)
        for k in range(blocks):
            place = block_place(own_ref, 0, k, size)
            grad_gates = jnp.sum(
                cot_refs[k][...].astype(jnp.float32) * part_refs[k][...].astype(jnp.float32),
                1,
                keepdims=True,
            )
            gates_k = gates_ref[place, :]
            lane_k = lax.broadcasted_iota(jnp.int32, (size, 128), 1) - router_lane
            sides_k = (lane_k == own_ref[0]).astype(jnp.float32) - (
                lane_k == other_ref[place, :]
            ).astype(jnp.float32)
            high, rest = split_low(gates_k[:, 0:1] * gates_k[:, 1:2] * grad_gates * sides_k)
            routed = contract(high, table, 1, 1) + contract(rest, table, 1, 1)
            back = back_sum[place, :].astype(jnp.bfloat16).astype(jnp.float32)
            back_ref[place, :] = (back + routed).astype(jnp.bfloat16)
            rows_k = rows_ref[place, :]
            total = total + contract(high, rows_k, 0, 0) + contract(rest, rows_k, 0, 0)
        router_ref[...] = total


def expert_backward_pass(
    own, cot_blocks, part_blocks, rows, gates, pre_gate, pre_up, inner, outer, head_weights, other,
    router_lane, tile,
):
    height, width = rows.shape
    units = outer[0].shape[0]
    steps = units // tile
    lanes = head_weights.shape[1]
    blocks = len(cot_blocks)
    whole = lambda shape: pl.BlockSpec(shape, lambda i, own: (0, 0))
    tiled = lambda rows, off: pl.BlockSpec((rows, tile), lambda i, own: (0, off + i))
    low, f32 = jnp.bfloat16, jnp.float32
    return pl.pallas_call(
        functools.partial(expert_back_kernel, router_lane, blocks),
        grid_spec=pltpu.PrefetchScalarGridSpec(
            num_scalar_prefetch=1,
            grid=(steps,),
            in_specs=[whole((height // blocks, width))] * (2 * blocks)
            + [
                whole(rows.shape),
                whole(gates.shape),
                tiled(height, 0),
                tiled(height, 0),
            ]
            + weight_specs(inner, outer, tile, steps)
            + [
                pl.BlockSpec((width, 128), lambda i, own: (0, lanes // 128 - 1)),
                whole(other.shape),
            ],
            out_specs=[
                tiled(height, 0),
                tiled(height, 0),
                whole((height, width)),
                whole((height, width)),
                whole((128, width)),
            ],
            scratch_shapes=[
                pltpu.VMEM((height, width), low),
                pltpu.VMEM((height, width), f32),
                pltpu.VMEM((width, tile), low),
                pltpu.VMEM((width, tile), low),
                pltpu.VMEM((tile, width), low),
            ],
        ),
        out_shape=[
            jax.ShapeDtypeStruct((height, units), low),
            jax.ShapeDtypeStruct((height, units), low),
            jax.ShapeDtypeStruct((height, width), low),
            jax.ShapeDtypeStruct((height, width), low),
            jax.ShapeDtypeStruct((128, width), f32),
        ],
        compiler_params=pltpu.CompilerParams(vmem_limit_bytes=56 * 2**20),
        name="expert_backward",
    )(
        own, *cot_blocks, *part_blocks, rows, gates, pre_gate, pre_up, *inner, *inner, *outer,
        head_weights, other,
    )


def back_kernel(
    lane, middle_ref, cot_ref, home_ref, weight_ref, table_ref, slots_ref,
    grad_ref, branch_ref, gain_ref, mixed_ref,
):
    first, second = hits(slots_ref[...], home_ref.shape[0])
    grad_in = contract((first | second).astype(jnp.bfloat16), home_ref[...], 0, 0)
    unit, factor = unit_of(middle_ref[...])
    gain_ref[...] = jnp.sum(grad_in * unit, 0, keepdims=True)
    scaled = grad_in * column_as_row(table_ref[...], lane)
    inner_part = factor * (scaled - unit * jnp.mean(scaled * unit, -1, keepdims=True))
    grad_middle = cot_ref[...].astype(jnp.float32) + inner_part
    grad_ref[...] = grad_middle
    branch = grad_middle.astype(jnp.bfloat16)
    branch_ref[...] = branch
    mixed = jnp.dot(branch, weight_ref[...], preferred_element_type=jnp.float32)
    mixed_ref[...] = mixed.T.astype(jnp.bfloat16)


def back_part(middle, cot, home, weight, head_weights, slots, lane):
    rows, width = middle.shape
    lanes = head_weights.shape[1]
    whole = lambda shape: pl.BlockSpec(shape, lambda i: (0, 0))
    return pl.pallas_call(
        functools.partial(back_kernel, lane),
        grid=(1,),
        in_specs=[
            whole((rows, width)),
            whole((rows, width)),
            whole(home.shape),
            whole(weight.shape),
            pl.BlockSpec((width, 128), lambda i: (0, lanes // 128 - 1)),
            whole(slots.shape),
        ],
        out_specs=[
            whole((rows, width)),
            whole((rows, width)),
            whole((1, width)),
            whole((weight.shape[1], rows)),
        ],
        out_shape=[
            jax.ShapeDtypeStruct((rows, width), jnp.float32),
            jax.ShapeDtypeStruct((rows, width), jnp.bfloat16),
            jax.ShapeDtypeStruct((1, width), jnp.float32),
            jax.ShapeDtypeStruct((weight.shape[1], rows), jnp.bfloat16),
        ],
        compiler_params=pltpu.CompilerParams(vmem_limit_bytes=48 * 2**20),
        name="back",
    )(middle, cot, home, weight, head_weights, slots)


def weight_kernel(place, normed_ref, grads_ref, router_ref, gain_ref, out_ref):
    total = jnp.dot(grads_ref[...], normed_ref[...], preferred_element_type=jnp.float32)
    wide, span = total.shape
    rest = jnp.zeros((out_ref.shape[2] - wide - router_ref.shape[0] - 8, span), jnp.float32)
    gain = jnp.concatenate([gain_ref[...], jnp.zeros((7, span), jnp.float32)], 0)
    out_ref[0] = jnp.concatenate([total, router_ref[...], gain, rest], 0).T.astype(jnp.bfloat16)


def weight_terms(place, normed, grads, router, gain, router_lane, experts, lanes, parts):
    length, width = normed.shape
    wide = grads.shape[0]
    span = width // parts
    near = lambda row: lambda k, place: (row, jnp.bitwise_xor(place[0], k))
    return pl.pallas_call(
        weight_kernel,
        grid_spec=pltpu.PrefetchScalarGridSpec(
            num_scalar_prefetch=1,
            grid=(parts,),
            in_specs=[
                pl.BlockSpec((length, span), near(0)),
                pl.BlockSpec((wide, length), lambda k, place: (0, 0)),
                pl.BlockSpec((experts, span), near(router_lane // experts)),
                pl.BlockSpec((1, span), near(0)),
            ],
            out_specs=pl.BlockSpec((1, span, lanes), lambda k, place: (k, 0, 0)),
        ),
        out_shape=jax.ShapeDtypeStruct((parts, span, lanes), jnp.bfloat16),
        compiler_params=pltpu.CompilerParams(vmem_limit_bytes=40 * 2**20),
        name="weight_terms",
    )(place, normed, grads, router, gain)


def tokens_back_kernel(
    lane, start_ref, middle_ref, grads_ref, weight_ref, table_ref, out_ref, total
):
    step = pl.program_id(0)

    @pl.when(step == 0)
    def _():
        total[...] = jnp.zeros_like(total)

    grads = jnp.concatenate([grads_ref[0], grads_ref[1]], 0).T
    total[...] += contract(grads, weight_ref[...], 1, 1)

    @pl.when(step == pl.num_programs(0) - 1)
    def _():
        unit, factor = unit_of(start_ref[...].astype(jnp.float32))
        scaled = total[...] * column_as_row(table_ref[...], lane)
        inner_part = factor * (scaled - unit * jnp.mean(scaled * unit, -1, keepdims=True))
        out_ref[...] = middle_ref[...] + inner_part


def tokens_back(start, grad_middle, grads, weight, head_weights, lane):
    rows, width = start.shape
    count, cols, _ = grads.shape
    lanes = head_weights.shape[1]
    whole = lambda shape: pl.BlockSpec(shape, lambda i: (0, 0))
    return pl.pallas_call(
        functools.partial(tokens_back_kernel, lane),
        grid=(count // 2,),
        in_specs=[
            whole(start.shape),
            whole(grad_middle.shape),
            pl.BlockSpec((2, cols, rows), lambda i: (i, 0, 0)),
            pl.BlockSpec((width, 2 * cols), lambda i: (0, i)),
            pl.BlockSpec((width, 128), lambda i: (0, lanes // 128 - 1)),
        ],
        out_specs=whole((rows, width)),
        out_shape=jax.ShapeDtypeStruct((rows, width), jnp.float32),
        scratch_shapes=[pltpu.VMEM((rows, width), jnp.float32)],
        compiler_params=pltpu.CompilerParams(vmem_limit_bytes=32 * 2**20),
        name="tokens_back",
    )(start, grad_middle, grads, weight, head_weights)


def mixture_kernel(slots_ref, gates_ref, middle_ref, *refs):
    part_refs, out_ref = refs[:-1], refs[-1]
    size = part_refs[0].shape[0]
    first, second = hits(slots_ref[...], size * len(part_refs))
    total = middle_ref[...]
    shares = gates_ref[...]
    for _ in range(3):
        piece = shares.astype(jnp.bfloat16)
        shares = shares - piece.astype(jnp.float32)
        piece = piece.astype(jnp.float32)
        weights = jnp.where(first, piece[0:1], 0.0) + jnp.where(second, piece[1:2], 0.0)
        weights = weights.astype(jnp.bfloat16)
        for k, ref in enumerate(part_refs):
            total = total + contract(weights[k * size : (k + 1) * size], ref[...], 0, 0)
    out_ref[...] = total.astype(jnp.bfloat16)


def mixture(slots, gates, middle, parts):
    return pl.pallas_call(
        mixture_kernel,
        out_shape=jax.ShapeDtypeStruct(middle.shape, jnp.bfloat16),
        compiler_params=pltpu.CompilerParams(vmem_limit_bytes=40 * 2**20),
        name="mixture",
    )(slots, gates, middle, *parts)


def weight_grads_kernel(
    share, home_ref, query_weight_ref, keyval_weight_ref,
    query_ref, keyval_ref, router_ref, gains_ref,
):
    count = home_ref.shape[0]
    cols = share + 2 * HEAD_SIZE
    half = count * HEAD_SIZE
    experts = router_ref.shape[1]
    small = jnp.zeros((home_ref.shape[1], home_ref.shape[2] - cols), jnp.float32)
    for e in range(count):
        part = home_ref[e].astype(jnp.float32)
        query_ref[:, e * share : (e + 1) * share] = part[:, :share]
        at = e * HEAD_SIZE
        keyval_ref[:, at : at + HEAD_SIZE] = part[:, share : share + HEAD_SIZE]
        keyval_ref[:, half + at : half + at + HEAD_SIZE] = part[:, share + HEAD_SIZE : cols]
        small = small + part[:, cols:]
    router_ref[...] = small[:, :experts]
    products = jnp.sum(
        query_ref[...] * query_weight_ref[...].astype(jnp.float32), 1, keepdims=True
    ) + jnp.sum(keyval_ref[...] * keyval_weight_ref[...].astype(jnp.float32), 1, keepdims=True)
    gains_ref[:, 0:1] = products
    gains_ref[:, 1:2] = small[:, experts : experts + 1]


def weight_grads(home, query_weight, keyval_weight, share, experts):
    shape = lambda width: jax.ShapeDtypeStruct((query_weight.shape[0], width), jnp.float32)
    return pl.pallas_call(
        functools.partial(weight_grads_kernel, share),
        out_shape=[
            shape(query_weight.shape[1]),
            shape(keyval_weight.shape[1]),
            shape(experts),
            shape(2),
        ],
        compiler_params=pltpu.CompilerParams(vmem_limit_bytes=40 * 2**20),
        name="weight_grads",
    )(home, query_weight, keyval_weight)


def sum_pairs_kernel(*refs):
    out_ref = refs[-1]
    count = len(refs) // 2
    for side in range(2):
        total = sum(ref[...].astype(jnp.float32) for ref in refs[side * count : (side + 1) * count])
        out_ref[:, side, :] = total


def sum_pairs(first, second, tile):
    rows, width = first[0].shape
    return pl.pallas_call(
        sum_pairs_kernel,
        grid=(rows // tile,),
        in_specs=[pl.BlockSpec((tile, width), lambda i: (i, 0))] * (len(first) + len(second)),
        out_specs=pl.BlockSpec((tile, 2, width), lambda i: (i, 0, 0)),
        out_shape=jax.ShapeDtypeStruct((rows, 2, width), jnp.float32),
        compiler_params=pltpu.CompilerParams(vmem_limit_bytes=40 * 2**20),
        name="sum_pairs",
    )(*first, *second)


def after(values, *earlier):
    return lax.optimization_barrier((values, earlier))[0]


def flip_exchange(block, axis, flip):
    count = lax.axis_size(axis)
    return lax.ppermute(block, axis, [(i, i ^ flip) for i in range(count)])


def swap_near_blocks(blocks, flips):
    return [flip_exchange(blocks[flip], "fsdp", flip) for flip in flips]


def swap_near(block, axis, flips):
    return [flip_exchange(block, axis, flip) for flip in flips]


def in_order(parts, axis):
    stacked = jnp.stack(parts)
    index = lax.axis_index(axis)
    return jnp.stack(
        [
            lax.dynamic_index_in_dim(stacked, jnp.bitwise_xor(index, j), 0, keepdims=False)
            for j in range(len(parts))
        ]
    )


def all_to_all(blocks):
    return lax.all_to_all(blocks, "fsdp", split_axis=0, concat_axis=0, tiled=True)


def gather(block, axis):
    return lax.all_gather(block, axis, axis=0, tiled=True)


def per_device_heads(
    tokens,
    segment_ids,
    routes,
    query_weight,
    key_value_weight,
    output_weight,
    router_weight,
    gain_before,
    gain_middle,
    inner_weight,
    outer_weight,
    cotangent,
):
    f32, low = jnp.float32, jnp.bfloat16
    _, rows, width = tokens.shape
    count = lax.axis_size("fsdp")
    experts = router_weight.shape[1]
    index, group = lax.axis_index("fsdp"), lax.axis_index("dp")
    core = index % 2
    capacity = 3 * rows // 8
    height = experts * capacity
    length = count * rows
    shard = query_weight.shape[0]
    share = QUERY_HEADS // KEY_VALUE_HEADS * HEAD_SIZE
    cols = share + 2 * HEAD_SIZE
    half = KEY_VALUE_HEADS * HEAD_SIZE
    ff = outer_weight.shape[0]
    size = inner_weight.shape[0]

    start_low = tokens.reshape(rows, width)
    cot_low = cotangent.reshape(rows, width)

    route = routes.reshape(rows, 2)
    route_flat = route.reshape(rows * 2)
    picks = route_flat[:, None] == jnp.arange(experts, dtype=jnp.int32)[None, :]
    before = jnp.dot(
        jnp.tril(jnp.ones((rows * 2, rows * 2), low), -1),
        picks.astype(low),
        preferred_element_type=f32,
    )
    rank = jnp.sum(jnp.where(picks, before, 0.0), 1).astype(jnp.int32).reshape(rows, 2)
    route_lines = route.T
    slots = (route * capacity + rank).T
    slots_near = (jnp.bitwise_xor(route, index) * capacity + rank).T
    spots = jnp.arange(height, dtype=jnp.int32)[:, None]
    other_route = jnp.sum(
        jnp.where(slots[0:1] == spots, route_lines[1:2], 0)
        + jnp.where(slots[1:2] == spots, route_lines[0:1], 0),
        1,
    )

    by_head = jnp.concatenate(
        [
            query_weight.reshape(shard, count, share),
            key_value_weight[:, :half].reshape(shard, count, HEAD_SIZE),
            key_value_weight[:, half:].reshape(shard, count, HEAD_SIZE),
        ],
        2,
    )
    lanes = 128 * -(-(cols + 2 + experts) // 128)
    table_lane = lanes - 128
    router_lane = cols - table_lane
    first_lane, second_lane = router_lane + experts, router_lane + experts + 1
    extras = jnp.concatenate([router_weight, gain_before[:, None], gain_middle[:, None]], 1)
    extras = jnp.broadcast_to(extras[None], (count, shard, 2 + experts))
    head_block = jnp.concatenate([by_head.transpose(1, 0, 2), extras], 2)
    head_block = jnp.pad(head_block, ((0, 0), (0, 0), (0, lanes - cols - 2 - experts)))
    seg_line = jnp.broadcast_to(segment_ids.reshape(1, 1, rows), (count, 1, rows)).astype(low)
    seg_line = jnp.pad(seg_line, ((0, 0), (0, 0), (0, lanes - rows)))
    other_line = other_route.reshape(experts, 1, capacity).astype(low)
    other_line = jnp.pad(other_line, ((0, 0), (0, 14), (0, lanes - capacity)))
    head_block = jnp.concatenate([head_block, seg_line, other_line], 1)
    chip = index // 2
    tokens_all = gather(start_low, "fsdp")
    arrived = all_to_all(head_block)

    inner_own = inner_weight.reshape(size, 2 * ff)
    inner_x, inner_y = swap_near(inner_own, "dp", (1, 2))
    outer_x, outer_y = swap_near(outer_weight, "dp", (1, 2))
    arrived, inner_x, inner_y, outer_x, outer_y = after(
        (arrived, inner_x, inner_y, outer_x, outer_y)
    )
    segments = arrived[:, shard, :rows].reshape(length).astype(jnp.int32)
    other_expert = arrived[:, shard + 1, :capacity].reshape(height, 1).astype(jnp.int32)
    head_rows = arrived[:, :shard].reshape(count * shard, lanes)
    head_near = swap_near(head_rows, "dp", (1, 2, 3))
    head_weights = in_order([head_rows] + head_near, "dp").reshape(width, lanes)
    cot_sent = spread_rows(slots_near, cot_low, capacity, experts)

    firsts = segments.reshape(count, rows)
    starts = jnp.sum(segments[None, :] < firsts[:, :1], 1) // rows
    wholes = (jnp.sum(segments[None, :] < firsts[:, -1:], 1) + rows - 1) // rows
    wholes = jnp.minimum(wholes, jnp.arange(count))
    spans = jnp.stack([starts, wholes]).astype(jnp.int32)
    seg_row, seg_col = segments.reshape(1, length), segments.reshape(length, 1)

    by_head_line = by_head.reshape(shard, count * cols)
    tokens_all, cot_sent, head_weights, by_head_line, output_own, spans, seg_row, seg_col = after(
        (
            tokens_all, cot_sent, head_weights, by_head_line, output_weight.T, spans, seg_row,
            seg_col,
        )
    )
    output_all = gather(output_own, ("dp", "fsdp"))
    normed, projected = project(tokens_all, head_weights, cols, first_lane, rows)
    cot_first = swap_near_blocks(cot_sent, (4, 6, 2))
    mixed_head, mixed_exact, totals = attend(spans, projected, seg_row, seg_col)
    mixed_head, cot_first, by_head_line = after((mixed_head, cot_first, by_head_line))
    project_line = gather(by_head_line, "fsdp")
    mixed = all_to_all(mixed_head).reshape(count * share, rows)

    middle, sent, gates = middle_part(
        start_low, mixed, output_all, head_weights, slots, route_lines,
        second_lane, router_lane, height,
    )

    rows_in = all_to_all(sent)
    inner_far = flip_exchange(after(inner_x, sent), "dp", 2)
    outer_far = flip_exchange(after(outer_y, sent), "dp", 1)
    rows_in, cot_sent, project_line, inner_far, outer_far = after(
        (rows_in, cot_sent, project_line, inner_far, outer_far)
    )
    inner_parts = [inner_own, inner_x, inner_y, inner_far]
    outer_parts = [outer_weight, outer_x, outer_y, outer_far]
    project_all = gather(project_line, "dp")
    cot_last = swap_near_blocks(cot_sent, (5, 7, 3, 1))
    own_expert = jnp.stack([index, group]).astype(jnp.int32)
    (pre_gate, pre_up, hidden, slot_gates), parts = expert_forward_pass(
        own_expert, rows_in, inner_parts, outer_parts, head_weights, other_expert,
        router_lane, 256, experts,
    )
    hidden, parts, cot_last = after((hidden, parts, cot_last))
    part_first = swap_near_blocks(parts, (4, 6, 2, 1, 3))
    cot_in = [cot_sent[0], cot_last[3], cot_first[2], cot_last[2]]
    cot_in = cot_in + [cot_first[0], cot_last[0], cot_first[1], cot_last[1]]
    grad_gate, grad_up, grad_in, grad_rows, router_part = expert_backward_pass(
        own_expert, cot_in, parts, rows_in, slot_gates, pre_gate, pre_up, inner_parts, outer_parts,
        head_weights, other_expert, router_lane, 512,
    )
    grad_rows, part_first, grad_gate, grad_up, grad_in = after(
        (grad_rows, part_first, grad_gate, grad_up, grad_in)
    )
    grad_home = all_to_all(grad_rows)

    def cut(value, k):
        return lax.dynamic_slice_in_dim(value, jnp.bitwise_xor(group, k) * size, size, 1)

    rows_near = [cut(rows_in, k) for k in range(4)]
    gate_terms = [contract(near, grad_gate, 0, 0).astype(low) for near in rows_near]
    up_terms = [contract(near, grad_up, 0, 0).astype(low) for near in rows_near]
    near_a, far_a = [flip_exchange(gate_terms[k], "dp", 1) for k in (1, 3)]
    near_b, far_b = [flip_exchange(up_terms[k], "dp", 2) for k in (2, 3)]
    passed_a = (gate_terms[2].astype(f32) + far_a.astype(f32)).astype(low)
    passed_b = (up_terms[1].astype(f32) + far_b.astype(f32)).astype(low)
    outer_term = jnp.concatenate(
        [contract(hidden, grad_in[:, k * size : (k + 1) * size], 0, 0) for k in range(4)]
    ).astype(low)
    grad_home, outer_term, passed_a, passed_b, gate_terms, up_terms, near_a, near_b, project_all = after(
        (
            grad_home, outer_term, passed_a, passed_b, gate_terms, up_terms, near_a, near_b,
            project_all,
        )
    )
    side_a, side_b = flip_exchange(passed_a, "dp", 2), flip_exchange(passed_b, "dp", 1)

    grad_middle, grad_branch, gain_part, mixed_grad = back_part(
        middle, cot_low, grad_home, output_all, head_weights, slots, second_lane
    )
    mixed_grad = all_to_all(mixed_grad.reshape(count, share, rows))

    branch_near = jnp.concatenate([cut(grad_branch, k) for k in range(4)], 1)
    half_width = width // 2

    def half_terms(side):
        heads = lax.dynamic_slice_in_dim(mixed, side * half_width, half_width, 0)
        return contract(branch_near, heads, 0, 1).astype(low)

    from_core = flip_exchange(half_terms(1 - core), "fsdp", 1)
    output_part = half_terms(core).astype(f32) + from_core.astype(f32)
    output_part = output_part.astype(low).reshape(4, size, half_width)
    mixed_grad, output_part, parts, side_a, side_b, outer_term = after(
        (mixed_grad, output_part, parts, side_a, side_b, outer_term)
    )
    outer_sum = lax.psum_scatter(outer_term, "dp", scatter_dimension=0, tiled=True)
    output_near = flip_exchange(output_part[2:], "dp", 2)
    part_last = swap_near_blocks(parts, (5, 7))

    grads_blocks, grads_line = attend_backward(
        spans, projected, mixed_grad, seg_row, seg_col, mixed_exact, totals
    )
    grads_blocks, grads_line, part_last = after((grads_blocks, grads_line, part_last))
    part_home = [parts[0], part_first[3], part_first[2], part_first[4]]
    part_home = part_home + [part_first[0], part_last[0], part_first[1], part_last[1]]
    grad_mine = all_to_all(grads_blocks)
    own_group = group.reshape(1).astype(jnp.int32)
    terms = weight_terms(
        own_group, normed, grads_line, router_part, gain_part, router_lane, experts, lanes, 4
    )
    terms, output_part, output_near = after((terms, output_part, output_near))
    output_sum = output_part[:2].astype(f32) + output_near.astype(f32)
    inner_grad = sum_pairs(
        [gate_terms[0], near_a, side_a], [up_terms[0], near_b, side_b], size // 4
    )
    outer_grad = outer_sum.astype(f32)
    block_out = mixture(slots_near, gates, middle, after(part_home, outer_grad))
    weights_near = after(
        [flip_exchange(terms[k], "dp", k) for k in range(1, 4)], inner_grad, block_out
    )
    weight_sum = terms[0].astype(f32)
    for near in weights_near:
        weight_sum = weight_sum + near.astype(f32)
    weight_sum, output_passed = after((weight_sum.astype(low), output_sum[1].astype(low)))
    output_side = flip_exchange(output_passed, "dp", 1)
    tokens_grad = tokens_back(
        start_low, grad_middle, after(grad_mine, inner_grad, outer_grad, block_out), project_all,
        head_weights, first_lane,
    )
    output_sum = output_sum[0] + output_side.astype(f32)
    weight_sum = after(weight_sum, grad_mine)
    weight_home = all_to_all(weight_sum.reshape(count, shard, lanes))
    chips, pair = count // 2, 2 * shard
    output_low = output_sum.astype(low)

    def line_part(value, k):
        at = jnp.bitwise_xor(index // 2, k) * pair
        return lax.dynamic_slice_in_dim(value, at, pair, 0)

    output_line = [
        flip_exchange(line_part(output_low, k), "fsdp", 2 * k) for k in range(1, chips)
    ]
    output_line, weight_home = after((output_line, weight_home), tokens_grad)
    query_grad, keyval_grad, router_grad, gains = weight_grads(
        weight_home, query_weight, key_value_weight, share, experts
    )
    before_grad, middle_grad = gains[:, 0] / gain_before.astype(f32), gains[:, 1]
    output_grad = line_part(output_sum, 0)
    for near in output_line:
        output_grad = output_grad + near.astype(f32)
    own_half = lax.dynamic_slice_in_dim(output_grad, core * shard, shard, 0)
    other_half = flip_exchange(
        lax.dynamic_slice_in_dim(output_grad, (1 - core) * shard, shard, 0), "fsdp", 1
    )
    output_grad = jnp.where(
        core == 0,
        jnp.concatenate([own_half, other_half], 1),
        jnp.concatenate([other_half, own_half], 1),
    ).T
    return (
        block_out[None],
        tokens_grad[None],
        query_grad,
        keyval_grad,
        output_grad,
        router_grad,
        before_grad,
        middle_grad,
        inner_grad,
        outer_grad,
    )


def solution(mesh):
    by_heads = (mesh.shape["dp"], mesh.shape["fsdp"]) == (4, KEY_VALUE_HEADS)
    in_specs = (
        P("dp", "fsdp", None),
        P("dp", "fsdp"),
        P("dp", "fsdp", None),
        P(("dp", "fsdp"), None),
        P(("dp", "fsdp"), None),
        P(None, ("dp", "fsdp")),
        P(("dp", "fsdp"), None),
        P(("dp", "fsdp")),
        P(("dp", "fsdp")),
        P("dp", None, "fsdp"),
        P("fsdp", "dp"),
        P("dp", "fsdp", None),
    )
    out_specs = (
        P("dp", "fsdp", None),
        P("dp", "fsdp", None),
        P(("dp", "fsdp"), None),
        P(("dp", "fsdp"), None),
        P(None, ("dp", "fsdp")),
        P(("dp", "fsdp"), None),
        P(("dp", "fsdp")),
        P(("dp", "fsdp")),
        P("dp", None, "fsdp"),
        P("fsdp", "dp"),
    )
    return jax.shard_map(
        per_device_heads if by_heads else per_device, mesh=mesh, in_specs=in_specs, out_specs=out_specs, check_vma=False
    )
```

```python
import functools

import jax
import jax.numpy as jnp
from jax import lax
from jax.experimental import pallas as pl
from jax.experimental.pallas import tpu as pltpu
from jax.sharding import PartitionSpec as P

QUERY_HEADS = 24
KEY_VALUE_HEADS = 8
HEAD_SIZE = 64


HIGHEST_PRECISION = lax.Precision.HIGHEST
EPSILON = 1e-05
NEGATIVE_LARGE = -1e30


def normalize(hidden, gain_vec):
    factor = lax.rsqrt(jnp.mean(hidden * hidden, -1, keepdims=True) + EPSILON)
    unit_rows = hidden * factor
    return (unit_rows * gain_vec.astype(jnp.float32), unit_rows, factor)


def normalize_back(grad_rows, unit_rows, factor, gain_vec):
    scaled = grad_rows * gain_vec.astype(jnp.float32)
    inner_part = factor * (scaled - unit_rows * jnp.mean(scaled * unit_rows, -1, keepdims=True))
    return (inner_part, jnp.sum(grad_rows * unit_rows, 0))


def split_block(gathered, offset, key_tile_block):
    sequence_count = gathered.shape[0]
    portion_rows = lax.slice_in_dim(gathered, offset, offset + key_tile_block, axis=1)
    half_columns = KEY_VALUE_HEADS * HEAD_SIZE
    key_portion = portion_rows[..., :half_columns].reshape(
        sequence_count, key_tile_block, KEY_VALUE_HEADS, HEAD_SIZE
    )
    value_portion = portion_rows[..., half_columns:].reshape(
        sequence_count, key_tile_block, KEY_VALUE_HEADS, HEAD_SIZE
    )
    return (key_portion, value_portion)


def block_scores(query_matrix, key_portion, allowed):
    raw_scores = jnp.einsum(
        "sikgd,sjkd->skgij", query_matrix, key_portion, preferred_element_type=jnp.float32
    ) * HEAD_SIZE ** (-0.5)
    return jnp.where(allowed[:, None, None], raw_scores, NEGATIVE_LARGE)


def mask_for(seg_all, seg_mine, positions, offset, key_tile_block):
    key_seg = lax.slice_in_dim(seg_all, offset, offset + key_tile_block, axis=1)
    key_spots = offset + jnp.arange(key_tile_block, dtype=jnp.int32)
    same_doc = seg_mine[:, :, None] == key_seg[:, None, :]
    causal = key_spots[None, None, :] <= positions[None, :, None]
    return same_doc & causal


def log_totals(query_matrix, gathered, block_masks, key_tile_block):
    sequence_count, resident_rows = (query_matrix.shape[0], query_matrix.shape[1])
    running_totals = jnp.full(
        (sequence_count, KEY_VALUE_HEADS, QUERY_HEADS // KEY_VALUE_HEADS, resident_rows),
        NEGATIVE_LARGE,
        jnp.float32,
    )
    for block_index, allowed in enumerate(block_masks):
        key_portion, value_portion = split_block(
            gathered, block_index * key_tile_block, key_tile_block
        )

        def log_live(present_value, key_portion=key_portion, allowed=allowed):
            scores = block_scores(query_matrix, key_portion, allowed)
            return jnp.logaddexp(present_value, jax.nn.logsumexp(scores, -1))

        running_totals = lax.cond(
            jnp.any(allowed), log_live, lambda present_value: present_value, running_totals
        )
    return running_totals


def attend_values(query_matrix, gathered, block_masks, key_tile_block, running_totals):
    result = jnp.zeros(query_matrix.shape, jnp.float32)
    for block_index, allowed in enumerate(block_masks):
        key_portion, value_portion = split_block(
            gathered, block_index * key_tile_block, key_tile_block
        )

        def attend_live(
            present_value, key_portion=key_portion, value_portion=value_portion, allowed=allowed
        ):
            probs = jnp.exp(
                block_scores(query_matrix, key_portion, allowed) - running_totals[..., None]
            ).astype(jnp.bfloat16)
            return present_value + jnp.einsum(
                "skgij,sjkd->sikgd", probs, value_portion, preferred_element_type=jnp.float32
            )

        result = lax.cond(
            jnp.any(allowed), attend_live, lambda present_value: present_value, result
        )
    token_count = query_matrix.shape[0] * query_matrix.shape[1]
    return result.reshape(token_count, -1).astype(jnp.bfloat16)


def attend_back(
    query_matrix, mixed_gradient, gathered, block_masks, key_tile_block, running_totals
):
    sequence_count = query_matrix.shape[0]
    delta = jnp.zeros(running_totals.shape, jnp.float32)
    for block_index, allowed in enumerate(block_masks):
        key_portion, value_portion = split_block(
            gathered, block_index * key_tile_block, key_tile_block
        )

        def live_delta(
            present_value, key_portion=key_portion, value_portion=value_portion, allowed=allowed
        ):
            probs = jnp.exp(
                block_scores(query_matrix, key_portion, allowed) - running_totals[..., None]
            )
            grad_probs = jnp.einsum(
                "sikgd,sjkd->skgij",
                mixed_gradient,
                value_portion,
                preferred_element_type=jnp.float32,
            )
            return present_value + jnp.sum(probs * grad_probs, -1)

        delta = lax.cond(jnp.any(allowed), live_delta, lambda present_value: present_value, delta)
    grad_queries = jnp.zeros(query_matrix.shape, jnp.float32)
    key_terms = []
    for block_index, allowed in enumerate(block_masks):
        key_portion, value_portion = split_block(
            gathered, block_index * key_tile_block, key_tile_block
        )

        def live_grad(
            present_value, key_portion=key_portion, value_portion=value_portion, allowed=allowed
        ):
            probs = jnp.exp(
                block_scores(query_matrix, key_portion, allowed) - running_totals[..., None]
            )
            grad_probs = jnp.einsum(
                "sikgd,sjkd->skgij",
                mixed_gradient,
                value_portion,
                preferred_element_type=jnp.float32,
            )
            grad_scores = (probs * (grad_probs - delta[..., None])).astype(jnp.bfloat16)
            updated = present_value + jnp.einsum(
                "skgij,sjkd->sikgd", grad_scores, key_portion, preferred_element_type=jnp.float32
            ) * HEAD_SIZE ** (-0.5)
            grad_keys = jnp.einsum(
                "skgij,sikgd->sjkd", grad_scores, query_matrix, preferred_element_type=jnp.float32
            ) * HEAD_SIZE ** (-0.5)
            grad_values = jnp.einsum(
                "skgij,sikgd->sjkd",
                probs.astype(jnp.bfloat16),
                mixed_gradient,
                preferred_element_type=jnp.float32,
            )
            both_parts = jnp.concatenate(
                [
                    grad_keys.reshape(sequence_count, key_tile_block, -1),
                    grad_values.reshape(sequence_count, key_tile_block, -1),
                ],
                -1,
            )
            return (updated, both_parts)

        def dead_grad(present_value):
            return (
                present_value,
                jnp.zeros(
                    (sequence_count, key_tile_block, 2 * KEY_VALUE_HEADS * HEAD_SIZE), jnp.float32
                ),
            )

        grad_queries, block_term = lax.cond(jnp.any(allowed), live_grad, dead_grad, grad_queries)
        key_terms.append(block_term)
    return (grad_queries, jnp.concatenate(key_terms, 1), delta)


def expert_forward(inner_use, outer_use, received):
    model_width = received.shape[-1]
    rows_in = received.reshape(-1, model_width)
    pre_rows = jnp.dot(rows_in, inner_use, preferred_element_type=jnp.float32)
    slab_width = outer_use.shape[0]
    hidden_rows = (jax.nn.silu(pre_rows[:, :slab_width]) * pre_rows[:, slab_width:]).astype(
        jnp.bfloat16
    )
    part_rows = jnp.dot(hidden_rows, outer_use, preferred_element_type=jnp.float32).astype(
        jnp.bfloat16
    )
    return part_rows.reshape(received.shape)


def expert_back(inner_use, outer_use, rows_flat, grad_flat):
    pre_rows = jnp.dot(rows_flat, inner_use, preferred_element_type=jnp.float32)
    slab_width = outer_use.shape[0]
    gate_pre = pre_rows[:, :slab_width]
    up_pre = pre_rows[:, slab_width:]
    sigma = jax.nn.sigmoid(gate_pre)
    swish = gate_pre * sigma
    hidden_rows = (swish * up_pre).astype(jnp.bfloat16)
    grad_hidden = jnp.dot(grad_flat, outer_use.T, preferred_element_type=jnp.float32)
    grad_gate = grad_hidden * up_pre * sigma * (1.0 + gate_pre * (1.0 - sigma))
    grad_up = grad_hidden * swish
    grad_pre = jnp.concatenate([grad_gate, grad_up], 1).astype(jnp.bfloat16)
    grad_in = jnp.dot(grad_pre, inner_use.T, preferred_element_type=jnp.float32).astype(
        jnp.bfloat16
    )
    return (hidden_rows, grad_pre, grad_in)


def per_device(
    tokens,
    segment_ids,
    routes,
    query_weight,
    key_value_weight,
    output_weight,
    router_weight,
    gain_before,
    gain_middle,
    inner_weight,
    outer_weight,
    cotangent,
):
    sequence_count, resident_rows, model_width = tokens.shape
    token_count = sequence_count * resident_rows
    experts = router_weight.shape[1]
    copies = lax.axis_size("fsdp") // experts
    capacity = 3 * token_count // 8
    seg_all = lax.all_gather(segment_ids, "fsdp", axis=1, tiled=True)
    seq_length = seg_all.shape[1]
    key_tile_block = min(256, seq_length)
    positions = lax.axis_index("fsdp") * resident_rows + jnp.arange(resident_rows, dtype=jnp.int32)
    block_masks = [
        mask_for(seg_all, segment_ids, positions, offset, key_tile_block)
        for offset in range(0, seq_length, key_tile_block)
    ]
    start_rows = tokens.reshape(token_count, model_width).astype(jnp.float32)
    route_flat = routes.reshape(token_count * 2)
    picks = route_flat[:, None] == jnp.arange(experts, dtype=jnp.int32)[None, :]
    marks = picks.astype(jnp.int32)
    slot_index = route_flat * capacity + jnp.sum((jnp.cumsum(marks, 0) - marks) * marks, 1)
    chosen_mask = picks.reshape(token_count, 2, experts)

    def layer_weights():
        return (
            lax.all_gather(query_weight, ("dp", "fsdp"), axis=0, tiled=True),
            lax.all_gather(key_value_weight, ("dp", "fsdp"), axis=0, tiled=True),
            lax.all_gather(output_weight, ("dp", "fsdp"), axis=1, tiled=True),
            lax.all_gather(router_weight, ("dp", "fsdp"), axis=0, tiled=True),
            lax.all_gather(gain_before, ("dp", "fsdp"), axis=0, tiled=True),
            lax.all_gather(gain_middle, ("dp", "fsdp"), axis=0, tiled=True),
        )

    def expert_weights():
        inner_full, outer_full = (
            lax.all_gather(inner_weight, "dp", axis=0, tiled=True),
            lax.all_gather(outer_weight, "dp", axis=1, tiled=True),
        )
        return (inner_full.reshape(model_width, -1), outer_full)

    def attention_front(weights):
        normed, unit_rows, factor = normalize(start_rows, weights[4])
        normed_low = normed.astype(jnp.bfloat16)
        query_matrix = jnp.dot(normed_low, weights[0], preferred_element_type=jnp.float32).astype(
            jnp.bfloat16
        )
        query_matrix = query_matrix.reshape(
            sequence_count,
            resident_rows,
            KEY_VALUE_HEADS,
            QUERY_HEADS // KEY_VALUE_HEADS,
            HEAD_SIZE,
        )
        key_value_rows = jnp.dot(normed_low, weights[1], preferred_element_type=jnp.float32).astype(
            jnp.bfloat16
        )
        gathered = lax.all_gather(
            key_value_rows.reshape(sequence_count, resident_rows, -1), "fsdp", axis=1, tiled=True
        )
        return (normed_low, unit_rows, factor, query_matrix, gathered)

    def middle_part(weights, mixed_low):
        middle = start_rows + jnp.dot(mixed_low, weights[2], preferred_element_type=jnp.float32)
        expert_in, unit_rows, factor = normalize(middle, weights[5])
        expert_low = expert_in.astype(jnp.bfloat16)
        logits = jnp.dot(
            expert_low.astype(jnp.float32),
            weights[3].astype(jnp.float32),
            precision=HIGHEST_PRECISION,
        )
        return (middle, unit_rows, factor, expert_low, logits)

    def gates_for(logits):
        chosen_logits = jnp.sum(jnp.where(chosen_mask, logits[:, None, :], 0.0), -1)
        return jax.nn.softmax(chosen_logits, -1)

    def to_slots(pair_rows):
        packed = (
            jnp.zeros((experts * capacity, model_width), pair_rows.dtype)
            .at[slot_index]
            .set(pair_rows)
        )
        return jnp.repeat(packed.reshape(experts, capacity, model_width), copies, axis=0)

    def from_slots(returned_rows):
        summed = jnp.sum(
            returned_rows.reshape(experts, copies, capacity, model_width).astype(jnp.float32), 1
        )
        return summed.reshape(experts * capacity, model_width)[slot_index]

    weights = layer_weights()
    inner_all, outer_all = expert_weights()
    normed_low, unit_first, factor_first, query_matrix, gathered = attention_front(weights)
    running_totals = log_totals(query_matrix, gathered, block_masks, key_tile_block)
    mixed_low = attend_values(query_matrix, gathered, block_masks, key_tile_block, running_totals)
    middle, unit_second, factor_second, expert_low, logits = middle_part(weights, mixed_low)
    gates = gates_for(logits)
    sent = to_slots(jnp.repeat(expert_low, 2, axis=0))
    part_rows = expert_forward(
        inner_all, outer_all, lax.all_to_all(sent, "fsdp", split_axis=0, concat_axis=0, tiled=True)
    )
    returned_part = lax.all_to_all(part_rows, "fsdp", split_axis=0, concat_axis=0, tiled=True)
    returned_rows = returned_part
    expert_sum = from_slots(returned_rows).reshape(token_count, 2, model_width)
    block_out = (middle + jnp.sum(gates[..., None] * expert_sum, 1)).astype(jnp.bfloat16)
    grad_out = cotangent.reshape(token_count, model_width).astype(jnp.float32)
    weights = layer_weights()
    inner_use, outer_use = expert_weights()
    normed_low, unit_first, factor_first, query_matrix, gathered = attention_front(weights)
    mixed_low = attend_values(query_matrix, gathered, block_masks, key_tile_block, running_totals)
    middle, unit_second, factor_second, expert_low, logits = middle_part(weights, mixed_low)
    gates = gates_for(logits)
    sent = to_slots(jnp.repeat(expert_low, 2, axis=0))
    grad_sent = to_slots(
        (gates[..., None] * grad_out[:, None, :])
        .astype(jnp.bfloat16)
        .reshape(2 * token_count, model_width)
    )
    rows_in = lax.all_to_all(sent, "fsdp", split_axis=0, concat_axis=0, tiled=True)
    rows_grad = lax.all_to_all(grad_sent, "fsdp", split_axis=0, concat_axis=0, tiled=True)
    row_shape = rows_in.shape
    hidden_flat, grad_pre_flat, grad_in_flat = expert_back(
        inner_use, outer_use, rows_in.reshape(-1, model_width), rows_grad.reshape(-1, model_width)
    )
    part_rows = jnp.dot(hidden_flat, outer_use, preferred_element_type=jnp.float32).astype(
        jnp.bfloat16
    )
    grad_home = lax.all_to_all(
        grad_in_flat.reshape(row_shape), "fsdp", split_axis=0, concat_axis=0, tiled=True
    )
    part_home = lax.all_to_all(
        part_rows.reshape(row_shape), "fsdp", split_axis=0, concat_axis=0, tiled=True
    )
    item_shape = row_shape[:2]
    grad_pre = grad_pre_flat.reshape(item_shape + (-1,))
    hidden_rows = hidden_flat.reshape(item_shape + (-1,))
    expert_sum = from_slots(part_home).reshape(token_count, 2, model_width)
    rows_flat = rows_in.reshape(-1, model_width)
    row_total = rows_flat.shape[0]
    inner_grad_all = jnp.dot(
        rows_flat.T, grad_pre.reshape(row_total, -1), preferred_element_type=jnp.float32
    )
    outer_grad_all = jnp.dot(
        hidden_rows.reshape(row_total, -1).T,
        rows_grad.reshape(row_total, model_width),
        preferred_element_type=jnp.float32,
    )
    inner_grad, outer_grad = (
        lax.psum_scatter(
            inner_grad_all.reshape(model_width, 2, -1).astype(jnp.bfloat16),
            "dp",
            scatter_dimension=0,
            tiled=True,
        ).astype(jnp.float32),
        lax.psum_scatter(
            outer_grad_all.astype(jnp.bfloat16), "dp", scatter_dimension=1, tiled=True
        ).astype(jnp.float32),
    )
    grad_gates = jnp.sum(grad_out[:, None, :] * expert_sum, -1)
    grad_choice = gates * (grad_gates - jnp.sum(gates * grad_gates, -1, keepdims=True))
    grad_logits = jnp.sum(jnp.where(chosen_mask, grad_choice[..., None], 0.0), 1)
    router_grad_all = jnp.dot(
        expert_low.astype(jnp.float32).T, grad_logits, precision=HIGHEST_PRECISION
    )
    grad_expert_in = jnp.sum(from_slots(grad_home).reshape(token_count, 2, model_width), 1)
    grad_expert_in = grad_expert_in + jnp.dot(
        grad_logits, weights[3].astype(jnp.float32).T, precision=HIGHEST_PRECISION
    )
    grad_norm_second, middle_gain_grad = normalize_back(
        grad_expert_in, unit_second, factor_second, weights[5]
    )
    grad_middle = grad_out + grad_norm_second
    grad_branch = grad_middle.astype(jnp.bfloat16)
    output_grad_all = jnp.dot(mixed_low.T, grad_branch, preferred_element_type=jnp.float32)
    mixed_gradient = jnp.dot(grad_branch, weights[2].T, preferred_element_type=jnp.float32).astype(
        jnp.bfloat16
    )
    mixed_gradient = mixed_gradient.reshape(
        sequence_count, resident_rows, KEY_VALUE_HEADS, QUERY_HEADS // KEY_VALUE_HEADS, HEAD_SIZE
    )
    grad_queries, key_terms, delta = attend_back(
        query_matrix, mixed_gradient, gathered, block_masks, key_tile_block, running_totals
    )
    key_grads = lax.psum_scatter(
        key_terms.astype(jnp.bfloat16), "fsdp", scatter_dimension=1, tiled=True
    ).reshape(token_count, -1)
    query_low = grad_queries.reshape(token_count, -1).astype(jnp.bfloat16)
    grad_normed = jnp.dot(query_low, weights[0].T, preferred_element_type=jnp.float32) + jnp.dot(
        key_grads, weights[1].T, preferred_element_type=jnp.float32
    )
    query_grad_all = jnp.dot(normed_low.T, query_low, preferred_element_type=jnp.float32)
    keyval_grad_all = jnp.dot(normed_low.T, key_grads, preferred_element_type=jnp.float32)
    grad_norm_first, before_gain_grad = normalize_back(
        grad_normed, unit_first, factor_first, weights[4]
    )
    tokens_grad = grad_middle + grad_norm_first
    summed_grads = (
        lax.psum_scatter(query_grad_all, ("dp", "fsdp"), scatter_dimension=0, tiled=True),
        lax.psum_scatter(keyval_grad_all, ("dp", "fsdp"), scatter_dimension=0, tiled=True),
        lax.psum_scatter(output_grad_all, ("dp", "fsdp"), scatter_dimension=1, tiled=True),
        lax.psum_scatter(router_grad_all, ("dp", "fsdp"), scatter_dimension=0, tiled=True),
        lax.psum_scatter(before_gain_grad, ("dp", "fsdp"), scatter_dimension=0, tiled=True),
        lax.psum_scatter(middle_gain_grad, ("dp", "fsdp"), scatter_dimension=0, tiled=True),
    )
    return (
        block_out.reshape(sequence_count, resident_rows, model_width),
        tokens_grad.reshape(sequence_count, resident_rows, model_width),
        summed_grads[0],
        summed_grads[1],
        summed_grads[2],
        summed_grads[3],
        summed_grads[4],
        summed_grads[5],
        inner_grad,
        outer_grad,
    )


def contract(left, right, left_axis, right_axis):
    return lax.dot_general(
        left, right, (((left_axis,), (right_axis,)), ((), ())), preferred_element_type=jnp.float32
    )


def unit_of(rows):
    factor = lax.rsqrt(jnp.mean(rows * rows, -1, keepdims=True) + EPSILON)
    return (rows * factor, factor)


def column_as_row(table, lane):
    pick = (lax.broadcasted_iota(jnp.int32, (8, table.shape[1]), 1) == lane).astype(jnp.bfloat16)
    return contract(pick, table, 1, 1)[:1]


def split_low(value):
    high = value.astype(jnp.bfloat16)
    return (high, (value - high.astype(jnp.float32)).astype(jnp.bfloat16))


def project_kernel(lane, rows_ref, weight_ref, table_ref, normed_ref, heads_ref, gain):
    @pl.when(pl.program_id(0) == 0)
    def _():
        gain[...] = column_as_row(table_ref[...], lane)

    unit, _ = unit_of(rows_ref[...].astype(jnp.float32))
    normed = (unit * gain[...]).astype(jnp.bfloat16)
    normed_ref[...] = normed
    heads = jnp.dot(normed, weight_ref[...], preferred_element_type=jnp.float32)
    heads_ref[0] = heads.T[: heads_ref.shape[1]].astype(jnp.bfloat16)


def project(rows, head_weights, wide, lane, block):
    length, width = rows.shape
    lanes = head_weights.shape[1]
    blocks = length // block
    return pl.pallas_call(
        functools.partial(project_kernel, lane),
        grid=(blocks,),
        in_specs=[
            pl.BlockSpec((block, width), lambda i: (i, 0)),
            pl.BlockSpec((width, lanes), lambda i: (0, 0)),
            pl.BlockSpec((width, 128), lambda i: (0, lanes // 128 - 1)),
        ],
        out_specs=[
            pl.BlockSpec((block, width), lambda i: (i, 0)),
            pl.BlockSpec((1, wide, block), lambda i: (i, 0, 0)),
        ],
        out_shape=[
            jax.ShapeDtypeStruct((length, width), jnp.bfloat16),
            jax.ShapeDtypeStruct((blocks, wide, block), jnp.bfloat16),
        ],
        scratch_shapes=[pltpu.VMEM((1, width), jnp.float32)],
        compiler_params=pltpu.CompilerParams(vmem_limit_bytes=60 * 2**20),
        name="project",
    )(rows, head_weights, head_weights)


def beside(rows, block, heads):
    return jnp.concatenate([rows[h * HEAD_SIZE : (h + 1) * HEAD_SIZE] for h in range(heads)], 1)


def attend_kernel(spans, q_ref, heads_ref, segr_ref, segc_ref, low_ref, mixed_ref, totals_ref):
    step = pl.program_id(0)
    block = q_ref.shape[2]
    heads = QUERY_HEADS // KEY_VALUE_HEADS
    share = heads * HEAD_SIZE
    queries = beside(q_ref[0, :share, :] * jnp.bfloat16(HEAD_SIZE ** (-0.5)), block, heads)
    seg_row = segr_ref[...]

    def scores_of(j):
        return contract(heads_ref[j, share : share + HEAD_SIZE, :], queries, 0, 0)

    def same_doc(j):
        return segc_ref[pl.ds(pl.multiple_of(j * block, block), block), :] == seg_row

    def fold(span, scores, carry):
        top, total, out = carry
        values = jnp.concatenate(
            [heads_ref[j, share + HEAD_SIZE : share + 2 * HEAD_SIZE, :] for j in span], 1
        )
        new_top = jnp.maximum(top, jnp.max(scores, 0, keepdims=True))
        probs = jnp.exp(scores - new_top)
        decay = jnp.exp(top - new_top)
        total = total * decay + jnp.sum(probs, 0, keepdims=True)
        out = out * decay + jnp.dot(
            values, probs.astype(jnp.bfloat16), preferred_element_type=jnp.float32
        )
        return (new_top, total, out)

    def masked(j, carry):
        allowed = jnp.concatenate([same_doc(j)] * heads, 1)
        return fold([j], jnp.where(allowed, scores_of(j), NEGATIVE_LARGE), carry)

    columns = heads * block
    carry = (
        jnp.full((1, columns), NEGATIVE_LARGE, jnp.float32),
        jnp.zeros((1, columns), jnp.float32),
        jnp.zeros((HEAD_SIZE, columns), jnp.float32),
    )
    first, full = spans[0, step], spans[1, step]
    carry = lax.fori_loop(first, full, masked, carry)
    pairs = (step - full) // 2

    def whole_pair(p, kept):
        j = full + 2 * p
        return fold([j, j + 1], jnp.concatenate([scores_of(j), scores_of(j + 1)], 0), kept)

    carry = lax.fori_loop(0, pairs, whole_pair, carry)
    carry = lax.fori_loop(
        full + 2 * pairs, step, lambda j, kept: fold([j], scores_of(j), kept), carry
    )
    key_spot = lax.broadcasted_iota(jnp.int32, (block, block), 0)
    query_spot = lax.broadcasted_iota(jnp.int32, (block, block), 1)
    allowed = same_doc(step) & (key_spot <= query_spot)
    allowed = jnp.concatenate([allowed] * heads, 1)
    top, total, out = fold([step], jnp.where(allowed, scores_of(step), NEGATIVE_LARGE), carry)
    out = out / total
    totals = top + jnp.log(total)
    for h in range(heads):
        part = out[:, h * block : (h + 1) * block]
        mixed_ref[0, h * HEAD_SIZE : (h + 1) * HEAD_SIZE, :] = part
        low_ref[0, h * HEAD_SIZE : (h + 1) * HEAD_SIZE, :] = part.astype(jnp.bfloat16)
        totals_ref[0, h : h + 1, :] = totals[:, h * block : (h + 1) * block]


def attend(spans, projected, seg_row, seg_col):
    blocks, wide, block = projected.shape
    share = wide - 2 * HEAD_SIZE
    length = blocks * block
    each = lambda height: pl.BlockSpec((1, height, block), lambda i, spans: (i, 0, 0))
    return pl.pallas_call(
        attend_kernel,
        grid_spec=pltpu.PrefetchScalarGridSpec(
            num_scalar_prefetch=1,
            grid=(blocks,),
            in_specs=[
                pl.BlockSpec((1, wide, block), lambda i, spans: (i, 0, 0)),
                pl.BlockSpec((blocks, wide, block), lambda i, spans: (0, 0, 0)),
                pl.BlockSpec((1, block), lambda i, spans: (0, i)),
                pl.BlockSpec((length, 1), lambda i, spans: (0, 0)),
            ],
            out_specs=[each(share), each(share), each(8)],
        ),
        out_shape=[
            jax.ShapeDtypeStruct((blocks, share, block), jnp.bfloat16),
            jax.ShapeDtypeStruct((blocks, share, block), jnp.float32),
            jax.ShapeDtypeStruct((blocks, 8, block), jnp.float32),
        ],
        compiler_params=pltpu.CompilerParams(vmem_limit_bytes=40 * 2**20),
        name="attend",
    )(spans, projected, projected, seg_row, seg_col)


def attend_back_kernel(
    spans, q_ref, g_ref, heads_ref, segr_ref, segc_ref, mixed_ref, totals_ref,
    blocks_ref, line_ref, dk_sum, dv_sum,
):
    step = pl.program_id(0)
    blocks, _, block = heads_ref.shape
    heads = QUERY_HEADS // KEY_VALUE_HEADS
    share = heads * HEAD_SIZE
    queries = beside(q_ref[0, :share, :] * jnp.bfloat16(HEAD_SIZE ** (-0.5)), block, heads)
    grads = beside(g_ref[0], block, heads)
    delta = jnp.sum(
        grads.astype(jnp.float32) * beside(mixed_ref[0], block, heads), 0, keepdims=True
    )
    totals = jnp.concatenate([totals_ref[0, h : h + 1, :] for h in range(heads)], 1)
    seg_row = segr_ref[...]

    @pl.when(step == 0)
    def _():
        dk_sum[...] = jnp.zeros_like(dk_sum)
        dv_sum[...] = jnp.zeros_like(dv_sum)

    def turn(j, query_sum, allowed):
        keys = heads_ref[j, share : share + HEAD_SIZE, :]
        values = heads_ref[j, share + HEAD_SIZE : share + 2 * HEAD_SIZE, :]
        probs = jnp.exp(contract(keys, queries, 0, 0) - totals)
        if allowed is not None:
            probs = jnp.where(jnp.concatenate([allowed] * heads, 1), probs, 0.0)
        grad_scores = (probs * (contract(values, grads, 0, 0) - delta)).astype(jnp.bfloat16)
        dv_sum[j] += contract(grads, probs.astype(jnp.bfloat16), 1, 1)
        dk_sum[j] += contract(queries, grad_scores, 1, 1)
        return query_sum + jnp.dot(keys, grad_scores, preferred_element_type=jnp.float32)

    def same_doc(j):
        return segc_ref[pl.ds(pl.multiple_of(j * block, block), block), :] == seg_row

    query_sum = jnp.zeros((HEAD_SIZE, heads * block), jnp.float32)
    first, full = spans[0, step], spans[1, step]
    query_sum = lax.fori_loop(first, full, lambda j, c: turn(j, c, same_doc(j)), query_sum)
    pairs = (step - full) // 2

    def whole_pair(p, kept):
        j = full + 2 * p
        return turn(j + 1, turn(j, kept, None), None)

    query_sum = lax.fori_loop(0, pairs, whole_pair, query_sum)
    query_sum = lax.fori_loop(
        full + 2 * pairs, step, lambda j, c: turn(j, c, None), query_sum
    )
    key_spot = lax.broadcasted_iota(jnp.int32, (block, block), 0)
    query_spot = lax.broadcasted_iota(jnp.int32, (block, block), 1)
    query_sum = turn(step, query_sum, same_doc(step) & (key_spot <= query_spot))
    query_sum = (query_sum * HEAD_SIZE ** (-0.5)).astype(jnp.bfloat16)

    def spread(j, at, size, value):
        blocks_ref[j, at : at + size, :] = value
        there = pl.ds(pl.multiple_of(j * block, block), block)
        line_ref[at : at + size, there] = value

    for h in range(heads):
        spread(step, h * HEAD_SIZE, HEAD_SIZE, query_sum[:, h * block : (h + 1) * block])

    @pl.when(step == pl.num_programs(0) - 1)
    def _():
        for j in range(blocks):
            spread(j, share, HEAD_SIZE, dk_sum[j].astype(jnp.bfloat16))
            spread(j, share + HEAD_SIZE, HEAD_SIZE, dv_sum[j].astype(jnp.bfloat16))


def attend_backward(spans, projected, grads, seg_row, seg_col, mixed, totals):
    blocks, wide, block = projected.shape
    share = wide - 2 * HEAD_SIZE
    length = blocks * block
    each = lambda height: pl.BlockSpec((1, height, block), lambda i, spans: (i, 0, 0))
    return pl.pallas_call(
        attend_back_kernel,
        grid_spec=pltpu.PrefetchScalarGridSpec(
            num_scalar_prefetch=1,
            grid=(blocks,),
            in_specs=[
                pl.BlockSpec((1, wide, block), lambda i, spans: (i, 0, 0)),
                each(share),
                pl.BlockSpec((blocks, wide, block), lambda i, spans: (0, 0, 0)),
                pl.BlockSpec((1, block), lambda i, spans: (0, i)),
                pl.BlockSpec((length, 1), lambda i, spans: (0, 0)),
                each(share),
                each(8),
            ],
            out_specs=[
                pl.BlockSpec((blocks, wide, block), lambda i, spans: (0, 0, 0)),
                pl.BlockSpec((wide, length), lambda i, spans: (0, 0)),
            ],
            scratch_shapes=[
                pltpu.VMEM((blocks, HEAD_SIZE, block), jnp.float32),
                pltpu.VMEM((blocks, HEAD_SIZE, block), jnp.float32),
            ],
        ),
        out_shape=[
            jax.ShapeDtypeStruct((blocks, wide, block), jnp.bfloat16),
            jax.ShapeDtypeStruct((wide, length), jnp.bfloat16),
        ],
        compiler_params=pltpu.CompilerParams(vmem_limit_bytes=40 * 2**20),
        name="attend_backward",
    )(spans, projected, grads, projected, seg_row, seg_col, mixed, totals)


def hits(slots, height):
    spot = lax.broadcasted_iota(jnp.int32, (height, slots.shape[1]), 0)
    return (spot == slots[0:1, :], spot == slots[1:2, :])


def spread_kernel(slots_ref, rows_ref, *out_refs):
    size = out_refs[0].shape[0]
    first, second = hits(slots_ref[...], size * len(out_refs))
    chosen = (first | second).astype(jnp.bfloat16)
    for k, out_ref in enumerate(out_refs):
        out_ref[...] = jnp.dot(
            chosen[k * size : (k + 1) * size], rows_ref[...], preferred_element_type=jnp.float32
        ).astype(jnp.bfloat16)


def spread_rows(slots, rows, size, blocks):
    return pl.pallas_call(
        spread_kernel,
        out_shape=[jax.ShapeDtypeStruct((size, rows.shape[1]), jnp.bfloat16)] * blocks,
        compiler_params=pltpu.CompilerParams(vmem_limit_bytes=40 * 2**20),
        name="spread_rows",
    )(slots, rows)


def middle_kernel(
    lane, router_lane, start_ref, mixed_ref, weight_ref, table_ref, slots_ref, routes_ref,
    middle_ref, sent_ref, gates_ref,
):
    table = table_ref[...]
    middle = start_ref[...].astype(jnp.float32) + contract(mixed_ref[...].T, weight_ref[...], 1, 1)
    middle_ref[...] = middle
    unit, _ = unit_of(middle)
    expert_low = (unit * column_as_row(table, lane)).astype(jnp.bfloat16)
    first, second = hits(slots_ref[...], sent_ref.shape[0])
    sent_ref[...] = jnp.dot(
        (first | second).astype(jnp.bfloat16), expert_low, preferred_element_type=jnp.float32
    ).astype(jnp.bfloat16)
    logits = jnp.dot(expert_low, table, preferred_element_type=jnp.float32).T
    spot = lax.broadcasted_iota(jnp.int32, logits.shape, 0) - router_lane
    chosen = [
        jnp.sum(jnp.where(spot == routes_ref[c : c + 1, :], logits, 0.0), 0, keepdims=True)
        for c in range(2)
    ]
    top = jnp.maximum(chosen[0], chosen[1])
    parts = [jnp.exp(value - top) for value in chosen]
    gates_ref[...] = jnp.concatenate([part / (parts[0] + parts[1]) for part in parts], 0)


def middle_part(start, mixed, weight, head_weights, slots, routes, lane, router_lane, height):
    rows, width = start.shape
    lanes = head_weights.shape[1]
    whole = lambda shape: pl.BlockSpec(shape, lambda i: (0, 0))
    return pl.pallas_call(
        functools.partial(middle_kernel, lane, router_lane),
        grid=(1,),
        in_specs=[
            whole(start.shape),
            whole(mixed.shape),
            whole(weight.shape),
            pl.BlockSpec((width, 128), lambda i: (0, lanes // 128 - 1)),
            whole(slots.shape),
            whole(routes.shape),
        ],
        out_specs=[whole((rows, width)), whole((height, width)), whole((2, rows))],
        out_shape=[
            jax.ShapeDtypeStruct((rows, width), jnp.float32),
            jax.ShapeDtypeStruct((height, width), jnp.bfloat16),
            jax.ShapeDtypeStruct((2, rows), jnp.float32),
        ],
        compiler_params=pltpu.CompilerParams(vmem_limit_bytes=60 * 2**20),
        name="middle",
    )(start, mixed, weight, head_weights, slots, routes)


def block_place(own_ref, axis, k, size):
    return pl.ds(pl.multiple_of(jnp.bitwise_xor(own_ref[axis], k) * size, size), size)


def assemble_weights(own_ref, part_refs, gate, up, outer):
    count = len(part_refs) // 3
    for k in range(count):
        size = part_refs[k].shape[0]
        place = block_place(own_ref, 1, k, size)
        gate[place, :] = part_refs[k][...]
        up[place, :] = part_refs[count + k][...]
        outer[:, place] = part_refs[2 * count + k][...]


def expert_kernel(router_lane, blocks, own_ref, rows_ref, *refs):
    weight_refs, (table_ref, other_ref) = refs[:12], refs[12:14]
    pre_gate_ref, pre_up_ref, hidden_ref, gates_ref = refs[14:18]
    part_refs, (part_sum, gate, up, outer) = refs[18 : 18 + blocks], refs[18 + blocks :]
    step = pl.program_id(0)
    size = part_refs[0].shape[0]
    rows = rows_ref[...]
    assemble_weights(own_ref, weight_refs, gate, up, outer)

    @pl.when(step == 0)
    def _():
        lane = lax.broadcasted_iota(jnp.int32, (rows.shape[0], 128), 1) - router_lane
        logits = jnp.dot(rows, table_ref[...], preferred_element_type=jnp.float32)
        own = jnp.sum(jnp.where(lane == own_ref[0], logits, 0.0), 1, keepdims=True)
        other = jnp.sum(jnp.where(lane == other_ref[...], logits, 0.0), 1, keepdims=True)
        top = jnp.maximum(own, other)
        own, other = jnp.exp(own - top), jnp.exp(other - top)
        gates_ref[:, 0:1] = own / (own + other)
        gates_ref[:, 1:2] = other / (own + other)
        part_sum[...] = jnp.zeros_like(part_sum)

    gate_pre = jnp.dot(rows, gate[...], preferred_element_type=jnp.float32)
    up_pre = jnp.dot(rows, up[...], preferred_element_type=jnp.float32)
    pre_gate_ref[...] = gate_pre
    pre_up_ref[...] = up_pre
    hidden = (gate_pre / (1.0 + jnp.exp(-gate_pre)) * up_pre).astype(jnp.bfloat16)
    hidden_ref[...] = hidden
    part_sum[...] += jnp.dot(hidden, outer[...], preferred_element_type=jnp.float32)

    @pl.when(step == pl.num_programs(0) - 1)
    def _():
        for k, ref in enumerate(part_refs):
            ref[...] = part_sum[block_place(own_ref, 0, k, size), :].astype(jnp.bfloat16)


def weight_specs(inner, outer, tile, steps):
    size = inner[0].shape[0]
    return (
        [pl.BlockSpec((size, tile), lambda i, own: (0, i))] * len(inner)
        + [pl.BlockSpec((size, tile), lambda i, own: (0, steps + i))] * len(inner)
        + [pl.BlockSpec((tile, size), lambda i, own: (i, 0))] * len(outer)
    )


def expert_forward_pass(own, rows, inner, outer, head_weights, other, router_lane, tile, blocks):
    height, width = rows.shape
    units = outer[0].shape[0]
    steps = units // tile
    lanes = head_weights.shape[1]
    whole = lambda shape: pl.BlockSpec(shape, lambda i, own: (0, 0))
    tiled = lambda rows, off: pl.BlockSpec((rows, tile), lambda i, own: (0, off + i))
    shape = jax.ShapeDtypeStruct
    low, f32 = jnp.bfloat16, jnp.float32
    outcome = pl.pallas_call(
        functools.partial(expert_kernel, router_lane, blocks),
        grid_spec=pltpu.PrefetchScalarGridSpec(
            num_scalar_prefetch=1,
            grid=(steps,),
            in_specs=[whole(rows.shape)]
            + weight_specs(inner, outer, tile, steps)
            + [
                pl.BlockSpec((width, 128), lambda i, own: (0, lanes // 128 - 1)),
                whole(other.shape),
            ],
            out_specs=[tiled(height, 0)] * 3
            + [whole((height, 128))]
            + [whole((height // blocks, width))] * blocks,
            scratch_shapes=[
                pltpu.VMEM((height, width), f32),
                pltpu.VMEM((width, tile), low),
                pltpu.VMEM((width, tile), low),
                pltpu.VMEM((tile, width), low),
            ],
        ),
        out_shape=[shape((height, units), f32)] * 2
        + [shape((height, units), low), shape((height, 128), f32)]
        + [shape((height // blocks, width), low)] * blocks,
        compiler_params=pltpu.CompilerParams(vmem_limit_bytes=56 * 2**20),
        name="expert",
    )(own, rows, *inner, *inner, *outer, head_weights, other)
    return outcome[:4], list(outcome[4:])


def expert_back_kernel(router_lane, blocks, own_ref, *refs):
    cot_refs, part_refs, refs = refs[:blocks], refs[blocks : 2 * blocks], refs[2 * blocks :]
    rows_ref, gates_ref, pre_gate_ref, pre_up_ref = refs[:4]
    weight_refs, refs = refs[4:16], refs[16:]
    table_ref, other_ref, grad_gate_ref, grad_up_ref, grad_ref, back_ref, router_ref = refs[:7]
    cot, back_sum, gate, up, outer = refs[7:]
    step = pl.program_id(0)
    assemble_weights(own_ref, weight_refs, gate, up, outer)
    size = cot_refs[0].shape[0]
    gates = gates_ref[...]

    @pl.when(step == 0)
    def _():
        for k, ref in enumerate(cot_refs):
            cot[block_place(own_ref, 0, k, size), :] = ref[...]
        grad_ref[...] = (gates[:, 0:1] * cot[...].astype(jnp.float32)).astype(jnp.bfloat16)
        back_sum[...] = jnp.zeros_like(back_sum)

    gate_pre, up_pre = pre_gate_ref[...], pre_up_ref[...]
    grad_hidden = contract(grad_ref[...], outer[...], 1, 1)
    sigma = 1.0 / (1.0 + jnp.exp(-gate_pre))
    grad_gate = grad_hidden * up_pre * sigma * (1.0 + gate_pre * (1.0 - sigma))
    grad_gate = grad_gate.astype(jnp.bfloat16)
    grad_up = (grad_hidden * (gate_pre * sigma)).astype(jnp.bfloat16)
    grad_gate_ref[...] = grad_gate
    grad_up_ref[...] = grad_up
    back_sum[...] += contract(grad_gate, gate[...], 1, 1) + contract(grad_up, up[...], 1, 1)

    @pl.when(step == pl.num_programs(0) - 1)
    def _():
        table = table_ref[...]
        total = jnp.zeros(router_ref.shape, jnp.float32)
        for k in range(blocks):
            place = block_place(own_ref, 0, k, size)
            grad_gates = jnp.sum(
                cot_refs[k][...].astype(jnp.float32) * part_refs[k][...].astype(jnp.float32),
                1,
                keepdims=True,
            )
            gates_k = gates_ref[place, :]
            lane_k = lax.broadcasted_iota(jnp.int32, (size, 128), 1) - router_lane
            sides_k = (lane_k == own_ref[0]).astype(jnp.float32) - (
                lane_k == other_ref[place, :]
            ).astype(jnp.float32)
            high, rest = split_low(gates_k[:, 0:1] * gates_k[:, 1:2] * grad_gates * sides_k)
            routed = contract(high, table, 1, 1) + contract(rest, table, 1, 1)
            back = back_sum[place, :].astype(jnp.bfloat16).astype(jnp.float32)
            back_ref[place, :] = (back + routed).astype(jnp.bfloat16)
            rows_k = rows_ref[place, :]
            total = total + contract(high, rows_k, 0, 0) + contract(rest, rows_k, 0, 0)
        router_ref[...] = total


def expert_backward_pass(
    own, cot_blocks, part_blocks, rows, gates, pre_gate, pre_up, inner, outer, head_weights, other,
    router_lane, tile,
):
    height, width = rows.shape
    units = outer[0].shape[0]
    steps = units // tile
    lanes = head_weights.shape[1]
    blocks = len(cot_blocks)
    whole = lambda shape: pl.BlockSpec(shape, lambda i, own: (0, 0))
    tiled = lambda rows, off: pl.BlockSpec((rows, tile), lambda i, own: (0, off + i))
    low, f32 = jnp.bfloat16, jnp.float32
    return pl.pallas_call(
        functools.partial(expert_back_kernel, router_lane, blocks),
        grid_spec=pltpu.PrefetchScalarGridSpec(
            num_scalar_prefetch=1,
            grid=(steps,),
            in_specs=[whole((height // blocks, width))] * (2 * blocks)
            + [
                whole(rows.shape),
                whole(gates.shape),
                tiled(height, 0),
                tiled(height, 0),
            ]
            + weight_specs(inner, outer, tile, steps)
            + [
                pl.BlockSpec((width, 128), lambda i, own: (0, lanes // 128 - 1)),
                whole(other.shape),
            ],
            out_specs=[
                tiled(height, 0),
                tiled(height, 0),
                whole((height, width)),
                whole((height, width)),
                whole((128, width)),
            ],
            scratch_shapes=[
                pltpu.VMEM((height, width), low),
                pltpu.VMEM((height, width), f32),
                pltpu.VMEM((width, tile), low),
                pltpu.VMEM((width, tile), low),
                pltpu.VMEM((tile, width), low),
            ],
        ),
        out_shape=[
            jax.ShapeDtypeStruct((height, units), low),
            jax.ShapeDtypeStruct((height, units), low),
            jax.ShapeDtypeStruct((height, width), low),
            jax.ShapeDtypeStruct((height, width), low),
            jax.ShapeDtypeStruct((128, width), f32),
        ],
        compiler_params=pltpu.CompilerParams(vmem_limit_bytes=56 * 2**20),
        name="expert_backward",
    )(
        own, *cot_blocks, *part_blocks, rows, gates, pre_gate, pre_up, *inner, *inner, *outer,
        head_weights, other,
    )


def back_kernel(
    lane, middle_ref, cot_ref, home_ref, weight_ref, table_ref, slots_ref,
    grad_ref, branch_ref, gain_ref, mixed_ref,
):
    first, second = hits(slots_ref[...], home_ref.shape[0])
    grad_in = contract((first | second).astype(jnp.bfloat16), home_ref[...], 0, 0)
    unit, factor = unit_of(middle_ref[...])
    gain_ref[...] = jnp.sum(grad_in * unit, 0, keepdims=True)
    scaled = grad_in * column_as_row(table_ref[...], lane)
    inner_part = factor * (scaled - unit * jnp.mean(scaled * unit, -1, keepdims=True))
    grad_middle = cot_ref[...].astype(jnp.float32) + inner_part
    grad_ref[...] = grad_middle
    branch = grad_middle.astype(jnp.bfloat16)
    branch_ref[...] = branch
    mixed = jnp.dot(branch, weight_ref[...], preferred_element_type=jnp.float32)
    mixed_ref[...] = mixed.T.astype(jnp.bfloat16)


def back_part(middle, cot, home, weight, head_weights, slots, lane):
    rows, width = middle.shape
    lanes = head_weights.shape[1]
    whole = lambda shape: pl.BlockSpec(shape, lambda i: (0, 0))
    return pl.pallas_call(
        functools.partial(back_kernel, lane),
        grid=(1,),
        in_specs=[
            whole((rows, width)),
            whole((rows, width)),
            whole(home.shape),
            whole(weight.shape),
            pl.BlockSpec((width, 128), lambda i: (0, lanes // 128 - 1)),
            whole(slots.shape),
        ],
        out_specs=[
            whole((rows, width)),
            whole((rows, width)),
            whole((1, width)),
            whole((weight.shape[1], rows)),
        ],
        out_shape=[
            jax.ShapeDtypeStruct((rows, width), jnp.float32),
            jax.ShapeDtypeStruct((rows, width), jnp.bfloat16),
            jax.ShapeDtypeStruct((1, width), jnp.float32),
            jax.ShapeDtypeStruct((weight.shape[1], rows), jnp.bfloat16),
        ],
        compiler_params=pltpu.CompilerParams(vmem_limit_bytes=48 * 2**20),
        name="back",
    )(middle, cot, home, weight, head_weights, slots)


def weight_kernel(place, normed_ref, grads_ref, router_ref, gain_ref, out_ref):
    total = jnp.dot(grads_ref[...], normed_ref[...], preferred_element_type=jnp.float32)
    wide, span = total.shape
    rest = jnp.zeros((out_ref.shape[2] - wide - router_ref.shape[0] - 8, span), jnp.float32)
    gain = jnp.concatenate([gain_ref[...], jnp.zeros((7, span), jnp.float32)], 0)
    out_ref[0] = jnp.concatenate([total, router_ref[...], gain, rest], 0).T.astype(jnp.bfloat16)


def weight_terms(place, normed, grads, router, gain, router_lane, experts, lanes, parts):
    length, width = normed.shape
    wide = grads.shape[0]
    span = width // parts
    near = lambda row: lambda k, place: (row, jnp.bitwise_xor(place[0], k))
    return pl.pallas_call(
        weight_kernel,
        grid_spec=pltpu.PrefetchScalarGridSpec(
            num_scalar_prefetch=1,
            grid=(parts,),
            in_specs=[
                pl.BlockSpec((length, span), near(0)),
                pl.BlockSpec((wide, length), lambda k, place: (0, 0)),
                pl.BlockSpec((experts, span), near(router_lane // experts)),
                pl.BlockSpec((1, span), near(0)),
            ],
            out_specs=pl.BlockSpec((1, span, lanes), lambda k, place: (k, 0, 0)),
        ),
        out_shape=jax.ShapeDtypeStruct((parts, span, lanes), jnp.bfloat16),
        compiler_params=pltpu.CompilerParams(vmem_limit_bytes=40 * 2**20),
        name="weight_terms",
    )(place, normed, grads, router, gain)


def tokens_back_kernel(
    lane, start_ref, middle_ref, grads_ref, weight_ref, table_ref, out_ref, total
):
    step = pl.program_id(0)

    @pl.when(step == 0)
    def _():
        total[...] = jnp.zeros_like(total)

    grads = jnp.concatenate([grads_ref[0], grads_ref[1]], 0).T
    total[...] += contract(grads, weight_ref[...], 1, 1)

    @pl.when(step == pl.num_programs(0) - 1)
    def _():
        unit, factor = unit_of(start_ref[...].astype(jnp.float32))
        scaled = total[...] * column_as_row(table_ref[...], lane)
        inner_part = factor * (scaled - unit * jnp.mean(scaled * unit, -1, keepdims=True))
        out_ref[...] = middle_ref[...] + inner_part


def tokens_back(start, grad_middle, grads, weight, head_weights, lane):
    rows, width = start.shape
    count, cols, _ = grads.shape
    lanes = head_weights.shape[1]
    whole = lambda shape: pl.BlockSpec(shape, lambda i: (0, 0))
    return pl.pallas_call(
        functools.partial(tokens_back_kernel, lane),
        grid=(count // 2,),
        in_specs=[
            whole(start.shape),
            whole(grad_middle.shape),
            pl.BlockSpec((2, cols, rows), lambda i: (i, 0, 0)),
            pl.BlockSpec((width, 2 * cols), lambda i: (0, i)),
            pl.BlockSpec((width, 128), lambda i: (0, lanes // 128 - 1)),
        ],
        out_specs=whole((rows, width)),
        out_shape=jax.ShapeDtypeStruct((rows, width), jnp.float32),
        scratch_shapes=[pltpu.VMEM((rows, width), jnp.float32)],
        compiler_params=pltpu.CompilerParams(vmem_limit_bytes=56 * 2**20),
        name="tokens_back",
    )(start, grad_middle, grads, weight, head_weights)


def mixture_kernel(slots_ref, gates_ref, middle_ref, *refs):
    part_refs, out_ref = refs[:-1], refs[-1]
    size = part_refs[0].shape[0]
    first, second = hits(slots_ref[...], size * len(part_refs))
    total = middle_ref[...]
    shares = gates_ref[...]
    for _ in range(3):
        piece = shares.astype(jnp.bfloat16)
        shares = shares - piece.astype(jnp.float32)
        piece = piece.astype(jnp.float32)
        weights = jnp.where(first, piece[0:1], 0.0) + jnp.where(second, piece[1:2], 0.0)
        weights = weights.astype(jnp.bfloat16)
        for k, ref in enumerate(part_refs):
            total = total + contract(weights[k * size : (k + 1) * size], ref[...], 0, 0)
    out_ref[...] = total.astype(jnp.bfloat16)


def mixture(slots, gates, middle, parts):
    return pl.pallas_call(
        mixture_kernel,
        out_shape=jax.ShapeDtypeStruct(middle.shape, jnp.bfloat16),
        compiler_params=pltpu.CompilerParams(vmem_limit_bytes=40 * 2**20),
        name="mixture",
    )(slots, gates, middle, *parts)


def weight_grads_kernel(
    share, home_ref, query_weight_ref, keyval_weight_ref,
    query_ref, keyval_ref, router_ref, gains_ref,
):
    count = home_ref.shape[0]
    cols = share + 2 * HEAD_SIZE
    half = count * HEAD_SIZE
    experts = router_ref.shape[1]
    small = jnp.zeros((home_ref.shape[1], home_ref.shape[2] - cols), jnp.float32)
    for e in range(count):
        part = home_ref[e].astype(jnp.float32)
        query_ref[:, e * share : (e + 1) * share] = part[:, :share]
        at = e * HEAD_SIZE
        keyval_ref[:, at : at + HEAD_SIZE] = part[:, share : share + HEAD_SIZE]
        keyval_ref[:, half + at : half + at + HEAD_SIZE] = part[:, share + HEAD_SIZE : cols]
        small = small + part[:, cols:]
    router_ref[...] = small[:, :experts]
    products = jnp.sum(
        query_ref[...] * query_weight_ref[...].astype(jnp.float32), 1, keepdims=True
    ) + jnp.sum(keyval_ref[...] * keyval_weight_ref[...].astype(jnp.float32), 1, keepdims=True)
    gains_ref[:, 0:1] = products
    gains_ref[:, 1:2] = small[:, experts : experts + 1]


def weight_grads(home, query_weight, keyval_weight, share, experts):
    shape = lambda width: jax.ShapeDtypeStruct((query_weight.shape[0], width), jnp.float32)
    return pl.pallas_call(
        functools.partial(weight_grads_kernel, share),
        out_shape=[
            shape(query_weight.shape[1]),
            shape(keyval_weight.shape[1]),
            shape(experts),
            shape(2),
        ],
        compiler_params=pltpu.CompilerParams(vmem_limit_bytes=40 * 2**20),
        name="weight_grads",
    )(home, query_weight, keyval_weight)


def sum_pairs_kernel(*refs):
    out_ref = refs[-1]
    count = len(refs) // 2
    for side in range(2):
        total = sum(ref[...].astype(jnp.float32) for ref in refs[side * count : (side + 1) * count])
        out_ref[:, side, :] = total


def sum_pairs(first, second, tile):
    rows, width = first[0].shape
    return pl.pallas_call(
        sum_pairs_kernel,
        grid=(rows // tile,),
        in_specs=[pl.BlockSpec((tile, width), lambda i: (i, 0))] * (len(first) + len(second)),
        out_specs=pl.BlockSpec((tile, 2, width), lambda i: (i, 0, 0)),
        out_shape=jax.ShapeDtypeStruct((rows, 2, width), jnp.float32),
        compiler_params=pltpu.CompilerParams(vmem_limit_bytes=40 * 2**20),
        name="sum_pairs",
    )(*first, *second)


def after(values, *earlier):
    return lax.optimization_barrier((values, earlier))[0]


def flip_exchange(block, axis, flip):
    count = lax.axis_size(axis)
    return lax.ppermute(block, axis, [(i, i ^ flip) for i in range(count)])


def swap_near_blocks(blocks, flips):
    return [flip_exchange(blocks[flip], "fsdp", flip) for flip in flips]


def swap_near(block, axis, flips):
    return [flip_exchange(block, axis, flip) for flip in flips]


def in_order(parts, axis):
    stacked = jnp.stack(parts)
    index = lax.axis_index(axis)
    return jnp.stack(
        [
            lax.dynamic_index_in_dim(stacked, jnp.bitwise_xor(index, j), 0, keepdims=False)
            for j in range(len(parts))
        ]
    )


def all_to_all(blocks):
    return lax.all_to_all(blocks, "fsdp", split_axis=0, concat_axis=0, tiled=True)


def gather(block, axis):
    return lax.all_gather(block, axis, axis=0, tiled=True)


def per_device_heads(
    tokens,
    segment_ids,
    routes,
    query_weight,
    key_value_weight,
    output_weight,
    router_weight,
    gain_before,
    gain_middle,
    inner_weight,
    outer_weight,
    cotangent,
):
    f32, low = jnp.float32, jnp.bfloat16
    _, rows, width = tokens.shape
    count = lax.axis_size("fsdp")
    experts = router_weight.shape[1]
    index, group = lax.axis_index("fsdp"), lax.axis_index("dp")
    core = index % 2
    capacity = 3 * rows // 8
    height = experts * capacity
    length = count * rows
    shard = query_weight.shape[0]
    share = QUERY_HEADS // KEY_VALUE_HEADS * HEAD_SIZE
    cols = share + 2 * HEAD_SIZE
    half = KEY_VALUE_HEADS * HEAD_SIZE
    ff = outer_weight.shape[0]
    size = inner_weight.shape[0]

    start_low = tokens.reshape(rows, width)
    cot_low = cotangent.reshape(rows, width)

    route = routes.reshape(rows, 2)
    route_flat = route.reshape(rows * 2)
    picks = route_flat[:, None] == jnp.arange(experts, dtype=jnp.int32)[None, :]
    before = jnp.dot(
        jnp.tril(jnp.ones((rows * 2, rows * 2), low), -1),
        picks.astype(low),
        preferred_element_type=f32,
    )
    rank = jnp.sum(jnp.where(picks, before, 0.0), 1).astype(jnp.int32).reshape(rows, 2)
    route_lines = route.T
    slots = (route * capacity + rank).T
    slots_near = (jnp.bitwise_xor(route, index) * capacity + rank).T
    spots = jnp.arange(height, dtype=jnp.int32)[:, None]
    other_route = jnp.sum(
        jnp.where(slots[0:1] == spots, route_lines[1:2], 0)
        + jnp.where(slots[1:2] == spots, route_lines[0:1], 0),
        1,
    )

    by_head = jnp.concatenate(
        [
            query_weight.reshape(shard, count, share),
            key_value_weight[:, :half].reshape(shard, count, HEAD_SIZE),
            key_value_weight[:, half:].reshape(shard, count, HEAD_SIZE),
        ],
        2,
    )
    lanes = 128 * -(-(cols + 2 + experts) // 128)
    table_lane = lanes - 128
    router_lane = cols - table_lane
    first_lane, second_lane = router_lane + experts, router_lane + experts + 1
    extras = jnp.concatenate([router_weight, gain_before[:, None], gain_middle[:, None]], 1)
    extras = jnp.broadcast_to(extras[None], (count, shard, 2 + experts))
    head_block = jnp.concatenate([by_head.transpose(1, 0, 2), extras], 2)
    head_block = jnp.pad(head_block, ((0, 0), (0, 0), (0, lanes - cols - 2 - experts)))
    seg_line = jnp.broadcast_to(segment_ids.reshape(1, 1, rows), (count, 1, rows)).astype(low)
    seg_line = jnp.pad(seg_line, ((0, 0), (0, 0), (0, lanes - rows)))
    other_line = other_route.reshape(experts, 1, capacity).astype(low)
    other_line = jnp.pad(other_line, ((0, 0), (0, 14), (0, lanes - capacity)))
    head_block = jnp.concatenate([head_block, seg_line, other_line], 1)
    chip = index // 2
    tokens_all = gather(start_low, "fsdp")
    arrived = all_to_all(head_block)

    inner_own = inner_weight.reshape(size, 2 * ff)
    inner_x, inner_y = swap_near(inner_own, "dp", (1, 2))
    outer_x, outer_y = swap_near(outer_weight, "dp", (1, 2))
    arrived, inner_x, inner_y, outer_x, outer_y = after(
        (arrived, inner_x, inner_y, outer_x, outer_y)
    )
    segments = arrived[:, shard, :rows].reshape(length).astype(jnp.int32)
    other_expert = arrived[:, shard + 1, :capacity].reshape(height, 1).astype(jnp.int32)
    head_rows = arrived[:, :shard].reshape(count * shard, lanes)
    head_near = swap_near(head_rows, "dp", (1, 2, 3))
    head_weights = in_order([head_rows] + head_near, "dp").reshape(width, lanes)
    cot_sent = spread_rows(slots_near, cot_low, capacity, experts)

    firsts = segments.reshape(count, rows)
    starts = jnp.sum(segments[None, :] < firsts[:, :1], 1) // rows
    wholes = (jnp.sum(segments[None, :] < firsts[:, -1:], 1) + rows - 1) // rows
    wholes = jnp.minimum(wholes, jnp.arange(count))
    spans = jnp.stack([starts, wholes]).astype(jnp.int32)
    seg_row, seg_col = segments.reshape(1, length), segments.reshape(length, 1)

    by_head_line = by_head.reshape(shard, count * cols)
    tokens_all, cot_sent, head_weights, by_head_line, output_own, spans, seg_row, seg_col = after(
        (
            tokens_all, cot_sent, head_weights, by_head_line, output_weight.T, spans, seg_row,
            seg_col,
        )
    )
    output_all = gather(output_own, ("dp", "fsdp"))
    normed, projected = project(tokens_all, head_weights, cols, first_lane, rows)
    cot_first = swap_near_blocks(cot_sent, (4, 6, 2))
    mixed_head, mixed_exact, totals = attend(spans, projected, seg_row, seg_col)
    mixed_head, cot_first, by_head_line = after((mixed_head, cot_first, by_head_line))
    project_line = gather(by_head_line, "fsdp")
    mixed = all_to_all(mixed_head).reshape(count * share, rows)

    middle, sent, gates = middle_part(
        start_low, mixed, output_all, head_weights, slots, route_lines,
        second_lane, router_lane, height,
    )

    rows_in = all_to_all(sent)
    inner_far = flip_exchange(after(inner_x, sent), "dp", 2)
    outer_far = flip_exchange(after(outer_y, sent), "dp", 1)
    rows_in, cot_sent, project_line, inner_far, outer_far = after(
        (rows_in, cot_sent, project_line, inner_far, outer_far)
    )
    inner_parts = [inner_own, inner_x, inner_y, inner_far]
    outer_parts = [outer_weight, outer_x, outer_y, outer_far]
    project_all = gather(project_line, "dp")
    cot_last = swap_near_blocks(cot_sent, (5, 7, 3, 1))
    own_expert = jnp.stack([index, group]).astype(jnp.int32)
    (pre_gate, pre_up, hidden, slot_gates), parts = expert_forward_pass(
        own_expert, rows_in, inner_parts, outer_parts, head_weights, other_expert,
        router_lane, 256, experts,
    )
    hidden, parts, cot_last = after((hidden, parts, cot_last))
    part_first = swap_near_blocks(parts, (4, 6, 2, 1, 3))
    cot_in = [cot_sent[0], cot_last[3], cot_first[2], cot_last[2]]
    cot_in = cot_in + [cot_first[0], cot_last[0], cot_first[1], cot_last[1]]
    grad_gate, grad_up, grad_in, grad_rows, router_part = expert_backward_pass(
        own_expert, cot_in, parts, rows_in, slot_gates, pre_gate, pre_up, inner_parts, outer_parts,
        head_weights, other_expert, router_lane, 512,
    )
    grad_rows, part_first, grad_gate, grad_up, grad_in = after(
        (grad_rows, part_first, grad_gate, grad_up, grad_in)
    )
    grad_home = all_to_all(grad_rows)

    def cut(value, k):
        return lax.dynamic_slice_in_dim(value, jnp.bitwise_xor(group, k) * size, size, 1)

    rows_near = [cut(rows_in, k) for k in range(4)]
    gate_terms = [contract(near, grad_gate, 0, 0).astype(low) for near in rows_near]
    up_terms = [contract(near, grad_up, 0, 0).astype(low) for near in rows_near]
    near_a, far_a = [flip_exchange(gate_terms[k], "dp", 1) for k in (1, 3)]
    near_b, far_b = [flip_exchange(up_terms[k], "dp", 2) for k in (2, 3)]
    passed_a = (gate_terms[2].astype(f32) + far_a.astype(f32)).astype(low)
    passed_b = (up_terms[1].astype(f32) + far_b.astype(f32)).astype(low)
    outer_term = jnp.concatenate(
        [contract(hidden, grad_in[:, k * size : (k + 1) * size], 0, 0) for k in range(4)]
    ).astype(low)
    grad_home, outer_term, passed_a, passed_b, gate_terms, up_terms, near_a, near_b, project_all = after(
        (
            grad_home, outer_term, passed_a, passed_b, gate_terms, up_terms, near_a, near_b,
            project_all,
        )
    )
    side_a, side_b = flip_exchange(passed_a, "dp", 2), flip_exchange(passed_b, "dp", 1)

    grad_middle, grad_branch, gain_part, mixed_grad = back_part(
        middle, cot_low, grad_home, output_all, head_weights, slots, second_lane
    )
    mixed_grad = all_to_all(mixed_grad.reshape(count, share, rows))

    branch_near = jnp.concatenate([cut(grad_branch, k) for k in range(4)], 1)
    half_width = width // 2

    def half_terms(side):
        heads = lax.dynamic_slice_in_dim(mixed, side * half_width, half_width, 0)
        return contract(branch_near, heads, 0, 1).astype(low)

    from_core = flip_exchange(half_terms(1 - core), "fsdp", 1)
    output_part = half_terms(core).astype(f32) + from_core.astype(f32)
    output_part = output_part.astype(low).reshape(4, size, half_width)
    mixed_grad, output_part, parts, side_a, side_b, outer_term = after(
        (mixed_grad, output_part, parts, side_a, side_b, outer_term)
    )
    outer_sum = lax.psum_scatter(outer_term, "dp", scatter_dimension=0, tiled=True)
    output_near = flip_exchange(output_part[2:], "dp", 2)
    part_last = swap_near_blocks(parts, (5, 7))

    grads_blocks, grads_line = attend_backward(
        spans, projected, mixed_grad, seg_row, seg_col, mixed_exact, totals
    )
    grads_blocks, grads_line, part_last = after((grads_blocks, grads_line, part_last))
    part_home = [parts[0], part_first[3], part_first[2], part_first[4]]
    part_home = part_home + [part_first[0], part_last[0], part_first[1], part_last[1]]
    grad_mine = all_to_all(grads_blocks)
    own_group = group.reshape(1).astype(jnp.int32)
    terms = weight_terms(
        own_group, normed, grads_line, router_part, gain_part, router_lane, experts, lanes, 4
    )
    terms, output_part, output_near, near_a, near_b, part_home = after(
        (terms, output_part, output_near, near_a, near_b, part_home)
    )
    output_sum = output_part[:2].astype(f32) + output_near.astype(f32)
    inner_grad = sum_pairs(
        [gate_terms[0], near_a, side_a], [up_terms[0], near_b, side_b], size // 4
    )
    outer_grad = outer_sum.astype(f32)
    block_out = mixture(slots_near, gates, middle, part_home)
    weights_near = after(
        [flip_exchange(terms[k], "dp", k) for k in range(1, 4)], inner_grad, block_out
    )
    weight_sum = terms[0].astype(f32)
    for near in weights_near:
        weight_sum = weight_sum + near.astype(f32)
    weight_sum, output_passed = after((weight_sum.astype(low), output_sum[1].astype(low)))
    output_side = flip_exchange(output_passed, "dp", 1)
    tokens_grad = tokens_back(
        start_low, grad_middle, after(grad_mine, inner_grad, outer_grad, block_out), project_all,
        head_weights, first_lane,
    )
    output_sum = output_sum[0] + output_side.astype(f32)
    weight_sum = after(weight_sum, grad_mine)
    weight_home = all_to_all(weight_sum.reshape(count, shard, lanes))
    chips, pair = count // 2, 2 * shard
    output_low = output_sum.astype(low)

    def line_part(value, k):
        at = jnp.bitwise_xor(index // 2, k) * pair
        return lax.dynamic_slice_in_dim(value, at, pair, 0)

    output_line = [
        flip_exchange(line_part(output_low, k), "fsdp", 2 * k) for k in range(1, chips)
    ]
    output_line, weight_home = after((output_line, weight_home), tokens_grad)
    query_grad, keyval_grad, router_grad, gains = weight_grads(
        weight_home, query_weight, key_value_weight, share, experts
    )
    before_grad, middle_grad = gains[:, 0] / gain_before.astype(f32), gains[:, 1]
    output_grad = line_part(output_sum, 0)
    for near in output_line:
        output_grad = output_grad + near.astype(f32)
    own_half = lax.dynamic_slice_in_dim(output_grad, core * shard, shard, 0)
    other_half = flip_exchange(
        lax.dynamic_slice_in_dim(output_grad, (1 - core) * shard, shard, 0), "fsdp", 1
    )
    output_grad = jnp.where(
        core == 0,
        jnp.concatenate([own_half, other_half], 1),
        jnp.concatenate([other_half, own_half], 1),
    ).T
    return (
        block_out[None],
        tokens_grad[None],
        query_grad,
        keyval_grad,
        output_grad,
        router_grad,
        before_grad,
        middle_grad,
        inner_grad,
        outer_grad,
    )


def solution(mesh):
    by_heads = (mesh.shape["dp"], mesh.shape["fsdp"]) == (4, KEY_VALUE_HEADS)
    in_specs = (
        P("dp", "fsdp", None),
        P("dp", "fsdp"),
        P("dp", "fsdp", None),
        P(("dp", "fsdp"), None),
        P(("dp", "fsdp"), None),
        P(None, ("dp", "fsdp")),
        P(("dp", "fsdp"), None),
        P(("dp", "fsdp")),
        P(("dp", "fsdp")),
        P("dp", None, "fsdp"),
        P("fsdp", "dp"),
        P("dp", "fsdp", None),
    )
    out_specs = (
        P("dp", "fsdp", None),
        P("dp", "fsdp", None),
        P(("dp", "fsdp"), None),
        P(("dp", "fsdp"), None),
        P(None, ("dp", "fsdp")),
        P(("dp", "fsdp"), None),
        P(("dp", "fsdp")),
        P(("dp", "fsdp")),
        P("dp", None, "fsdp"),
        P("fsdp", "dp"),
    )
    return jax.shard_map(
        per_device_heads if by_heads else per_device, mesh=mesh, in_specs=in_specs, out_specs=out_specs, check_vma=False
    )
```
